32 devices in a mesh: grp: 4 (over z), elem: 8 (over y, x, core).
Axes of the slice: x: 2, y: 2, z: 4, core: 2. Of those that a mesh axis runs over, the one named last changes fastest.
Arguments:
- state: float32 [8, 72, 8192], P(None, None, ('grp', 'elem')), may hold values from -6 to 6
- kappa: float32 [8192], P(('grp', 'elem')), may hold values from 0.08 to 0.8
- edge_nbrs: int32 [512, 4], P(('grp', 'elem')), may hold values from 0 to 511, as said below
- stencil: int32 [8192, 9], P(('grp', 'elem')), may hold values from 0 to 8191, as said below
- owner: int32 [8192], P(('grp', 'elem')), may hold values from -1 to 31, as said below
- w_first: bfloat16 [216, 256], replicated, may hold values from -0.75 to 0.75
- w_inner: bfloat16 [5, 768, 256], replicated, may hold values from -0.375 to 0.375
- w_last: bfloat16 [768, 8], replicated, may hold values from -0.375 to 0.375
Outputs:
- new_state: float32 [8, 72, 8192], P(None, None, ('grp', 'elem'))
The draws below stay inside these ranges and needn't reach their ends.
Inputs may be any that keep to these rules, and one draw needn't show every extreme that they name: `edge_nbrs`: the neighbour across edge k of an element is held by the same device or by the device just before or after it along grp+elem, the last and the first device counting as adjacent; if e' is across edge k of e, then e is across edge (k + 2) mod 4 of e'. `stencil`: entry 4 of a column's block is the column itself; all nine entries name columns held by the same device. Every owner 0 to 31 is named by exactly 64 columns; the columns of one device name one owner at most 8 times, and in every draw some device names every owner exactly 8 times.
All inputs are finite; a program needn't handle non-finite values.
Results may differ from the reference program's by a relative error of at most 0.012.
Values may be sent and summed in bfloat16 or wider, within the bound.
No kernel may reach another device: no remote copies, remote signals or barrier semaphores. Data moves between devices by JAX's collectives and lax.ppermute only.
A program may use at most 64 MiB of HBM per device.

```python
import math
import jax
import jax.numpy as jnp
import numpy as np
from jax import lax

F = 8
LEV = 72
CH = 256
E_DEV = 16
COL_DEV = 256
EMU_ROWS = 64
NELEM = 512
NCOL = 8192
N_GRP = 4
N_ELEM = 8


def draw_edge_nbrs(key, part):
    key = jax.random.fold_in(key, 11)
    devs = NELEM // E_DEV
    scores = jax.random.randint(key, (devs, E_DEV), 0, 1 << 20)
    order = jnp.argsort(scores, axis=1, stable=True).astype(jnp.int32)
    inverse = jnp.argsort(order, axis=1, stable=True).astype(jnp.int32)
    across = E_DEV // 2
    rows_total = NELEM // across
    grid = (jnp.arange(devs, dtype=jnp.int32)[:, None] * E_DEV + order).reshape(-1)
    line = grid // across
    place = grid % across
    down = jnp.mod(line - 1, rows_total) * across + place
    right = line * across + jnp.mod(place + 1, across)
    upward = jnp.mod(line + 1, rows_total) * across + place
    leftward = line * across + jnp.mod(place - 1, across)
    targets = jnp.stack([down, right, upward, leftward], axis=1)
    holder = targets // E_DEV
    return (holder * E_DEV + inverse[holder, targets % E_DEV]).astype(jnp.int32)


def draw_stencil(key, part):
    key = jax.random.fold_in(key, 23)
    devs = NCOL // COL_DEV
    scores = jax.random.randint(key, (devs, COL_DEV), 0, 1 << 20)
    order = jnp.argsort(scores, axis=1, stable=True).astype(jnp.int32)
    inverse = jnp.argsort(order, axis=1, stable=True).astype(jnp.int32)
    height = COL_DEV // 16
    line = order // 16
    place = order % 16
    blocks = []
    for shift_line in (-1, 0, 1):
        for shift_place in (-1, 0, 1):
            nearby = jnp.clip(line + shift_line, 0, height - 1) * 16 + jnp.clip(place + shift_place, 0, 15)
            blocks.append(jnp.take_along_axis(inverse, nearby, axis=1) + jnp.arange(devs, dtype=jnp.int32)[:, None] * COL_DEV)
    return jnp.stack(blocks, axis=2).reshape(NCOL, 9).astype(jnp.int32)


def draw_owner(key, part):
    key = jax.random.fold_in(key, 37)
    devs = NCOL // COL_DEV
    first_key, second_key, third_key, fourth_key = jax.random.split(key, 4)
    busiest = jax.random.randint(first_key, (), 0, devs)
    base = jax.random.randint(second_key, (devs, COL_DEV), 0, 4096)
    lifted = jax.random.randint(third_key, (devs, 1), 0, 4) * 1024
    scores = jnp.where(jnp.arange(devs)[:, None] == busiest, 8192, base + lifted).reshape(-1)
    picked = jnp.argsort(-scores, stable=True)[:devs * EMU_ROWS]
    active = jnp.zeros((NCOL,), jnp.int32).at[picked].set(1)
    ranking = jnp.cumsum(active) - 1
    labels = jax.random.permutation(fourth_key, devs).astype(jnp.int32)
    return jnp.where(active > 0, labels[jnp.mod(ranking, devs)], -1).astype(jnp.int32)


def level_of(rng, extent, shards, smallest, high):
    def one(position, blocks):
        steps = jax.random.uniform(jax.random.fold_in(jax.random.fold_in(rng, 6), position), (blocks,), jnp.float32, smallest / len(shards), high / len(shards))
        return jnp.repeat(jnp.exp(steps), extent[position] // blocks).reshape((-1,) + (1,) * (len(extent) - position - 1))

    factor_of = one(*shards[0])
    for cut in shards[1:]:
        factor_of = factor_of * one(*cut)
    return factor_of


def gaussian(rng, extent, spread, reach, cuts=(), held_as=jnp.bfloat16):
    drawn = spread * jax.random.normal(rng, extent, jnp.float32)
    if cuts:
        drawn = drawn * level_of(rng, extent, cuts, -0.22, 0.18)
    return jnp.clip(drawn, -reach, reach).astype(held_as)


def setup_inputs(seed: int = 0) -> dict:
    key_of = jax.random.split(jax.random.key(seed), 9)
    return {
        "state": gaussian(key_of[0], (F, LEV, NCOL), 1.0, 6.0, ((2, 32),), jnp.float32),
        "kappa": jnp.clip(jnp.exp(math.log(0.8) - 2.3025851 * jax.random.uniform(key_of[1], (NCOL,), jnp.float32) ** level_of(key_of[1], (NCOL,), ((0, 32),), -0.2, 0.2)), 0.08, 0.8),
        "edge_nbrs": draw_edge_nbrs(jax.random.fold_in(key_of[8], 71), 0),
        "stencil": draw_stencil(jax.random.fold_in(key_of[8], 71), 0),
        "owner": draw_owner(jax.random.fold_in(key_of[8], 71), 0),
        "w_first": gaussian(key_of[5], (27 * F, CH), (9 * F) ** -0.5, 0.75),
        "w_inner": gaussian(key_of[6], (5, 3 * CH, CH), CH ** -0.5, 0.375),
        "w_last": gaussian(key_of[7], (3 * CH, F), CH ** -0.5, 0.375),
    }


EDGE_NODES = ((1, 2), (7, 11), (14, 13), (8, 4))

def second_derivative():
    points = np.array([-1.0, -math.sqrt(0.2), math.sqrt(0.2), 1.0])
    factors = np.array([1.0 / np.prod([points[j] - points[m] for m in range(4) if m != j]) for j in range(4)])
    deriv = np.zeros((4, 4))
    for i in range(4):
        for j in range(4):
            if i != j:
                deriv[i, j] = factors[j] / factors[i] / (points[i] - points[j])
        deriv[i, i] = -np.sum(deriv[i])
    return deriv @ deriv

def diffuse(state, kappa):
    fields, levels, columns = state.shape
    stiffness = jnp.asarray(second_derivative(), state.dtype)
    nodes = state.reshape(fields, levels, columns // 16, 4, 4)
    along_rows = jnp.einsum('ia,fleaj->fleij', stiffness, nodes, precision=lax.Precision.HIGHEST)
    along_cols = jnp.einsum('jb,fleib->fleij', stiffness, nodes, precision=lax.Precision.HIGHEST)
    return (kappa.reshape(columns // 16, 4, 4) * (along_rows + along_cols)).reshape(fields, levels, columns)

def edge_index():
    return jnp.array([n for pair in EDGE_NODES for n in pair], jnp.int32)

def edge_values(field):
    fields, levels, columns = field.shape
    nodes = field.reshape(fields, levels, columns // 16, 16)
    return nodes[:, :, :, edge_index()].reshape(fields, levels, columns // 2)

def facing_rows(base):
    offsets = jnp.array([[(k + 2) % 4 * 2 + 1 - m for m in range(2)] for k in range(4)], jnp.int32)
    return (base.astype(jnp.int32)[:, :, None] * 8 + offsets[None, :, :]).reshape(-1).astype(jnp.int32)

def smooth(field, edges, extended, rows):
    fields, levels, columns = field.shape
    facing = jnp.take(extended, rows, axis=2)
    merged = 0.5 * (edges + facing)
    nodes = field.reshape(fields, levels, columns // 16, 16)
    nodes = nodes.at[:, :, :, edge_index()].set(merged.reshape(fields, levels, columns // 16, 8))
    return nodes.reshape(fields, levels, columns)

def convolve(values, weight):
    batch, levels, channels = values.shape
    padded = jnp.pad(values, ((0, 0), (1, 1), (0, 0)))
    stacked = jnp.concatenate([padded[:, :-2], padded[:, 1:-1], padded[:, 2:]], axis=2)
    product = jnp.dot(stacked.reshape(batch * levels, 3 * channels), weight, preferred_element_type=jnp.float32)
    return product.reshape(batch, levels, weight.shape[1])

def activate(values):
    return jax.nn.silu(values).astype(jnp.bfloat16)

def halve(values):
    return ((values[:, 0::2].astype(jnp.float32) + values[:, 1::2].astype(jnp.float32)) * 0.5).astype(jnp.bfloat16)

def widen(coarse, fine):
    return (jnp.repeat(coarse, 2, axis=1).astype(jnp.float32) + fine.astype(jnp.float32)).astype(jnp.bfloat16)

def apply_network(gathered, w_first, w_inner, w_last):
    batch = gathered.shape[0]
    fields = w_last.shape[1]
    levels = gathered.shape[2] // fields
    inputs = gathered.reshape(batch, 9, fields, levels).transpose(0, 3, 1, 2).reshape(batch, levels, 9 * fields)
    first = activate(convolve(inputs, w_first))
    second = activate(convolve(first, w_inner[0]))
    third = activate(convolve(halve(second), w_inner[1]))
    deepest = activate(convolve(halve(third), w_inner[2]))
    upper = activate(convolve(widen(deepest, third), w_inner[3]))
    top = activate(convolve(widen(upper, second), w_inner[4]))
    output = convolve(top, w_last).astype(jnp.bfloat16)
    return output.transpose(0, 2, 1).reshape(batch, fields * levels)

def reference(state, kappa, edge_nbrs, stencil, owner, w_first, w_inner, w_last):
    fields, levels, columns = state.shape
    width = fields * levels
    dynamics = diffuse(state, kappa)
    edges = edge_values(dynamics)
    smoothed = smooth(dynamics, edges, edges, facing_rows(edge_nbrs))
    flat_state = jnp.transpose(state, (2, 0, 1)).reshape(columns, width).astype(jnp.bfloat16)
    active_count = N_GRP * N_ELEM * EMU_ROWS
    chosen = jnp.nonzero(owner >= 0, size=active_count)[0].astype(jnp.int32)
    blocks = chosen.reshape(active_count // EMU_ROWS, EMU_ROWS)

    def one_block(block):
        return apply_network(flat_state[stencil[block]], w_first, w_inner, w_last)
    outputs = lax.map(one_block, blocks).reshape(active_count, width)
    physics = jnp.zeros((columns, width), jnp.bfloat16).at[chosen].set(outputs)
    physics = physics.astype(jnp.float32).reshape(columns, fields, levels).transpose(1, 2, 0)
    return state + smoothed + physics
```

```python
import functools
import math

import jax
import jax.numpy as jnp
import numpy as np
from jax import lax
from jax.experimental import pallas as pl
from jax.experimental.pallas import tpu as pltpu
from jax.sharding import PartitionSpec as P

AXES = ("grp", "elem")
EDGE_NODES = ((1, 2), (7, 11), (14, 13), (8, 4))
VMEM = pl.BlockSpec(memory_space=pltpu.VMEM)
SMEM = pl.BlockSpec(memory_space=pltpu.SMEM)
HIGHEST = lax.Precision.HIGHEST
BF16 = jnp.bfloat16
F32 = jnp.float32
NB = 64
CHUNK = 512


def second_derivative():
    points = np.array([-1.0, -math.sqrt(0.2), math.sqrt(0.2), 1.0])
    factors = np.array(
        [1.0 / np.prod([points[j] - points[m] for m in range(4) if m != j]) for j in range(4)]
    )
    deriv = np.zeros((4, 4))
    for i in range(4):
        for j in range(4):
            if i != j:
                deriv[i, j] = factors[j] / factors[i] / (points[i] - points[j])
        deriv[i, i] = -np.sum(deriv[i])
    return deriv @ deriv


def diffusion_matrix(columns):
    lap = second_derivative()
    eye = np.eye(4)
    node = np.einsum("ia,jb->abij", lap, eye) + np.einsum("ia,jb->abij", eye, lap)
    return np.kron(np.eye(columns // 16), node.reshape(16, 16)).astype(np.float32)


def edge_matrix(columns):
    sel = np.zeros((columns, columns // 2), np.float32)
    for e in range(columns // 16):
        for k in range(4):
            for m in range(2):
                sel[16 * e + EDGE_NODES[k][m], 8 * e + 2 * k + m] = 1
    return sel


def node_tables(columns):
    on_edge = np.zeros((4, columns), np.float32)
    offset = np.zeros((1, columns), np.float32)
    for k in range(4):
        for m in range(2):
            on_edge[k, EDGE_NODES[k][m] :: 16] = 1
            offset[0, EDGE_NODES[k][m] :: 16] = (k + 2) % 4 * 2 + 1 - m
    holder = np.kron(np.eye(columns // 16), np.ones((1, 16))).astype(np.float32)
    table = np.concatenate([on_edge, offset, np.zeros((3, columns), np.float32)], axis=0)
    return table, holder


def iota(shape, dim):
    return lax.broadcasted_iota(jnp.int32, shape, dim)


def silu(values):
    half = 0.5 * values
    return half + half * jnp.tanh(half)


def edges_kernel(state_ref, kappa_ref, op_ref, sel_ref, dyn_ref, edge_ref):
    fields, levels, columns = state_ref.shape
    flat = state_ref[...].reshape(fields * levels, columns)
    dyn = kappa_ref[...] * jnp.dot(flat, op_ref[...], precision=HIGHEST)
    dyn_ref[...] = dyn
    edge_ref[...] = jnp.dot(dyn, sel_ref[...], precision=HIGHEST)


def final_kernel(total, dev_ref, state_ref, dyn_ref, low_ref, edge_ref, high_ref, nbr_ref, owner_ref,
                 table_ref, holder_ref, phys_ref, out_ref):
    fields, levels, columns = state_ref.shape
    elements = columns // 16
    rows = fields * levels
    rel = lax.rem(nbr_ref[...] - (dev_ref[0] - 1) * elements + total, total).astype(F32)
    spread = lax.dot_general(rel, holder_ref[...], (((0,), (0,)), ((), ())), precision=HIGHEST)
    on_edge = table_ref[0:4, :]
    is_edge = jnp.sum(on_edge, axis=0, keepdims=True)
    facing = 8.0 * jnp.sum(spread * on_edge, axis=0, keepdims=True) + table_ref[4:5, :]
    facing = jnp.where(is_edge > 0, facing, -1.0).astype(jnp.int32)
    half = columns // 2
    pieces = []
    for part, ref in enumerate((low_ref, edge_ref, high_ref)):
        pick = jnp.where(iota((half, columns), 0) + part * half == facing, 0.5, 0.0)
        pieces.append(jnp.dot(ref[...], pick, precision=HIGHEST))
    scale = 1.0 - 0.5 * is_edge
    smoothed = scale * dyn_ref[...] + (pieces[0] + pieces[1] + pieces[2])
    physics = jnp.where(owner_ref[...] >= 0, phys_ref[...].reshape(rows, columns), 0.0)
    out = state_ref[...].reshape(rows, columns) + smoothed + physics
    out_ref[...] = out.reshape(fields, levels, columns)


def conv_layer(levels, src, weight, emit, src_cols=None):
    step = min(levels, CHUNK // NB)
    while levels % step:
        step -= 1

    def one(i):
        l0 = i * step
        taps = []
        for t in range(3):
            if src_cols is None:
                tap = src[pl.ds(l0 + t, step)]
            else:
                tap = src[pl.ds(l0 + t, step), pl.ds(src_cols, NB), :]
            taps.append(tap.reshape(step * NB, tap.shape[-1]))
        acc = jnp.dot(jnp.concatenate(taps, axis=1), weight, preferred_element_type=F32)
        emit(l0, step, silu(acc).astype(BF16).reshape(step, NB, acc.shape[-1]))

    pl.loop(0, levels // step)(one)


def halve(y):
    y = y.reshape(y.shape[0] // 2, 2, *y.shape[1:]).astype(F32)
    return ((y[:, 0] + y[:, 1]) * 0.5).astype(BF16)


def widen(coarse, fine):
    step, cols, ch = coarse.shape
    wide = jnp.broadcast_to(coarse[:, None], (step, 2, cols, ch)).reshape(2 * step, cols, ch)
    return (wide.astype(F32) + fine.astype(F32)).astype(BF16)


def net_kernel(dev_ref, state_ref, sten_ref, w1_ref, wi_ref, w24_ref, out_ref,
               s_ref, oh_ref, g_ref, first_ref, second_ref, pool2_ref, third_ref, pool3_ref,
               join3_ref, join2_ref, top_ref, p_ref, r_ref, acc_ref):
    fields, levels, columns = state_ref.shape
    ch = wi_ref.shape[2]
    half2, half3 = levels // 2, levels // 4

    for ref, n in ((first_ref, levels), (pool2_ref, half2), (pool3_ref, half3), (join3_ref, half2),
                   (join2_ref, levels)):
        zero = jnp.zeros(ref.shape[1:], BF16)
        ref[0] = zero
        ref[n + 1] = zero
    zero = jnp.zeros((80, 128), BF16)
    g_ref[0] = zero
    g_ref[levels + 1] = zero
    p_ref[:, 0:NB] = jnp.zeros((24, NB), F32)
    p_ref[:, (levels + 1) * NB :] = jnp.zeros((24, NB), F32)

    for l in range(0, levels, 2):
        pair = jnp.concatenate([state_ref[:, l, :], state_ref[:, l + 1, :]], axis=0)
        s_ref[l * 8 : l * 8 + 16, :] = pair.astype(BF16)

    local = (sten_ref[...] - dev_ref[0] * columns).astype(F32)
    local = jnp.concatenate([local, jnp.zeros((columns, 119), F32)], axis=1)
    local = local.T.astype(jnp.int32)
    for k in range(9):
        oh_ref[k] = jnp.where(iota((columns, columns), 0) == local[k : k + 1, :], 1.0, 0.0).astype(BF16)

    for q in range(columns // 128):
        lanes = slice(q * 128, (q + 1) * 128)
        for k in range(0, 9, 2):
            parts = []
            for kk in (k, k + 1):
                if kk < 9:
                    part = jnp.dot(s_ref[...], oh_ref[kk, :, lanes], preferred_element_type=F32)
                else:
                    part = jnp.zeros((levels * fields, 128), F32)
                parts.append(part.reshape(levels, fields, 128))
            both = jnp.concatenate(parts, axis=1).astype(BF16)
            g_ref[1 : levels + 1, k * 8 : k * 8 + 16, :] = both

        @pl.loop(0, levels // 8)
        def _(i):
            for u in range(8):
                l = i * 8 + u
                x = g_ref[pl.ds(l, 3)].reshape(240, 128)
                acc = lax.dot_general(x, w1_ref[...], (((0,), (0,)), ((), ())),
                                      preferred_element_type=F32)
                first_ref[l + 1, lanes, :] = silu(acc).astype(BF16)

    acc_ref[...] = jnp.zeros_like(acc_ref)

    @pl.loop(0, columns // NB)
    def _(b):
        c0 = pl.multiple_of(b * NB, NB)

        def emit_second(l0, step, y):
            second_ref[pl.ds(l0, step)] = y
            pool2_ref[pl.ds(l0 // 2 + 1, step // 2)] = halve(y)

        conv_layer(levels, first_ref, wi_ref[0], emit_second, c0)

        def emit_third(l0, step, y):
            third_ref[pl.ds(l0, step)] = y
            pool3_ref[pl.ds(l0 // 2 + 1, step // 2)] = halve(y)

        conv_layer(half2, pool2_ref, wi_ref[1], emit_third)

        def emit_deepest(l0, step, y):
            fine = third_ref[pl.ds(2 * l0, 2 * step)]
            join3_ref[pl.ds(2 * l0 + 1, 2 * step)] = widen(y, fine)

        conv_layer(half3, pool3_ref, wi_ref[2], emit_deepest)

        def emit_upper(l0, step, y):
            fine = second_ref[pl.ds(2 * l0, 2 * step)]
            join2_ref[pl.ds(2 * l0 + 1, 2 * step)] = widen(y, fine)

        conv_layer(half2, join3_ref, wi_ref[3], emit_upper)

        def emit_top(l0, step, y):
            top_ref[pl.ds(l0, step)] = y

        conv_layer(levels, join2_ref, wi_ref[4], emit_top)

        group = 256 // NB
        for i in range(levels // group):
            x = top_ref[i * group : (i + 1) * group].reshape(256, ch)
            part = lax.dot_general(w24_ref[...], x, (((1,), (1,)), ((), ())),
                                   preferred_element_type=F32)
            p_ref[:, (i * group + 1) * NB : ((i + 1) * group + 1) * NB] = part
        for l in range(0, levels, 2):
            pair = []
            for u in (l, l + 1):
                pair.append(p_ref[0:8, u * NB : (u + 1) * NB]
                            + p_ref[8:16, (u + 1) * NB : (u + 2) * NB]
                            + p_ref[16:24, (u + 2) * NB : (u + 3) * NB])
            r_ref[l * 8 : l * 8 + 16, :] = jnp.concatenate(pair, axis=0).astype(BF16)
        place = jnp.where(iota((NB, columns), 1) == iota((NB, columns), 0) + c0, 1.0, 0.0).astype(BF16)
        acc_ref[...] += jnp.dot(r_ref[...], place, preferred_element_type=F32)

    for l in range(levels):
        out_ref[:, l, :] = acc_ref[l * 8 : (l + 1) * 8, :]


def per_device(state, kappa, edge_nbrs, stencil, owner, w_first, w_inner, w_last):
    fields, levels, columns = state.shape
    rows = fields * levels
    ch = w_inner.shape[2]
    devices = lax.axis_size(AXES)
    device = lax.axis_index(AXES)
    total = columns // 16 * devices
    dev = device.astype(jnp.int32).reshape(1)
    table, holder = node_tables(columns)
    f32 = functools.partial(jax.ShapeDtypeStruct, dtype=F32)

    dyn, edges = pl.pallas_call(
        edges_kernel,
        out_shape=(f32((rows, columns)), f32((rows, columns // 2))),
        in_specs=[VMEM] * 4,
        out_specs=(VMEM, VMEM),
        name="edges",
    )(state, kappa.reshape(1, columns), jnp.asarray(diffusion_matrix(columns)),
      jnp.asarray(edge_matrix(columns)))

    forward = [(i, (i + 1) % devices) for i in range(devices)]
    backward = [(i, (i - 1) % devices) for i in range(devices)]
    low = lax.ppermute(edges, AXES, forward)
    high = lax.ppermute(edges, AXES, backward)

    w1 = jnp.pad(w_first.reshape(3, 9 * fields, ch), ((0, 0), (0, 80 - 9 * fields), (0, 0)))
    w24 = w_last.reshape(3, ch, fields).transpose(0, 2, 1).reshape(3 * fields, ch)
    bf = lambda *shape: pltpu.VMEM(shape, BF16)
    physics = pl.pallas_call(
        net_kernel,
        out_shape=f32((fields, levels, columns)),
        in_specs=[SMEM] + [VMEM] * 5,
        out_specs=VMEM,
        scratch_shapes=[
            bf(rows, columns),
            bf(9, columns, columns),
            bf(levels + 2, 80, 128),
            bf(levels + 2, columns, ch),
            bf(levels, NB, ch),
            bf(levels // 2 + 2, NB, ch),
            bf(levels // 2, NB, ch),
            bf(levels // 4 + 2, NB, ch),
            bf(levels // 2 + 2, NB, ch),
            bf(levels + 2, NB, ch),
            bf(levels, NB, ch),
            pltpu.VMEM((24, (levels + 2) * NB), F32),
            bf(rows, NB),
            pltpu.VMEM((rows, columns), F32),
        ],
        compiler_params=pltpu.CompilerParams(vmem_limit_bytes=48 * 1024 * 1024),
        cost_estimate=pl.CostEstimate(
            flops=2 * columns * levels * ch * ch * 12, bytes_accessed=4 * 1024 * 1024,
            transcendentals=columns * levels * ch * 4),
        name="network",
    )(dev, state, stencil, w1.reshape(240, ch), w_inner, w24)

    return pl.pallas_call(
        functools.partial(final_kernel, total),
        out_shape=f32((fields, levels, columns)),
        in_specs=[SMEM] + [VMEM] * 10,
        out_specs=VMEM,
        name="combine",
    )(dev, state, dyn, low, edges, high, edge_nbrs, owner.reshape(1, columns), jnp.asarray(table),
      jnp.asarray(holder), physics)


def solution(mesh):
    in_specs = (
        P(None, None, AXES),
        P(AXES),
        P(AXES, None),
        P(AXES, None),
        P(AXES),
        P(),
        P(),
        P(),
    )
    return jax.shard_map(
        per_device, mesh=mesh, in_specs=in_specs, out_specs=P(None, None, AXES), check_vma=False
    )
```

```python
import functools
import math

import jax
import jax.numpy as jnp
import numpy as np
from jax import lax
from jax.experimental import pallas as pl
from jax.experimental.pallas import tpu as pltpu
from jax.sharding import PartitionSpec as P

AXES = ("grp", "elem")
EDGE_NODES = ((1, 2), (7, 11), (14, 13), (8, 4))
VMEM = pl.BlockSpec(memory_space=pltpu.VMEM)
SMEM = pl.BlockSpec(memory_space=pltpu.SMEM)
HIGHEST = lax.Precision.HIGHEST
BF16 = jnp.bfloat16
F32 = jnp.float32
NB = 32
STEP = 18
GROUP = 2


def second_derivative():
    points = np.array([-1.0, -math.sqrt(0.2), math.sqrt(0.2), 1.0])
    factors = np.array(
        [1.0 / np.prod([points[j] - points[m] for m in range(4) if m != j]) for j in range(4)]
    )
    deriv = np.zeros((4, 4))
    for i in range(4):
        for j in range(4):
            if i != j:
                deriv[i, j] = factors[j] / factors[i] / (points[i] - points[j])
        deriv[i, i] = -np.sum(deriv[i])
    return deriv @ deriv


def diffusion_matrix(columns):
    lap = second_derivative()
    eye = np.eye(4)
    node = np.einsum("ia,jb->abij", lap, eye) + np.einsum("ia,jb->abij", eye, lap)
    return np.kron(np.eye(columns // 16), node.reshape(16, 16)).astype(np.float32)


def edge_matrix(columns):
    sel = np.zeros((columns, columns // 2), np.float32)
    for e in range(columns // 16):
        for k in range(4):
            for m in range(2):
                sel[16 * e + EDGE_NODES[k][m], 8 * e + 2 * k + m] = 1
    return sel


def node_tables(columns):
    on_edge = np.zeros((4, columns), np.float32)
    offset = np.zeros((1, columns), np.float32)
    for k in range(4):
        for m in range(2):
            on_edge[k, EDGE_NODES[k][m] :: 16] = 1
            offset[0, EDGE_NODES[k][m] :: 16] = (k + 2) % 4 * 2 + 1 - m
    holder = np.kron(np.eye(columns // 16), np.ones((1, 16))).astype(np.float32)
    table = np.concatenate([on_edge, offset, np.zeros((3, columns), np.float32)], axis=0)
    return table, holder


def iota(shape, dim):
    return lax.broadcasted_iota(jnp.int32, shape, dim)


def silu(values):
    half = 0.5 * values
    return half + half * jnp.tanh(half)


def pack_kernel(dev_ref, state_ref, sten_ref, owner_ref, pay_ref):
    fields, levels, columns = state_ref.shape
    rows = fields * levels
    for l in range(0, levels, 2):
        pair = jnp.concatenate([state_ref[:, l, :], state_ref[:, l + 1, :]], axis=0)
        pay_ref[l * fields : (l + 2) * fields, :] = pair.astype(BF16)
    local = (sten_ref[...] - dev_ref[0] * columns).astype(F32)
    flag = jnp.where(owner_ref[...] >= 0, 1.0, 0.0)
    tail = jnp.concatenate([local, flag, jnp.zeros((6, columns), F32)], axis=0)
    pay_ref[rows : rows + 16, :] = tail.astype(BF16)


def edges_kernel(total, dev_ref, state_ref, kappa_ref, op_ref, sel_ref, nbr_ref, table_ref, holder_ref,
                 base_ref, edge_ref, facing_ref):
    fields, levels, columns = state_ref.shape
    elements = columns // 16
    flat = state_ref[...].reshape(fields * levels, columns)
    dyn = kappa_ref[...] * jnp.dot(flat, op_ref[...], precision=HIGHEST)
    edge = jnp.dot(dyn, sel_ref[...], precision=HIGHEST)
    edge_ref[...] = edge.astype(BF16)
    rel = lax.rem(nbr_ref[...] - (dev_ref[0] - 1) * elements + total, total).astype(F32)
    spread = jnp.dot(rel, holder_ref[...], precision=HIGHEST)
    on_edge = table_ref[0:4, :]
    is_edge = jnp.sum(on_edge, axis=0, keepdims=True)
    facing = 8.0 * jnp.sum(spread * on_edge, axis=0, keepdims=True) + table_ref[4:5, :]
    facing = jnp.where(is_edge > 0, facing, -1.0).astype(jnp.int32)
    facing_ref[...] = facing
    half = columns // 2
    pick = jnp.where(iota((half, columns), 0) + half == facing, 0.5, 0.0)
    own = jnp.dot(edge, pick, precision=HIGHEST)
    base_ref[...] = flat + (1.0 - 0.5 * is_edge) * dyn + own


def final_kernel(dev_ref, base_ref, low_ref, high_ref, facing_ref, rank_ref, mine_ref, other_ref, out_ref):
    rows, columns = base_ref.shape
    fields, levels, _ = out_ref.shape
    half = columns // 2
    facing = facing_ref[...]
    acc = base_ref[...]
    for part, ref in ((0, low_ref), (2, high_ref)):
        pick = jnp.where(iota((half, columns), 0) + part * half == facing, 0.5, 0.0).astype(BF16)
        acc = acc + jnp.dot(ref[...], pick, preferred_element_type=F32)
    out_ref[...] = acc.reshape(fields, levels, columns)
    me = lax.rem(dev_ref[0], GROUP)
    rank = rank_ref[...]
    slot = GROUP * iota((columns, columns), 0)
    put_mine = jnp.where(slot + me == rank, 1.0, 0.0).astype(BF16)
    put_other = jnp.where(slot + (1 - me) == rank, 1.0, 0.0).astype(BF16)
    physics = jnp.dot(mine_ref[...], put_mine, preferred_element_type=F32)
    physics = physics + jnp.dot(other_ref[...], put_other, preferred_element_type=F32)
    for l in range(levels):
        out_ref[:, l, :] += physics[l * fields : (l + 1) * fields, :]


def halve(y):
    y = y.reshape(y.shape[0] // 2, 2, *y.shape[1:]).astype(F32)
    return ((y[:, 0] + y[:, 1]) * 0.5).astype(BF16)


def widen(coarse, fine):
    step, cols, ch = coarse.shape
    wide = jnp.broadcast_to(coarse[:, None], (step, 2, cols, ch)).reshape(2 * step, cols, ch)
    return (wide.astype(F32) + fine.astype(F32)).astype(BF16)


def net_kernel(levels, fields, dev_ref, mine_ref, other_ref, w1_ref, wi_hbm, wl_ref, out_ref, rank_ref,
               pay_ref, oh_ref, g_ref, w1s_ref, w_ref, first_ref, second_ref, pool2_ref, third_ref,
               pool3_ref, join3_ref, join2_ref, top_ref, p_ref, acc_ref, sem):
    rows = fields * levels
    columns = mine_ref.shape[1]
    wide = GROUP * columns
    ch = wl_ref.shape[1] // 3
    taps = 9 * fields
    half2, half3 = levels // 2, levels // 4
    weights = pltpu.make_async_copy(wi_hbm, w_ref, sem)
    weights.start()

    for ref, n in ((first_ref, levels), (pool2_ref, half2), (pool3_ref, half3), (join3_ref, half2),
                   (join2_ref, levels)):
        zero = jnp.zeros(ref.shape[1:], BF16)
        ref[0] = zero
        ref[n + 1] = zero
    zero = jnp.zeros(g_ref.shape[1:], BF16)
    g_ref[0] = zero
    g_ref[levels + 1] = zero
    p_ref[:, 0:NB] = jnp.zeros((24, NB), F32)
    p_ref[:, (levels + 1) * NB :] = jnp.zeros((24, NB), F32)
    w1s_ref[...] = jnp.zeros(w1s_ref.shape, BF16)
    for t in range(3):
        w1s_ref[80 * t : 80 * t + taps, :] = w1_ref[taps * t : taps * (t + 1), :]
    acc_ref[...] = jnp.zeros(acc_ref.shape, F32)
    w24 = jnp.concatenate([wl_ref[:, ch * t : ch * (t + 1)].astype(F32) for t in range(3)], axis=0).astype(BF16)

    me = lax.rem(dev_ref[0], GROUP)
    pay_ref[:, pl.ds(pl.multiple_of(me * columns, columns), columns)] = mine_ref[...]
    pay_ref[:, pl.ds(pl.multiple_of((1 - me) * columns, columns), columns)] = other_ref[...]
    meta = pay_ref[rows : rows + 16, :]
    flags = meta.astype(F32)[9:10, :]
    upto = jnp.where(iota((wide, wide), 0) < iota((wide, wide), 1), 1.0, 0.0).astype(BF16)
    rank = jnp.dot(meta, upto, preferred_element_type=F32)[9:10, :]
    count = jnp.sum(flags).astype(jnp.int32)
    rank = jnp.where(flags > 0, rank, -1.0).astype(jnp.int32)
    rank_ref[...] = jnp.where(me == 0, rank[:, :columns], rank[:, columns:])
    share = (count - me + GROUP - 1) // GROUP
    slot = GROUP * iota((columns, wide), 0) + me
    choose = jnp.where(slot == rank, 1.0, 0.0).astype(BF16)
    flip = (((1,), (1,)), ((), ()))
    sten = lax.dot_general(meta, choose, flip, preferred_element_type=F32)
    part = jnp.where(iota((16, wide), 1) >= columns, 1.0, 0.0).astype(BF16)
    part = lax.dot_general(part, choose, flip, preferred_element_type=F32)
    sten = (sten + columns * part).astype(jnp.int32)

    @pl.loop(0, (share + 127) // 128)
    def _(q):
        lanes = pl.ds(pl.multiple_of(q * 128, 128), 128)
        for k in range(9):
            for half in range(columns // 128):
                here = sten[k : k + 1, half * 128 : (half + 1) * 128]
                picked = here if half == 0 else jnp.where(q == half, here, picked)
            oh_ref[:, k * 128 : (k + 1) * 128] = jnp.where(iota((wide, 128), 0) == picked, 1.0, 0.0).astype(BF16)
        for k in range(0, 9, 2):
            n = 2 if k < 8 else 1
            got = jnp.dot(pay_ref[0:rows, :], oh_ref[:, k * 128 : (k + n) * 128], preferred_element_type=F32)
            parts = [got[:, u * 128 : (u + 1) * 128].reshape(levels, fields, 128) for u in range(n)]
            if n == 1:
                parts.append(jnp.zeros_like(parts[0]))
            g_ref[1 : levels + 1, k * 8 : k * 8 + 16, :] = jnp.concatenate(parts, axis=1).astype(BF16)

        @pl.loop(0, levels // 12)
        def _(i):
            for u in range(12):
                l = i * 12 + u
                x = g_ref[pl.ds(l, 3)].reshape(240, 128)
                acc = lax.dot_general(x, w1s_ref[...], (((0,), (0,)), ((), ())),
                                      preferred_element_type=F32)
                first_ref[l + 1, pl.ds(pl.multiple_of(q * 128, 128), 128), :] = silu(acc).astype(BF16)

    weights.wait()
    mask = jnp.where(iota((128 // NB * 8, 128), 0) // 8 == iota((128 // NB * 8, 128), 1) // NB, 1.0, 0.0)

    @pl.loop(0, (share + NB - 1) // NB)
    def _(b):
        c0 = pl.multiple_of(b * NB, NB)

        def conv(load, layer, n, emit):
            for l0 in range(0, n, STEP):
                x = [load(l0 + t).reshape(STEP * NB, ch) for t in range(3)]
                acc = jnp.dot(jnp.concatenate(x, axis=1), w_ref[layer], preferred_element_type=F32)
                emit(l0, silu(acc).astype(BF16).reshape(STEP, NB, ch))

        def emit_second(l0, y):
            second_ref[l0 : l0 + STEP] = y
            pool2_ref[l0 // 2 + 1 : l0 // 2 + 1 + STEP // 2] = halve(y)

        def emit_third(l0, y):
            third_ref[l0 : l0 + STEP] = y
            pool3_ref[l0 // 2 + 1 : l0 // 2 + 1 + STEP // 2] = halve(y)

        def emit_deepest(l0, y):
            fine = third_ref[2 * l0 : 2 * (l0 + STEP)]
            join3_ref[2 * l0 + 1 : 2 * (l0 + STEP) + 1] = widen(y, fine)

        def emit_upper(l0, y):
            fine = second_ref[2 * l0 : 2 * (l0 + STEP)]
            join2_ref[2 * l0 + 1 : 2 * (l0 + STEP) + 1] = widen(y, fine)

        def emit_top(l0, y):
            top_ref[l0 : l0 + STEP] = y

        conv(lambda l: first_ref[l : l + STEP, pl.ds(c0, NB), :], 0, levels, emit_second)
        conv(lambda l: pool2_ref[l : l + STEP], 1, half2, emit_third)
        conv(lambda l: pool3_ref[l : l + STEP], 2, half3, emit_deepest)
        conv(lambda l: join3_ref[l : l + STEP], 3, half2, emit_upper)
        conv(lambda l: join2_ref[l : l + STEP], 4, levels, emit_top)

        group = 256 // NB
        for i in range(levels // group):
            x = top_ref[i * group : (i + 1) * group].reshape(256, ch)
            p_ref[:, (i * group + 1) * NB : ((i + 1) * group + 1) * NB] = lax.dot_general(
                w24, x, flip, preferred_element_type=F32)
        n = levels * NB
        out = p_ref[0:8, 0:n] + p_ref[8:16, NB : n + NB] + p_ref[16:24, 2 * NB : n + 2 * NB]
        tiles = []
        for i in range(n // 128):
            tile = out[:, i * 128 : (i + 1) * 128]
            tiles.append(jnp.concatenate([tile] * (128 // NB), axis=0) * mask)
        flat = jnp.concatenate(tiles, axis=0).astype(BF16)
        place = lax.rem(iota((128, columns), 0), NB) + c0 == iota((128, columns), 1)
        acc_ref[...] += jnp.dot(flat, jnp.where(place, 1.0, 0.0).astype(BF16), preferred_element_type=F32)

    out_ref[...] = acc_ref[...].astype(BF16)


def per_device(state, kappa, edge_nbrs, stencil, owner, w_first, w_inner, w_last):
    fields, levels, columns = state.shape
    rows = fields * levels
    ch = w_inner.shape[2]
    devices = lax.axis_size(AXES)
    device = lax.axis_index(AXES)
    total = columns // 16 * devices
    dev = device.astype(jnp.int32).reshape(1)
    table, holder = node_tables(columns)
    f32 = functools.partial(jax.ShapeDtypeStruct, dtype=F32)
    bf16 = functools.partial(jax.ShapeDtypeStruct, dtype=BF16)
    i32 = functools.partial(jax.ShapeDtypeStruct, dtype=jnp.int32)

    payload = pl.pallas_call(
        pack_kernel,
        out_shape=bf16((rows + 16, columns)),
        in_specs=[SMEM] + [VMEM] * 3,
        out_specs=VMEM,
        name="pack",
    )(dev, state, stencil.T, owner.reshape(1, columns))
    swap = [(i, i ^ 1) for i in range(devices)]
    other = lax.ppermute(payload, AXES, swap)

    base, edges, facing = pl.pallas_call(
        functools.partial(edges_kernel, total),
        out_shape=(f32((rows, columns)), bf16((rows, columns // 2)), i32((1, columns))),
        in_specs=[SMEM] + [VMEM] * 7,
        out_specs=(VMEM, VMEM, VMEM),
        cost_estimate=pl.CostEstimate(flops=3 * 10**9, bytes_accessed=2**21, transcendentals=0),
        name="edges",
    )(dev, state, kappa.reshape(1, columns), jnp.asarray(diffusion_matrix(columns)),
      jnp.asarray(edge_matrix(columns)), edge_nbrs.T, jnp.asarray(table), jnp.asarray(holder))

    bf = lambda *shape: pltpu.VMEM(shape, BF16)
    results, rank = pl.pallas_call(
        functools.partial(net_kernel, levels, fields),
        out_shape=(bf16((rows, columns)), i32((1, columns))),
        in_specs=[SMEM, VMEM, VMEM, VMEM, pl.BlockSpec(memory_space=pl.ANY), VMEM],
        out_specs=(VMEM, VMEM),
        scratch_shapes=[
            bf(rows + 16, GROUP * columns),
            bf(GROUP * columns, 9 * 128),
            bf(levels + 2, 80, 128),
            bf(240, ch),
            bf(*w_inner.shape),
            bf(levels + 2, columns, ch),
            bf(levels, NB, ch),
            bf(levels // 2 + 2, NB, ch),
            bf(levels // 2, NB, ch),
            bf(levels // 4 + 2, NB, ch),
            bf(levels // 2 + 2, NB, ch),
            bf(levels + 2, NB, ch),
            bf(levels, NB, ch),
            pltpu.VMEM((24, (levels + 2) * NB), F32),
            pltpu.VMEM((rows, columns), F32),
            pltpu.SemaphoreType.DMA,
        ],
        compiler_params=pltpu.CompilerParams(vmem_limit_bytes=48 * 1024 * 1024),
        name="network",
    )(dev, payload, other, w_first, w_inner, w_last.T)

    edges, results = lax.optimization_barrier((edges, results))
    back = lax.ppermute(results, AXES, swap)
    low = lax.ppermute(edges, AXES, [(i, (i + 1) % devices) for i in range(devices)])
    high = lax.ppermute(edges, AXES, [(i, (i - 1) % devices) for i in range(devices)])

    return pl.pallas_call(
        final_kernel,
        out_shape=f32((fields, levels, columns)),
        in_specs=[SMEM] + [VMEM] * 7,
        out_specs=VMEM,
        name="combine",
    )(dev, base, low, high, facing, rank, results, back)


def solution(mesh):
    in_specs = (
        P(None, None, AXES),
        P(AXES),
        P(AXES, None),
        P(AXES, None),
        P(AXES),
        P(),
        P(),
        P(),
    )
    return jax.shard_map(
        per_device, mesh=mesh, in_specs=in_specs, out_specs=P(None, None, AXES), check_vma=False
    )
```

```python
import functools
import math

import jax
import jax.numpy as jnp
import numpy as np
from jax import lax
from jax.experimental import pallas as pl
from jax.experimental.pallas import tpu as pltpu
from jax.sharding import PartitionSpec as P

AXES = ("grp", "elem")
EDGE_NODES = ((1, 2), (7, 11), (14, 13), (8, 4))
VMEM = pl.BlockSpec(memory_space=pltpu.VMEM)
SMEM = pl.BlockSpec(memory_space=pltpu.SMEM)
HIGHEST = lax.Precision.HIGHEST
BF16 = jnp.bfloat16
F32 = jnp.float32
NB = 32
STEP = 36
GROUP = 4


def second_derivative():
    points = np.array([-1.0, -math.sqrt(0.2), math.sqrt(0.2), 1.0])
    factors = np.array(
        [1.0 / np.prod([points[j] - points[m] for m in range(4) if m != j]) for j in range(4)]
    )
    deriv = np.zeros((4, 4))
    for i in range(4):
        for j in range(4):
            if i != j:
                deriv[i, j] = factors[j] / factors[i] / (points[i] - points[j])
        deriv[i, i] = -np.sum(deriv[i])
    return deriv @ deriv


def diffusion_matrix(columns):
    lap = second_derivative()
    eye = np.eye(4)
    node = np.einsum("ia,jb->abij", lap, eye) + np.einsum("ia,jb->abij", eye, lap)
    return np.kron(np.eye(columns // 16), node.reshape(16, 16)).astype(np.float32)


def edge_matrix(columns):
    sel = np.zeros((columns, columns // 2), np.float32)
    for e in range(columns // 16):
        for k in range(4):
            for m in range(2):
                sel[16 * e + EDGE_NODES[k][m], 8 * e + 2 * k + m] = 1
    return sel


def node_tables(columns):
    on_edge = np.zeros((4, columns), np.float32)
    offset = np.zeros((1, columns), np.float32)
    for k in range(4):
        for m in range(2):
            on_edge[k, EDGE_NODES[k][m] :: 16] = 1
            offset[0, EDGE_NODES[k][m] :: 16] = (k + 2) % 4 * 2 + 1 - m
    holder = np.kron(np.eye(columns // 16), np.ones((1, 16))).astype(np.float32)
    table = np.concatenate([on_edge, offset, np.zeros((3, columns), np.float32)], axis=0)
    return table, holder


def iota(shape, dim):
    return lax.broadcasted_iota(jnp.int32, shape, dim)


def silu(values):
    half = 0.5 * values
    return half + half * jnp.tanh(half)


def pack_kernel(dev_ref, state_ref, sten_ref, owner_ref, pay_ref):
    fields, levels, columns = state_ref.shape
    rows = fields * levels
    for l in range(0, levels, 2):
        pair = jnp.concatenate([state_ref[:, l, :], state_ref[:, l + 1, :]], axis=0)
        pay_ref[l * fields : (l + 2) * fields, :] = pair.astype(BF16)
    local = (sten_ref[...] - dev_ref[0] * columns).astype(F32)
    flag = jnp.where(owner_ref[...] >= 0, 1.0, 0.0)
    tail = jnp.concatenate([local, flag, jnp.zeros((6, columns), F32)], axis=0)
    pay_ref[rows : rows + 16, :] = tail.astype(BF16)


def edges_kernel(total, dev_ref, state_ref, kappa_ref, op_ref, sel_ref, nbr_ref, table_ref, holder_ref,
                 base_ref, edge_ref, facing_ref):
    fields, levels, columns = state_ref.shape
    elements = columns // 16
    flat = state_ref[...].reshape(fields * levels, columns)
    dyn = kappa_ref[...] * jnp.dot(flat, op_ref[...], precision=HIGHEST)
    edge = jnp.dot(dyn, sel_ref[...], precision=HIGHEST)
    edge_ref[...] = edge.astype(BF16)
    rel = lax.rem(nbr_ref[...] - (dev_ref[0] - 1) * elements + total, total).astype(F32)
    spread = jnp.dot(rel, holder_ref[...], precision=HIGHEST)
    on_edge = table_ref[0:4, :]
    is_edge = jnp.sum(on_edge, axis=0, keepdims=True)
    facing = 8.0 * jnp.sum(spread * on_edge, axis=0, keepdims=True) + table_ref[4:5, :]
    facing = jnp.where(is_edge > 0, facing, -1.0).astype(jnp.int32)
    facing_ref[...] = facing
    half = columns // 2
    pick = jnp.where(iota((half, columns), 0) + half == facing, 0.5, 0.0)
    own = jnp.dot(edge, pick, precision=HIGHEST)
    base_ref[...] = flat + (1.0 - 0.5 * is_edge) * dyn + own


def final_kernel(base_ref, low_ref, high_ref, facing_ref, code_ref, r0_ref, r1_ref, r2_ref, r3_ref, out_ref):
    rows, columns = base_ref.shape
    fields, levels, _ = out_ref.shape
    half = columns // 2
    facing = facing_ref[...]
    acc = base_ref[...]
    for part, ref in ((0, low_ref), (2, high_ref)):
        pick = jnp.where(iota((half, columns), 0) + part * half == facing, 0.5, 0.0).astype(BF16)
        acc = acc + jnp.dot(ref[...], pick, preferred_element_type=F32)
    out_ref[...] = acc.reshape(fields, levels, columns)
    quota = columns // GROUP
    code = code_ref[...]
    got = jnp.concatenate([r0_ref[...], r1_ref[...], r2_ref[...], r3_ref[...]], axis=1)
    spot = iota((GROUP * 2 * quota, columns), 0)
    for h in range(2):
        want = jnp.where(code >= 0, code // quota * (2 * quota) + lax.rem(code, quota) + h * quota, -1)
        put = jnp.where(spot == want, 1.0, 0.0).astype(BF16)
        physics = jnp.dot(got, put, preferred_element_type=F32)
        for l in range(levels // 2):
            out_ref[:, h * (levels // 2) + l, :] += physics[l * fields : (l + 1) * fields, :]


def halve(y):
    y = y.reshape(y.shape[0] // 2, 2, *y.shape[1:]).astype(F32)
    return ((y[:, 0] + y[:, 1]) * 0.5).astype(BF16)


def widen(coarse, fine):
    step, cols, ch = coarse.shape
    wide = jnp.broadcast_to(coarse[:, None], (step, 2, cols, ch)).reshape(2 * step, cols, ch)
    return (wide.astype(F32) + fine.astype(F32)).astype(BF16)


def net_kernel(levels, fields, dev_ref, m0_ref, m1_ref, m2_ref, m3_ref, w1_ref, wi_hbm, wl_ref,
               r0_ref, r1_ref, r2_ref, r3_ref, code_ref,
               pay_ref, oh_ref, g_ref, w1s_ref, w_ref, first_ref, second_ref, pool2_ref, third_ref,
               pool3_ref, join3_ref, join2_ref, top_ref, p_ref, acc_ref, to_ref, sem):
    rows = fields * levels
    columns = m0_ref.shape[1]
    quota = columns // GROUP
    wide = GROUP * columns
    ch = wl_ref.shape[1] // 3
    taps = 9 * fields
    half2, half3 = levels // 2, levels // 4
    weights = pltpu.make_async_copy(wi_hbm, w_ref, sem)
    weights.start()

    for ref, n in ((first_ref, levels), (pool2_ref, half2), (pool3_ref, half3), (join3_ref, half2),
                   (join2_ref, levels)):
        zero = jnp.zeros(ref.shape[1:], BF16)
        ref[0] = zero
        ref[n + 1] = zero
    zero = jnp.zeros(g_ref.shape[1:], BF16)
    g_ref[0] = zero
    g_ref[levels + 1] = zero
    p_ref[:, 0:NB] = jnp.zeros((24, NB), F32)
    p_ref[:, (levels + 1) * NB :] = jnp.zeros((24, NB), F32)
    w1s_ref[...] = jnp.zeros(w1s_ref.shape, BF16)
    for t in range(3):
        w1s_ref[80 * t : 80 * t + taps, :] = w1_ref[taps * t : taps * (t + 1), :]
    acc_ref[...] = jnp.zeros(acc_ref.shape, F32)
    w24 = jnp.concatenate([wl_ref[:, ch * t : ch * (t + 1)].astype(F32) for t in range(3)], axis=0).astype(BF16)

    me = lax.rem(dev_ref[0], GROUP)
    for d, ref in enumerate((m0_ref, m1_ref, m2_ref, m3_ref)):
        pay_ref[:, pl.ds(pl.multiple_of((me ^ d) * columns, columns), columns)] = ref[...]
    meta = pay_ref[rows : rows + 16, :]
    flags = meta.astype(F32)[9:10, :]
    upto = jnp.where(iota((columns, columns), 0) < iota((columns, columns), 1), 1.0, 0.0).astype(BF16)
    start = jnp.zeros((1, 1), F32)
    ranks, targets, code = [], [], jnp.zeros((1, columns), F32)
    for m in range(GROUP):
        block = meta[:, m * columns : (m + 1) * columns]
        flag = flags[:, m * columns : (m + 1) * columns]
        local = jnp.dot(block, upto, preferred_element_type=F32)[9:10, :].astype(jnp.int32)
        rank = local + start.astype(jnp.int32)
        ranks.append(jnp.where(flag > 0, rank, -1))
        targets.append(jnp.where(flag > 0, (me ^ m) * quota + local // GROUP + 1, 0).astype(F32))
        mine = jnp.where(flag > 0, (lax.rem(rank, GROUP) ^ me) * quota + local // GROUP, -1)
        code = jnp.where(me == m, mine, code)
        start = start + jnp.sum(flag, axis=1, keepdims=True)
    code_ref[...] = code.astype(jnp.int32)
    rank = jnp.concatenate(ranks, axis=1)
    share = (jnp.sum(flags).astype(jnp.int32) - me + GROUP - 1) // GROUP
    slot = GROUP * iota((columns, wide), 0) + me
    choose = jnp.where(slot == rank, 1.0, 0.0).astype(BF16)
    flip = (((1,), (1,)), ((), ()))
    sten = lax.dot_general(meta, choose, flip, preferred_element_type=F32)
    part = (iota((16, wide), 1) // columns).astype(F32).astype(BF16)
    part = lax.dot_general(part, choose, flip, preferred_element_type=F32)
    sten = (sten + columns * part).astype(jnp.int32)
    target = jnp.broadcast_to(jnp.concatenate(targets, axis=1), (128, wide)).astype(BF16)
    to_ref[...] = lax.dot_general(choose, target, flip, preferred_element_type=F32) - 1.0

    @pl.loop(0, (share + 127) // 128)
    def _(q):
        lanes = pl.ds(pl.multiple_of(q * 128, 128), 128)
        for k in range(9):
            for half in range(columns // 128):
                here = sten[k : k + 1, half * 128 : (half + 1) * 128]
                picked = here if half == 0 else jnp.where(q == half, here, picked)
            oh_ref[:, k * 128 : (k + 1) * 128] = jnp.where(iota((wide, 128), 0) == picked, 1.0, 0.0).astype(BF16)
        for k in range(0, 9, 2):
            n = 2 if k < 8 else 1
            got = jnp.dot(pay_ref[0:rows, :], oh_ref[:, k * 128 : (k + n) * 128], preferred_element_type=F32)
            parts = [got[:, u * 128 : (u + 1) * 128].reshape(levels, fields, 128) for u in range(n)]
            if n == 1:
                parts.append(jnp.zeros_like(parts[0]))
            g_ref[1 : levels + 1, k * 8 : k * 8 + 16, :] = jnp.concatenate(parts, axis=1).astype(BF16)

        @pl.loop(0, levels // 12)
        def _(i):
            for u in range(12):
                l = i * 12 + u
                x = g_ref[pl.ds(l, 3)].reshape(240, 128)
                acc = lax.dot_general(x, w1s_ref[...], (((0,), (0,)), ((), ())),
                                      preferred_element_type=F32)
                first_ref[l + 1, pl.ds(pl.multiple_of(q * 128, 128), 128), :] = silu(acc).astype(BF16)

    weights.wait()
    mask = jnp.where(iota((128 // NB * 8, 128), 0) // 8 == iota((128 // NB * 8, 128), 1) // NB, 1.0, 0.0)

    @pl.loop(0, (share + NB - 1) // NB)
    def _(b):
        c0 = pl.multiple_of(b * NB, NB)

        def conv(load, layer, n, emit):
            step = min(n, STEP)
            for l0 in range(0, n, step):
                x = [load(l0 + t, step).reshape(step * NB, ch) for t in range(3)]
                acc = jnp.dot(jnp.concatenate(x, axis=1), w_ref[layer], preferred_element_type=F32)
                emit(l0, step, silu(acc).astype(BF16).reshape(step, NB, ch))

        def emit_second(l0, step, y):
            second_ref[l0 : l0 + step] = y
            pool2_ref[l0 // 2 + 1 : l0 // 2 + 1 + step // 2] = halve(y)

        def emit_third(l0, step, y):
            third_ref[l0 : l0 + step] = y
            pool3_ref[l0 // 2 + 1 : l0 // 2 + 1 + step // 2] = halve(y)

        def emit_deepest(l0, step, y):
            fine = third_ref[2 * l0 : 2 * (l0 + step)]
            join3_ref[2 * l0 + 1 : 2 * (l0 + step) + 1] = widen(y, fine)

        def emit_upper(l0, step, y):
            fine = second_ref[2 * l0 : 2 * (l0 + step)]
            join2_ref[2 * l0 + 1 : 2 * (l0 + step) + 1] = widen(y, fine)

        def emit_top(l0, step, y):
            top_ref[l0 : l0 + step] = y

        conv(lambda l, n: first_ref[l : l + n, pl.ds(c0, NB), :], 0, levels, emit_second)
        conv(lambda l, n: pool2_ref[l : l + n], 1, half2, emit_third)
        conv(lambda l, n: pool3_ref[l : l + n], 2, half3, emit_deepest)
        conv(lambda l, n: join3_ref[l : l + n], 3, half2, emit_upper)
        conv(lambda l, n: join2_ref[l : l + n], 4, levels, emit_top)

        group = 256 // NB
        for i in range(levels // group):
            x = top_ref[i * group : (i + 1) * group].reshape(256, ch)
            p_ref[:, (i * group + 1) * NB : ((i + 1) * group + 1) * NB] = lax.dot_general(
                w24, x, flip, preferred_element_type=F32)
        n = levels * NB
        out = p_ref[0:8, 0:n] + p_ref[8:16, NB : n + NB] + p_ref[16:24, 2 * NB : n + 2 * NB]
        tiles = []
        for i in range(n // 128):
            tile = out[:, i * 128 : (i + 1) * 128]
            tiles.append(jnp.concatenate([tile] * (128 // NB), axis=0) * mask)
        flat = jnp.concatenate(tiles, axis=0).astype(BF16)
        to = to_ref[pl.ds(c0, NB), :].astype(jnp.int32)
        for h in range(2):
            lane = jnp.where(to >= 0, to // quota * (2 * quota) + lax.rem(to, quota) + h * quota, -1)
            lane = jnp.concatenate([lane] * (128 // NB), axis=0)
            place = [jnp.where(lane == iota((128, 128), 1) + i * 128, 1.0, 0.0) for i in range(2 * columns // 128)]
            place = jnp.concatenate(place, axis=1).astype(BF16)
            acc_ref[...] += jnp.dot(flat[h * rows // 2 : (h + 1) * rows // 2], place, preferred_element_type=F32)

    for d, ref in enumerate((r0_ref, r1_ref, r2_ref, r3_ref)):
        ref[...] = acc_ref[:, d * 2 * quota : (d + 1) * 2 * quota].astype(BF16)


def per_device(state, kappa, edge_nbrs, stencil, owner, w_first, w_inner, w_last):
    fields, levels, columns = state.shape
    rows = fields * levels
    ch = w_inner.shape[2]
    devices = lax.axis_size(AXES)
    device = lax.axis_index(AXES)
    total = columns // 16 * devices
    dev = device.astype(jnp.int32).reshape(1)
    table, holder = node_tables(columns)
    f32 = functools.partial(jax.ShapeDtypeStruct, dtype=F32)
    bf16 = functools.partial(jax.ShapeDtypeStruct, dtype=BF16)
    i32 = functools.partial(jax.ShapeDtypeStruct, dtype=jnp.int32)

    payload = pl.pallas_call(
        pack_kernel,
        out_shape=bf16((rows + 16, columns)),
        in_specs=[SMEM] + [VMEM] * 3,
        out_specs=VMEM,
        name="pack",
    )(dev, state, stencil.T, owner.reshape(1, columns))
    def trade(x, d):
        return lax.ppermute(x, AXES, [(i, i ^ d) for i in range(devices)])

    member1 = trade(payload, 1)
    member2 = trade(payload, 2)

    base, edges, facing = pl.pallas_call(
        functools.partial(edges_kernel, total),
        out_shape=(f32((rows, columns)), bf16((rows, columns // 2)), i32((1, columns))),
        in_specs=[SMEM] + [VMEM] * 7,
        out_specs=(VMEM, VMEM, VMEM),
        cost_estimate=pl.CostEstimate(flops=3 * 10**9, bytes_accessed=2**21, transcendentals=0),
        name="edges",
    )(dev, state, kappa.reshape(1, columns), jnp.asarray(diffusion_matrix(columns)),
      jnp.asarray(edge_matrix(columns)), edge_nbrs.T, jnp.asarray(table), jnp.asarray(holder))

    member2, base = lax.optimization_barrier((member2, base))
    member3 = trade(member2, 1)
    low = lax.ppermute(edges, AXES, [(i, (i + 1) % devices) for i in range(devices)])
    high = lax.ppermute(edges, AXES, [(i, (i - 1) % devices) for i in range(devices)])

    bf = lambda *shape: pltpu.VMEM(shape, BF16)
    lanes = 2 * columns // GROUP
    *results, code = pl.pallas_call(
        functools.partial(net_kernel, levels, fields),
        out_shape=[bf16((rows // 2, lanes))] * GROUP + [i32((1, columns))],
        in_specs=[SMEM] + [VMEM] * (GROUP + 1) + [pl.BlockSpec(memory_space=pl.ANY), VMEM],
        out_specs=[VMEM] * (GROUP + 1),
        scratch_shapes=[
            bf(rows + 16, GROUP * columns),
            bf(GROUP * columns, 9 * 128),
            bf(levels + 2, 80, 128),
            bf(240, ch),
            bf(*w_inner.shape),
            bf(levels + 2, columns, ch),
            bf(levels, NB, ch),
            bf(levels // 2 + 2, NB, ch),
            bf(levels // 2, NB, ch),
            bf(levels // 4 + 2, NB, ch),
            bf(levels // 2 + 2, NB, ch),
            bf(levels + 2, NB, ch),
            bf(levels, NB, ch),
            pltpu.VMEM((24, (levels + 2) * NB), F32),
            pltpu.VMEM((rows // 2, GROUP * lanes), F32),
            pltpu.VMEM((columns, 128), F32),
            pltpu.SemaphoreType.DMA,
        ],
        compiler_params=pltpu.CompilerParams(vmem_limit_bytes=48 * 1024 * 1024),
        cost_estimate=pl.CostEstimate(flops=10**10, bytes_accessed=2**22, transcendentals=10**7),
        name="network",
    )(dev, payload, member1, member2, member3, w_first, w_inner, w_last.T)
    back = [trade(results[d], d) for d in range(1, GROUP)]

    return pl.pallas_call(
        final_kernel,
        out_shape=f32((fields, levels, columns)),
        in_specs=[VMEM] * 9,
        out_specs=VMEM,
        name="combine",
    )(base, low, high, facing, code, results[0], *back)


def solution(mesh):
    in_specs = (
        P(None, None, AXES),
        P(AXES),
        P(AXES, None),
        P(AXES, None),
        P(AXES),
        P(),
        P(),
        P(),
    )
    return jax.shard_map(
        per_device, mesh=mesh, in_specs=in_specs, out_specs=P(None, None, AXES), check_vma=False
    )
```

```python
import functools
import math

import jax
import jax.numpy as jnp
import numpy as np
from jax import lax
from jax.experimental import pallas as pl
from jax.experimental.pallas import tpu as pltpu
from jax.sharding import PartitionSpec as P

AXES = ("grp", "elem")
EDGE_NODES = ((1, 2), (7, 11), (14, 13), (8, 4))
VMEM = pl.BlockSpec(memory_space=pltpu.VMEM)
SMEM = pl.BlockSpec(memory_space=pltpu.SMEM)
HIGHEST = lax.Precision.HIGHEST
BF16 = jnp.bfloat16
F32 = jnp.float32
NB = 32
STEP = 12
GROUP = 4


def second_derivative():
    points = np.array([-1.0, -math.sqrt(0.2), math.sqrt(0.2), 1.0])
    factors = np.array(
        [1.0 / np.prod([points[j] - points[m] for m in range(4) if m != j]) for j in range(4)]
    )
    deriv = np.zeros((4, 4))
    for i in range(4):
        for j in range(4):
            if i != j:
                deriv[i, j] = factors[j] / factors[i] / (points[i] - points[j])
        deriv[i, i] = -np.sum(deriv[i])
    return deriv @ deriv


def diffusion_matrix(columns):
    lap = second_derivative()
    eye = np.eye(4)
    node = np.einsum("ia,jb->abij", lap, eye) + np.einsum("ia,jb->abij", eye, lap)
    return np.kron(np.eye(columns // 16), node.reshape(16, 16)).astype(np.float32)


def edge_matrix(columns):
    sel = np.zeros((columns, columns // 2), np.float32)
    for e in range(columns // 16):
        for k in range(4):
            for m in range(2):
                sel[16 * e + EDGE_NODES[k][m], 8 * e + 2 * k + m] = 1
    return sel


def node_tables(columns):
    on_edge = np.zeros((4, columns), np.float32)
    offset = np.zeros((1, columns), np.float32)
    for k in range(4):
        for m in range(2):
            on_edge[k, EDGE_NODES[k][m] :: 16] = 1
            offset[0, EDGE_NODES[k][m] :: 16] = (k + 2) % 4 * 2 + 1 - m
    holder = np.kron(np.eye(columns // 16), np.ones((1, 16))).astype(np.float32)
    table = np.concatenate([on_edge, offset, np.zeros((3, columns), np.float32)], axis=0)
    return table, holder


def iota(shape, dim):
    return lax.broadcasted_iota(jnp.int32, shape, dim)


def silu(values):
    half = 0.5 * values
    return half + half * jnp.tanh(half)


def reorder(outer, inner):
    n = outer * inner
    row = iota((n, n), 0)
    source = lax.rem(row, outer) * inner + row // outer
    return jnp.where(source == iota((n, n), 1), 1.0, 0.0).astype(BF16)


def pack_kernel(dev_ref, state_ref, sten_ref, owner_ref, pay_ref):
    fields, levels, columns = state_ref.shape
    rows = fields * levels
    flat = state_ref[...].reshape(rows, columns).astype(BF16)
    pay_ref[0:rows, :] = jnp.dot(reorder(fields, levels), flat, preferred_element_type=F32).astype(BF16)
    local = (sten_ref[...] - dev_ref[0] * columns).astype(F32)
    flag = jnp.where(owner_ref[...] >= 0, 1.0, 0.0)
    tail = jnp.concatenate([local, flag, jnp.zeros((6, columns), F32)], axis=0)
    pay_ref[rows : rows + 16, :] = tail.astype(BF16)


def edges_kernel(total, dev_ref, state_ref, kappa_ref, op_ref, sel_ref, nbr_ref, table_ref, holder_ref,
                 base_ref, edge_ref, facing_ref):
    fields, levels, columns = state_ref.shape
    elements = columns // 16
    flat = state_ref[...].reshape(fields * levels, columns)
    dyn = kappa_ref[...] * jnp.dot(flat, op_ref[...], precision=HIGHEST)
    edge = jnp.dot(dyn, sel_ref[...], precision=HIGHEST)
    edge_ref[...] = edge.astype(BF16)
    rel = lax.rem(nbr_ref[...] - (dev_ref[0] - 1) * elements + total, total).astype(F32)
    spread = jnp.dot(rel, holder_ref[...], precision=HIGHEST)
    on_edge = table_ref[0:4, :]
    is_edge = jnp.sum(on_edge, axis=0, keepdims=True)
    facing = 8.0 * jnp.sum(spread * on_edge, axis=0, keepdims=True) + table_ref[4:5, :]
    facing = jnp.where(is_edge > 0, facing, -1.0).astype(jnp.int32)
    facing_ref[...] = facing
    half = columns // 2
    pick = jnp.where(iota((half, columns), 0) + half == facing, 0.5, 0.0)
    own = jnp.dot(edge, pick, precision=HIGHEST)
    base_ref[...] = flat + (1.0 - 0.5 * is_edge) * dyn + own


def land(code, d, quota, columns):
    slot = jnp.where((code >= d * quota) & (code < (d + 1) * quota), code - d * quota, -2 * quota)
    spot = iota((2 * quota, columns), 0)
    return [jnp.where(spot == slot + h * quota, 1.0, 0.0).astype(BF16) for h in range(2)]


def middle_kernel(base_ref, low_ref, high_ref, facing_ref, out_ref):
    rows, columns = base_ref.shape
    half = columns // 2
    facing = facing_ref[...]
    acc = base_ref[...]
    for part, ref in ((0, low_ref), (2, high_ref)):
        pick = jnp.where(iota((half, columns), 0) + part * half == facing, 0.5, 0.0).astype(BF16)
        acc = acc + jnp.dot(ref[...], pick, preferred_element_type=F32)
    out_ref[...] = acc


def final_kernel(base_ref, code_ref, r0_ref, r1_ref, r2_ref, r3_ref, out_ref):
    rows, columns = base_ref.shape
    fields, levels, _ = out_ref.shape
    quota = columns // GROUP
    code = code_ref[...]
    got = jnp.concatenate([r0_ref[...], r1_ref[...], r2_ref[...], r3_ref[...]], axis=1)
    puts = [land(code, d, quota, columns) for d in range(GROUP)]
    physics = []
    for h in range(2):
        put = jnp.concatenate([p[h] for p in puts], axis=0)
        physics.append(jnp.dot(got, put, preferred_element_type=F32).astype(BF16))
    physics = jnp.concatenate(physics, axis=0)
    physics = jnp.dot(reorder(levels, fields), physics, preferred_element_type=F32)
    out_ref[...] = (base_ref[...] + physics).reshape(fields, levels, columns)


def halve(y):
    y = y.reshape(y.shape[0] // 2, 2, *y.shape[1:]).astype(F32)
    return ((y[:, 0] + y[:, 1]) * 0.5).astype(BF16)


def widen(coarse, fine):
    step, cols, ch = coarse.shape
    wide = jnp.broadcast_to(coarse[:, None], (step, 2, cols, ch)).reshape(2 * step, cols, ch)
    return (wide.astype(F32) + fine.astype(F32)).astype(BF16)


def net_kernel(levels, fields, dev_ref, m0_ref, m1_ref, m2_ref, m3_ref, w1_ref, wi_hbm, wl_ref,
               r0_ref, r1_ref, r2_ref, r3_ref, code_ref,
               pay_ref, oh_ref, g_ref, net_ref, w1s_ref, w_ref, first_ref, second_ref, pool2_ref, third_ref,
               pool3_ref, join3_ref, join2_ref, top_ref, p_ref, acc_ref, to_ref, sem):
    rows = fields * levels
    columns = m0_ref.shape[1]
    quota = columns // GROUP
    wide = GROUP * columns
    ch = wl_ref.shape[1] // 3
    taps = 9 * fields
    half2, half3 = levels // 2, levels // 4
    weights = pltpu.make_async_copy(wi_hbm, w_ref, sem)
    weights.start()

    for ref, n in ((first_ref, levels), (pool2_ref, half2), (pool3_ref, half3), (join3_ref, half2),
                   (join2_ref, levels)):
        zero = jnp.zeros(ref.shape[1:], BF16)
        ref[0] = zero
        ref[n + 1] = zero
    net_ref[0] = jnp.zeros(net_ref.shape[1:], BF16)
    net_ref[levels + 1] = jnp.zeros(net_ref.shape[1:], BF16)
    net_ref[:, :, 80:128] = jnp.zeros((levels + 2, columns, 48), BF16)
    p_ref[:, 0:NB] = jnp.zeros((24, NB), F32)
    p_ref[:, (levels + 1) * NB :] = jnp.zeros((24, NB), F32)
    w1s_ref[...] = jnp.zeros(w1s_ref.shape, BF16)
    for t in range(3):
        w1s_ref[128 * t : 128 * t + taps, :] = w1_ref[taps * t : taps * (t + 1), :]
    acc_ref[...] = jnp.zeros(acc_ref.shape, F32)
    w24 = jnp.concatenate([wl_ref[:, ch * t : ch * (t + 1)].astype(F32) for t in range(3)], axis=0).astype(BF16)

    me = lax.rem(dev_ref[0], GROUP)
    for d, ref in enumerate((m0_ref, m1_ref, m2_ref, m3_ref)):
        pay_ref[:, pl.ds(pl.multiple_of((me ^ d) * columns, columns), columns)] = ref[...]
    meta = pay_ref[rows : rows + 16, :]
    flags = meta.astype(F32)[9:10, :]
    upto = jnp.where(iota((columns, columns), 0) < iota((columns, columns), 1), 1.0, 0.0).astype(BF16)
    start = jnp.zeros((1, 1), F32)
    ranks, targets, code = [], [], jnp.zeros((1, columns), F32)
    for m in range(GROUP):
        block = meta[:, m * columns : (m + 1) * columns]
        flag = flags[:, m * columns : (m + 1) * columns]
        local = jnp.dot(block, upto, preferred_element_type=F32)[9:10, :].astype(jnp.int32)
        rank = local + start.astype(jnp.int32)
        ranks.append(jnp.where(flag > 0, rank, -1))
        targets.append(jnp.where(flag > 0, (me ^ m) * quota + local // GROUP + 1, 0).astype(F32))
        mine = jnp.where(flag > 0, (lax.rem(rank, GROUP) ^ me) * quota + local // GROUP, -1)
        code = jnp.where(me == m, mine, code)
        start = start + jnp.sum(flag, axis=1, keepdims=True)
    code_ref[...] = code.astype(jnp.int32)
    rank = jnp.concatenate(ranks, axis=1)
    share = (jnp.sum(flags).astype(jnp.int32) - me + GROUP - 1) // GROUP
    slot = GROUP * iota((columns, wide), 0) + me
    choose = jnp.where(slot == rank, 1.0, 0.0).astype(BF16)
    flip = (((1,), (1,)), ((), ()))
    sten = lax.dot_general(meta, choose, flip, preferred_element_type=F32)
    part = (iota((16, wide), 1) // columns).astype(F32).astype(BF16)
    part = lax.dot_general(part, choose, flip, preferred_element_type=F32)
    sten = (sten + columns * part).astype(jnp.int32)
    target = jnp.broadcast_to(jnp.concatenate(targets, axis=1), (128, wide)).astype(BF16)
    to_ref[...] = lax.dot_general(choose, target, flip, preferred_element_type=F32) - 1.0

    @pl.loop(0, (share + 127) // 128)
    def _(q):
        lanes = pl.ds(pl.multiple_of(q * 128, 128), 128)
        for k in range(9):
            for half in range(columns // 128):
                here = sten[k : k + 1, half * 128 : (half + 1) * 128]
                picked = here if half == 0 else jnp.where(q == half, here, picked)
            oh_ref[:, k * 128 : (k + 1) * 128] = jnp.where(iota((wide, 128), 0) == picked, 1.0, 0.0).astype(BF16)
        for k in range(0, 9, 2):
            n = 2 if k < 8 else 1
            got = jnp.dot(pay_ref[0:rows, :], oh_ref[:, k * 128 : (k + n) * 128], preferred_element_type=F32)
            parts = [got[:, u * 128 : (u + 1) * 128].reshape(levels, fields, 128) for u in range(n)]
            if n == 1:
                parts.append(jnp.zeros_like(parts[0]))
            g_ref[0:levels, k * 8 : k * 8 + 16, :] = jnp.concatenate(parts, axis=1).astype(BF16)

        for l in range(levels):
            net_ref[l + 1, lanes, 0:80] = g_ref[l].T

    weights.wait()
    mask = jnp.where(iota((128 // NB * 8, 128), 0) // 8 == iota((128 // NB * 8, 128), 1) // NB, 1.0, 0.0)

    @pl.loop(0, (share + NB - 1) // NB)
    def _(b):
        c0 = pl.multiple_of(b * NB, NB)

        def conv(load, weight, n, emit):
            step = max(s for s in range(1, STEP + 1) if n % s == 0)
            for l0 in range(0, n, step):
                x = [load(l0 + t, step).reshape(step * NB, -1) for t in range(3)]
                acc = jnp.dot(jnp.concatenate(x, axis=1), weight, preferred_element_type=F32)
                emit(l0, step, silu(acc).astype(BF16).reshape(step, NB, ch))

        def emit_first(l0, step, y):
            first_ref[l0 + 1 : l0 + 1 + step] = y

        def emit_second(l0, step, y):
            second_ref[l0 : l0 + step] = y
            pool2_ref[l0 // 2 + 1 : l0 // 2 + 1 + step // 2] = halve(y)

        def emit_third(l0, step, y):
            third_ref[l0 : l0 + step] = y
            pool3_ref[l0 // 2 + 1 : l0 // 2 + 1 + step // 2] = halve(y)

        def emit_deepest(l0, step, y):
            fine = third_ref[2 * l0 : 2 * (l0 + step)]
            join3_ref[2 * l0 + 1 : 2 * (l0 + step) + 1] = widen(y, fine)

        def emit_upper(l0, step, y):
            fine = second_ref[2 * l0 : 2 * (l0 + step)]
            join2_ref[2 * l0 + 1 : 2 * (l0 + step) + 1] = widen(y, fine)

        def emit_top(l0, step, y):
            top_ref[l0 : l0 + step] = y

        conv(lambda l, n: net_ref[l : l + n, pl.ds(c0, NB), :], w1s_ref[...], levels, emit_first)
        conv(lambda l, n: first_ref[l : l + n], w_ref[0], levels, emit_second)
        conv(lambda l, n: pool2_ref[l : l + n], w_ref[1], half2, emit_third)
        conv(lambda l, n: pool3_ref[l : l + n], w_ref[2], half3, emit_deepest)
        conv(lambda l, n: join3_ref[l : l + n], w_ref[3], half2, emit_upper)
        conv(lambda l, n: join2_ref[l : l + n], w_ref[4], levels, emit_top)

        group = 256 // NB
        for i in range(levels // group):
            x = top_ref[i * group : (i + 1) * group].reshape(256, ch)
            p_ref[:, (i * group + 1) * NB : ((i + 1) * group + 1) * NB] = lax.dot_general(
                w24, x, flip, preferred_element_type=F32)
        n = levels * NB
        out = p_ref[0:8, 0:n] + p_ref[8:16, NB : n + NB] + p_ref[16:24, 2 * NB : n + 2 * NB]
        tiles = []
        for i in range(n // 128):
            tile = out[:, i * 128 : (i + 1) * 128]
            tiles.append(jnp.concatenate([tile] * (128 // NB), axis=0) * mask)
        flat = jnp.concatenate(tiles, axis=0).astype(BF16)
        to = to_ref[pl.ds(c0, NB), :].astype(jnp.int32)
        for h in range(2):
            lane = jnp.where(to >= 0, to // quota * (2 * quota) + lax.rem(to, quota) + h * quota, -1)
            lane = jnp.concatenate([lane] * (128 // NB), axis=0)
            place = [jnp.where(lane == iota((128, 128), 1) + i * 128, 1.0, 0.0) for i in range(2 * columns // 128)]
            place = jnp.concatenate(place, axis=1).astype(BF16)
            acc_ref[...] += jnp.dot(flat[h * rows // 2 : (h + 1) * rows // 2], place, preferred_element_type=F32)

    for d, ref in enumerate((r0_ref, r1_ref, r2_ref, r3_ref)):
        ref[...] = acc_ref[:, d * 2 * quota : (d + 1) * 2 * quota].astype(BF16)


def per_device(state, kappa, edge_nbrs, stencil, owner, w_first, w_inner, w_last):
    fields, levels, columns = state.shape
    rows = fields * levels
    ch = w_inner.shape[2]
    devices = lax.axis_size(AXES)
    device = lax.axis_index(AXES)
    total = columns // 16 * devices
    dev = device.astype(jnp.int32).reshape(1)
    table, holder = node_tables(columns)
    f32 = functools.partial(jax.ShapeDtypeStruct, dtype=F32)
    bf16 = functools.partial(jax.ShapeDtypeStruct, dtype=BF16)
    i32 = functools.partial(jax.ShapeDtypeStruct, dtype=jnp.int32)

    payload = pl.pallas_call(
        pack_kernel,
        out_shape=bf16((rows + 16, columns)),
        in_specs=[SMEM] + [VMEM] * 3,
        out_specs=VMEM,
        name="pack",
    )(dev, state, stencil.T, owner.reshape(1, columns))
    def trade(x, d):
        return lax.ppermute(x, AXES, [(i, i ^ d) for i in range(devices)])

    member1 = trade(payload, 1)
    member2 = trade(payload, 2)

    base, edges, facing = pl.pallas_call(
        functools.partial(edges_kernel, total),
        out_shape=(f32((rows, columns)), bf16((rows, columns // 2)), i32((1, columns))),
        in_specs=[SMEM] + [VMEM] * 7,
        out_specs=(VMEM, VMEM, VMEM),
        cost_estimate=pl.CostEstimate(flops=3 * 10**9, bytes_accessed=2**21, transcendentals=0),
        name="edges",
    )(dev, state, kappa.reshape(1, columns), jnp.asarray(diffusion_matrix(columns)),
      jnp.asarray(edge_matrix(columns)), edge_nbrs.T, jnp.asarray(table), jnp.asarray(holder))

    member2, base = lax.optimization_barrier((member2, base))
    member3 = trade(member2, 1)
    low = lax.ppermute(edges, AXES, [(i, (i + 1) % devices) for i in range(devices)])
    high = lax.ppermute(edges, AXES, [(i, (i - 1) % devices) for i in range(devices)])

    bf = lambda *shape: pltpu.VMEM(shape, BF16)
    lanes = 2 * columns // GROUP
    *results, code = pl.pallas_call(
        functools.partial(net_kernel, levels, fields),
        out_shape=[bf16((rows // 2, lanes))] * GROUP + [i32((1, columns))],
        in_specs=[SMEM] + [VMEM] * (GROUP + 1) + [pl.BlockSpec(memory_space=pl.ANY), VMEM],
        out_specs=[VMEM] * (GROUP + 1),
        scratch_shapes=[
            bf(rows + 16, GROUP * columns),
            bf(GROUP * columns, 9 * 128),
            bf(levels, 80, 128),
            bf(levels + 2, columns, 128),
            bf(3 * 128, ch),
            bf(*w_inner.shape),
            bf(levels + 2, NB, ch),
            bf(levels, NB, ch),
            bf(levels // 2 + 2, NB, ch),
            bf(levels // 2, NB, ch),
            bf(levels // 4 + 2, NB, ch),
            bf(levels // 2 + 2, NB, ch),
            bf(levels + 2, NB, ch),
            bf(levels, NB, ch),
            pltpu.VMEM((24, (levels + 2) * NB), F32),
            pltpu.VMEM((rows // 2, GROUP * lanes), F32),
            pltpu.VMEM((columns, 128), F32),
            pltpu.SemaphoreType.DMA,
        ],
        compiler_params=pltpu.CompilerParams(vmem_limit_bytes=48 * 1024 * 1024),
        cost_estimate=pl.CostEstimate(flops=10**10, bytes_accessed=2**22, transcendentals=10**7),
        name="network",
    )(dev, payload, member1, member2, member3, w_first, w_inner, w_last.T)
    back = [trade(results[d], d) for d in range(1, GROUP)]

    middle = pl.pallas_call(
        middle_kernel,
        out_shape=f32((rows, columns)),
        in_specs=[VMEM] * 4,
        out_specs=VMEM,
        cost_estimate=pl.CostEstimate(flops=10**9, bytes_accessed=2**22, transcendentals=0),
        name="middle",
    )(*lax.optimization_barrier((base, low, high, facing, results[0]))[:4])

    return pl.pallas_call(
        final_kernel,
        out_shape=f32((fields, levels, columns)),
        in_specs=[VMEM] * 6,
        out_specs=VMEM,
        name="combine",
    )(middle, code, results[0], *back)


def solution(mesh):
    in_specs = (
        P(None, None, AXES),
        P(AXES),
        P(AXES, None),
        P(AXES, None),
        P(AXES),
        P(),
        P(),
        P(),
    )
    return jax.shard_map(
        per_device, mesh=mesh, in_specs=in_specs, out_specs=P(None, None, AXES), check_vma=False
    )
```

```python
import functools
import math

import jax
import jax.numpy as jnp
import numpy as np
from jax import lax
from jax.experimental import pallas as pl
from jax.experimental.pallas import tpu as pltpu
from jax.sharding import PartitionSpec as P

AXES = ("grp", "elem")
EDGE_NODES = ((1, 2), (7, 11), (14, 13), (8, 4))
VMEM = pl.BlockSpec(memory_space=pltpu.VMEM)
SMALL = pltpu.CompilerParams(vmem_limit_bytes=12 * 1024 * 1024)
SMEM = pl.BlockSpec(memory_space=pltpu.SMEM)
HIGHEST = lax.Precision.HIGHEST
BF16 = jnp.bfloat16
F32 = jnp.float32
NB = 32
STEP = 12
GROUP = 4


def second_derivative():
    points = np.array([-1.0, -math.sqrt(0.2), math.sqrt(0.2), 1.0])
    factors = np.array(
        [1.0 / np.prod([points[j] - points[m] for m in range(4) if m != j]) for j in range(4)]
    )
    deriv = np.zeros((4, 4))
    for i in range(4):
        for j in range(4):
            if i != j:
                deriv[i, j] = factors[j] / factors[i] / (points[i] - points[j])
        deriv[i, i] = -np.sum(deriv[i])
    return deriv @ deriv


def diffusion_matrix(columns):
    lap = second_derivative()
    eye = np.eye(4)
    node = np.einsum("ia,jb->abij", lap, eye) + np.einsum("ia,jb->abij", eye, lap)
    return np.kron(np.eye(columns // 16), node.reshape(16, 16)).astype(np.float32)


def edge_matrix(columns):
    sel = np.zeros((columns, columns // 2), np.float32)
    for e in range(columns // 16):
        for k in range(4):
            for m in range(2):
                sel[16 * e + EDGE_NODES[k][m], 8 * e + 2 * k + m] = 1
    return sel


def node_tables(columns):
    on_edge = np.zeros((4, columns), np.float32)
    offset = np.zeros((1, columns), np.float32)
    for k in range(4):
        for m in range(2):
            on_edge[k, EDGE_NODES[k][m] :: 16] = 1
            offset[0, EDGE_NODES[k][m] :: 16] = (k + 2) % 4 * 2 + 1 - m
    holder = np.kron(np.eye(columns // 16), np.ones((1, 16))).astype(np.float32)
    table = np.concatenate([on_edge, offset, np.zeros((3, columns), np.float32)], axis=0)
    return table, holder


def iota(shape, dim):
    return lax.broadcasted_iota(jnp.int32, shape, dim)


def silu(values):
    half = 0.5 * values
    return half + half * jnp.tanh(half)


def pack_kernel(dev_ref, state_ref, sten_ref, owner_ref, pay_ref):
    fields, levels, columns = state_ref.shape
    rows = fields * levels
    for l in range(0, levels, 2):
        pair = jnp.concatenate([state_ref[:, l, :], state_ref[:, l + 1, :]], axis=0)
        pay_ref[l * fields : (l + 2) * fields, :] = pair.astype(BF16)
    local = (sten_ref[...] - dev_ref[0] * columns).astype(F32)
    flag = jnp.where(owner_ref[...] >= 0, 1.0, 0.0)
    tail = jnp.concatenate([local, flag, jnp.zeros((6, columns), F32)], axis=0)
    pay_ref[rows : rows + 16, :] = tail.astype(BF16)


def edges_kernel(total, dev_ref, state_ref, kappa_ref, op_ref, sel_ref, nbr_ref, table_ref, holder_ref,
                 base_ref, edge_ref, facing_ref):
    fields, levels, columns = state_ref.shape
    elements = columns // 16
    flat = state_ref[...].reshape(fields * levels, columns)
    dyn = kappa_ref[...] * jnp.dot(flat, op_ref[...], precision=HIGHEST)
    edge = jnp.dot(dyn, sel_ref[...], precision=HIGHEST)
    edge_ref[...] = edge.astype(BF16)
    rel = lax.rem(nbr_ref[...] - (dev_ref[0] - 1) * elements + total, total).astype(F32)
    spread = jnp.dot(rel, holder_ref[...], precision=HIGHEST)
    on_edge = table_ref[0:4, :]
    is_edge = jnp.sum(on_edge, axis=0, keepdims=True)
    facing = 8.0 * jnp.sum(spread * on_edge, axis=0, keepdims=True) + table_ref[4:5, :]
    facing = jnp.where(is_edge > 0, facing, -1.0).astype(jnp.int32)
    facing_ref[...] = facing
    half = columns // 2
    pick = jnp.where(iota((half, columns), 0) + half == facing, 0.5, 0.0)
    own = jnp.dot(edge, pick, precision=HIGHEST)
    base_ref[...] = flat + (1.0 - 0.5 * is_edge) * dyn + own


def land(code, d, quota, columns):
    slot = jnp.where((code >= d * quota) & (code < (d + 1) * quota), code - d * quota, -2 * quota)
    spot = iota((2 * quota, columns), 0)
    return [jnp.where(spot == slot + h * quota, 1.0, 0.0).astype(BF16) for h in range(2)]


def middle_kernel(base_ref, low_ref, high_ref, facing_ref, out_ref):
    rows, columns = base_ref.shape
    half = columns // 2
    facing = facing_ref[...]
    acc = base_ref[...]
    for part, ref in ((0, low_ref), (2, high_ref)):
        pick = jnp.where(iota((half, columns), 0) + part * half == facing, 0.5, 0.0).astype(BF16)
        acc = acc + jnp.dot(ref[...], pick, preferred_element_type=F32)
    out_ref[...] = acc


def final_kernel(base_ref, code_ref, r0_ref, r1_ref, r2_ref, r3_ref, out_ref):
    fields, levels, columns = out_ref.shape
    quota = columns // GROUP
    code = code_ref[...]
    got = jnp.concatenate([r0_ref[...], r1_ref[...], r2_ref[...], r3_ref[...]], axis=1)
    puts = [land(code, d, quota, columns) for d in range(GROUP)]
    for h in range(2):
        put = jnp.concatenate([p[h] for p in puts], axis=0)
        physics = jnp.dot(got, put, preferred_element_type=F32)
        for i in range(levels // 2):
            l = h * (levels // 2) + i
            out_ref[:, l, :] = base_ref[:, l, :] + physics[i * fields : (i + 1) * fields, :]


def halve(y):
    y = y.reshape(y.shape[0] // 2, 2, *y.shape[1:]).astype(F32)
    return ((y[:, 0] + y[:, 1]) * 0.5).astype(BF16)


def widen(coarse, fine):
    step, cols, ch = coarse.shape
    wide = jnp.broadcast_to(coarse[:, None], (step, 2, cols, ch)).reshape(2 * step, cols, ch)
    return (wide.astype(F32) + fine.astype(F32)).astype(BF16)


def net_kernel(levels, fields, dev_ref, m0_ref, m1_ref, m2_ref, m3_ref, w1_ref, wi_hbm, wl_ref,
               r0_ref, r1_ref, r2_ref, r3_ref, code_ref,
               pay_ref, oh_ref, g_ref, net_ref, w1s_ref, w_ref, first_ref, second_ref, pool2_ref, third_ref,
               pool3_ref, join3_ref, join2_ref, top_ref, p_ref, acc_ref, to_ref, sem):
    rows = fields * levels
    columns = m0_ref.shape[1]
    quota = columns // GROUP
    wide = GROUP * columns
    ch = wl_ref.shape[1] // 3
    taps = 9 * fields
    half2, half3 = levels // 2, levels // 4
    weights = pltpu.make_async_copy(wi_hbm, w_ref, sem)
    weights.start()

    for ref, n in ((first_ref, levels), (pool2_ref, half2), (pool3_ref, half3), (join3_ref, half2),
                   (join2_ref, levels)):
        zero = jnp.zeros(ref.shape[1:], BF16)
        ref[0] = zero
        ref[n + 1] = zero
    net_ref[0] = jnp.zeros(net_ref.shape[1:], BF16)
    net_ref[levels + 1] = jnp.zeros(net_ref.shape[1:], BF16)
    net_ref[:, :, 80:128] = jnp.zeros((levels + 2, columns, 48), BF16)
    p_ref[:, 0:NB] = jnp.zeros((24, NB), F32)
    p_ref[:, (levels + 1) * NB :] = jnp.zeros((24, NB), F32)
    w1s_ref[...] = jnp.zeros(w1s_ref.shape, BF16)
    for t in range(3):
        w1s_ref[128 * t : 128 * t + taps, :] = w1_ref[taps * t : taps * (t + 1), :]
    acc_ref[...] = jnp.zeros(acc_ref.shape, F32)
    w24 = jnp.concatenate([wl_ref[:, ch * t : ch * (t + 1)].astype(F32) for t in range(3)], axis=0).astype(BF16)

    me = lax.rem(dev_ref[0], GROUP)
    for d, ref in enumerate((m0_ref, m1_ref, m2_ref, m3_ref)):
        pay_ref[:, pl.ds(pl.multiple_of((me ^ d) * columns, columns), columns)] = ref[...]
    meta = pay_ref[rows : rows + 16, :]
    flags = meta.astype(F32)[9:10, :]
    upto = jnp.where(iota((columns, columns), 0) < iota((columns, columns), 1), 1.0, 0.0).astype(BF16)
    start = jnp.zeros((1, 1), F32)
    ranks, targets, code = [], [], jnp.zeros((1, columns), F32)
    for m in range(GROUP):
        block = meta[:, m * columns : (m + 1) * columns]
        flag = flags[:, m * columns : (m + 1) * columns]
        local = jnp.dot(block, upto, preferred_element_type=F32)[9:10, :].astype(jnp.int32)
        rank = local + start.astype(jnp.int32)
        ranks.append(jnp.where(flag > 0, rank, -1))
        targets.append(jnp.where(flag > 0, (me ^ m) * quota + local // GROUP + 1, 0).astype(F32))
        mine = jnp.where(flag > 0, (lax.rem(rank, GROUP) ^ me) * quota + local // GROUP, -1)
        code = jnp.where(me == m, mine, code)
        start = start + jnp.sum(flag, axis=1, keepdims=True)
    code_ref[...] = code.astype(jnp.int32)
    rank = jnp.concatenate(ranks, axis=1)
    share = (jnp.sum(flags).astype(jnp.int32) - me + GROUP - 1) // GROUP
    slot = GROUP * iota((columns, wide), 0) + me
    choose = jnp.where(slot == rank, 1.0, 0.0).astype(BF16)
    flip = (((1,), (1,)), ((), ()))
    sten = lax.dot_general(meta, choose, flip, preferred_element_type=F32)
    part = (iota((16, wide), 1) // columns).astype(F32).astype(BF16)
    part = lax.dot_general(part, choose, flip, preferred_element_type=F32)
    sten = (sten + columns * part).astype(jnp.int32)
    target = jnp.broadcast_to(jnp.concatenate(targets, axis=1), (128, wide)).astype(BF16)
    to_ref[...] = lax.dot_general(choose, target, flip, preferred_element_type=F32) - 1.0

    @pl.loop(0, (share + 127) // 128)
    def _(q):
        lanes = pl.ds(pl.multiple_of(q * 128, 128), 128)
        for k in range(9):
            for half in range(columns // 128):
                here = sten[k : k + 1, half * 128 : (half + 1) * 128]
                picked = here if half == 0 else jnp.where(q == half, here, picked)
            oh_ref[:, k * 128 : (k + 1) * 128] = jnp.where(iota((wide, 128), 0) == picked, 1.0, 0.0).astype(BF16)
        for k in range(0, 9, 2):
            n = 2 if k < 8 else 1
            got = jnp.dot(pay_ref[0:rows, :], oh_ref[:, k * 128 : (k + n) * 128], preferred_element_type=F32)
            parts = [got[:, u * 128 : (u + 1) * 128].reshape(levels, fields, 128) for u in range(n)]
            if n == 1:
                parts.append(jnp.zeros_like(parts[0]))
            g_ref[0:levels, k * 8 : k * 8 + 16, :] = jnp.concatenate(parts, axis=1).astype(BF16)

        for l in range(levels):
            net_ref[l + 1, lanes, 0:80] = g_ref[l].T

    weights.wait()
    mask = jnp.where(iota((128 // NB * 8, 128), 0) // 8 == iota((128 // NB * 8, 128), 1) // NB, 1.0, 0.0)

    @pl.loop(0, (share + NB - 1) // NB)
    def _(b):
        c0 = pl.multiple_of(b * NB, NB)

        pending = []

        def flush():
            for item in pending:
                item()
            pending.clear()

        def conv(load, weight, n, emit):
            step = max(s for s in range(1, STEP + 1) if n % s == 0)
            for l0 in range(0, n, step):
                x = [load(l0 + t, step).reshape(step * NB, -1) for t in range(3)]
                acc = jnp.dot(jnp.concatenate(x, axis=1), weight, preferred_element_type=F32)
                flush()
                pending.append(lambda emit=emit, l0=l0, step=step, acc=acc: emit(
                    l0, step, silu(acc).astype(BF16).reshape(step, NB, ch)))

        def emit_first(l0, step, y):
            first_ref[l0 + 1 : l0 + 1 + step] = y

        def emit_second(l0, step, y):
            second_ref[l0 : l0 + step] = y
            pool2_ref[l0 // 2 + 1 : l0 // 2 + 1 + step // 2] = halve(y)

        def emit_third(l0, step, y):
            third_ref[l0 : l0 + step] = y
            pool3_ref[l0 // 2 + 1 : l0 // 2 + 1 + step // 2] = halve(y)

        def emit_deepest(l0, step, y):
            fine = third_ref[2 * l0 : 2 * (l0 + step)]
            join3_ref[2 * l0 + 1 : 2 * (l0 + step) + 1] = widen(y, fine)

        def emit_upper(l0, step, y):
            fine = second_ref[2 * l0 : 2 * (l0 + step)]
            join2_ref[2 * l0 + 1 : 2 * (l0 + step) + 1] = widen(y, fine)

        def emit_top(l0, step, y):
            top_ref[l0 : l0 + step] = y

        conv(lambda l, n: net_ref[l : l + n, pl.ds(c0, NB), :], w1s_ref[...], levels, emit_first)
        conv(lambda l, n: first_ref[l : l + n], w_ref[0], levels, emit_second)
        conv(lambda l, n: pool2_ref[l : l + n], w_ref[1], half2, emit_third)
        conv(lambda l, n: pool3_ref[l : l + n], w_ref[2], half3, emit_deepest)
        conv(lambda l, n: join3_ref[l : l + n], w_ref[3], half2, emit_upper)
        conv(lambda l, n: join2_ref[l : l + n], w_ref[4], levels, emit_top)

        flush()
        group = 256 // NB
        for i in range(levels // group):
            x = top_ref[i * group : (i + 1) * group].reshape(256, ch)
            p_ref[:, (i * group + 1) * NB : ((i + 1) * group + 1) * NB] = lax.dot_general(
                w24, x, flip, preferred_element_type=F32)
        n = levels * NB
        out = p_ref[0:8, 0:n] + p_ref[8:16, NB : n + NB] + p_ref[16:24, 2 * NB : n + 2 * NB]
        tiles = []
        for i in range(n // 128):
            tile = out[:, i * 128 : (i + 1) * 128]
            tiles.append(jnp.concatenate([tile] * (128 // NB), axis=0) * mask)
        flat = jnp.concatenate(tiles, axis=0).astype(BF16)
        to = to_ref[pl.ds(c0, NB), :].astype(jnp.int32)
        for h in range(2):
            lane = jnp.where(to >= 0, to // quota * (2 * quota) + lax.rem(to, quota) + h * quota, -1)
            lane = jnp.concatenate([lane] * (128 // NB), axis=0)
            place = [jnp.where(lane == iota((128, 128), 1) + i * 128, 1.0, 0.0) for i in range(2 * columns // 128)]
            place = jnp.concatenate(place, axis=1).astype(BF16)
            acc_ref[...] += jnp.dot(flat[h * rows // 2 : (h + 1) * rows // 2], place, preferred_element_type=F32)

    for d, ref in enumerate((r0_ref, r1_ref, r2_ref, r3_ref)):
        ref[...] = acc_ref[:, d * 2 * quota : (d + 1) * 2 * quota].astype(BF16)


def per_device(state, kappa, edge_nbrs, stencil, owner, w_first, w_inner, w_last):
    fields, levels, columns = state.shape
    rows = fields * levels
    ch = w_inner.shape[2]
    devices = lax.axis_size(AXES)
    device = lax.axis_index(AXES)
    total = columns // 16 * devices
    dev = device.astype(jnp.int32).reshape(1)
    table, holder = node_tables(columns)
    f32 = functools.partial(jax.ShapeDtypeStruct, dtype=F32)
    bf16 = functools.partial(jax.ShapeDtypeStruct, dtype=BF16)
    i32 = functools.partial(jax.ShapeDtypeStruct, dtype=jnp.int32)

    payload = pl.pallas_call(
        pack_kernel,
        out_shape=bf16((rows + 16, columns)),
        in_specs=[SMEM] + [VMEM] * 3,
        out_specs=VMEM,
        name="pack",
    )(dev, state, stencil.T, owner.reshape(1, columns))
    def trade(x, d):
        return lax.ppermute(x, AXES, [(i, i ^ d) for i in range(devices)])

    member1 = trade(payload, 1)
    member2 = trade(payload, 2)

    base, edges, facing = pl.pallas_call(
        functools.partial(edges_kernel, total),
        out_shape=(f32((rows, columns)), bf16((rows, columns // 2)), i32((1, columns))),
        in_specs=[SMEM] + [VMEM] * 7,
        out_specs=(VMEM, VMEM, VMEM),
        cost_estimate=pl.CostEstimate(flops=3 * 10**9, bytes_accessed=2**21, transcendentals=0),
        name="edges",
    )(dev, state, kappa.reshape(1, columns), jnp.asarray(diffusion_matrix(columns)),
      jnp.asarray(edge_matrix(columns)), edge_nbrs.T, jnp.asarray(table), jnp.asarray(holder))

    member2, base = lax.optimization_barrier((member2, base))
    member3 = trade(member2, 1)
    low = lax.ppermute(edges, AXES, [(i, (i + 1) % devices) for i in range(devices)])
    high = lax.ppermute(edges, AXES, [(i, (i - 1) % devices) for i in range(devices)])

    bf = lambda *shape: pltpu.VMEM(shape, BF16)
    lanes = 2 * columns // GROUP
    *results, code = pl.pallas_call(
        functools.partial(net_kernel, levels, fields),
        out_shape=[bf16((rows // 2, lanes))] * GROUP + [i32((1, columns))],
        in_specs=[SMEM] + [VMEM] * (GROUP + 1) + [pl.BlockSpec(memory_space=pl.ANY), VMEM],
        out_specs=[VMEM] * (GROUP + 1),
        scratch_shapes=[
            bf(rows + 16, GROUP * columns),
            bf(GROUP * columns, 9 * 128),
            bf(levels, 80, 128),
            bf(levels + 2, columns, 128),
            bf(3 * 128, ch),
            bf(*w_inner.shape),
            bf(levels + 2, NB, ch),
            bf(levels, NB, ch),
            bf(levels // 2 + 2, NB, ch),
            bf(levels // 2, NB, ch),
            bf(levels // 4 + 2, NB, ch),
            bf(levels // 2 + 2, NB, ch),
            bf(levels + 2, NB, ch),
            bf(levels, NB, ch),
            pltpu.VMEM((24, (levels + 2) * NB), F32),
            pltpu.VMEM((rows // 2, GROUP * lanes), F32),
            pltpu.VMEM((columns, 128), F32),
            pltpu.SemaphoreType.DMA,
        ],
        compiler_params=pltpu.CompilerParams(vmem_limit_bytes=30 * 1024 * 1024),
        cost_estimate=pl.CostEstimate(flops=10**10, bytes_accessed=2**22, transcendentals=10**7),
        name="network",
    )(dev, payload, member1, member2, member3, w_first, w_inner, w_last.T)
    back = [trade(results[d], d) for d in range(1, GROUP)]

    middle = pl.pallas_call(
        middle_kernel,
        out_shape=f32((rows, columns)),
        in_specs=[VMEM] * 4,
        out_specs=VMEM,
        cost_estimate=pl.CostEstimate(flops=10**9, bytes_accessed=2**22, transcendentals=0),
        compiler_params=SMALL,
        name="middle",
    )(*lax.optimization_barrier((base, low, high, facing, results[0]))[:4])

    return pl.pallas_call(
        final_kernel,
        out_shape=f32((fields, levels, columns)),
        in_specs=[VMEM] * 6,
        out_specs=VMEM,
        compiler_params=SMALL,
        name="combine",
    )(middle.reshape(fields, levels, columns), code, results[0], *back)


def solution(mesh):
    in_specs = (
        P(None, None, AXES),
        P(AXES),
        P(AXES, None),
        P(AXES, None),
        P(AXES),
        P(),
        P(),
        P(),
    )
    return jax.shard_map(
        per_device, mesh=mesh, in_specs=in_specs, out_specs=P(None, None, AXES), check_vma=False
    )
```

```python
import functools
import math

import jax
import jax.numpy as jnp
import numpy as np
from jax import lax
from jax.experimental import pallas as pl
from jax.experimental.pallas import tpu as pltpu
from jax.sharding import PartitionSpec as P

AXES = ("grp", "elem")
EDGE_NODES = ((1, 2), (7, 11), (14, 13), (8, 4))
VMEM = pl.BlockSpec(memory_space=pltpu.VMEM)
HBM = pl.BlockSpec(memory_space=pltpu.HBM)
SMALL = pltpu.CompilerParams(vmem_limit_bytes=12 * 1024 * 1024)
SMEM = pl.BlockSpec(memory_space=pltpu.SMEM)
HIGHEST = lax.Precision.HIGHEST
BF16 = jnp.bfloat16
F32 = jnp.float32
NB = 16
STEP = 12
GROUP = 4


def second_derivative():
    points = np.array([-1.0, -math.sqrt(0.2), math.sqrt(0.2), 1.0])
    factors = np.array(
        [1.0 / np.prod([points[j] - points[m] for m in range(4) if m != j]) for j in range(4)]
    )
    deriv = np.zeros((4, 4))
    for i in range(4):
        for j in range(4):
            if i != j:
                deriv[i, j] = factors[j] / factors[i] / (points[i] - points[j])
        deriv[i, i] = -np.sum(deriv[i])
    return deriv @ deriv


def diffusion_matrix(columns):
    lap = second_derivative()
    eye = np.eye(4)
    node = np.einsum("ia,jb->abij", lap, eye) + np.einsum("ia,jb->abij", eye, lap)
    return np.kron(np.eye(columns // 16), node.reshape(16, 16)).astype(np.float32)


def edge_matrix(columns):
    sel = np.zeros((columns, columns // 2), np.float32)
    for e in range(columns // 16):
        for k in range(4):
            for m in range(2):
                sel[16 * e + EDGE_NODES[k][m], 8 * e + 2 * k + m] = 1
    return sel


def node_tables(columns):
    on_edge = np.zeros((4, columns), np.float32)
    offset = np.zeros((1, columns), np.float32)
    for k in range(4):
        for m in range(2):
            on_edge[k, EDGE_NODES[k][m] :: 16] = 1
            offset[0, EDGE_NODES[k][m] :: 16] = (k + 2) % 4 * 2 + 1 - m
    holder = np.kron(np.eye(columns // 16), np.ones((1, 16))).astype(np.float32)
    table = np.concatenate([on_edge, offset, np.zeros((3, columns), np.float32)], axis=0)
    return table, holder


def iota(shape, dim):
    return lax.broadcasted_iota(jnp.int32, shape, dim)


def silu(values):
    half = 0.5 * values
    return half + half * jnp.tanh(half)


def pack_kernel(dev_ref, state_hbm, sten_hbm, owner_hbm, pay_ref, state_ref, sten_ref, owner_ref, sem):
    fields, levels, columns = state_ref.shape
    rows = fields * levels
    copies = [pltpu.make_async_copy(src, dst, sem.at[i]) for i, (src, dst) in enumerate((
        (state_hbm, state_ref), (sten_hbm, sten_ref), (owner_hbm, owner_ref)))]
    for copy in copies:
        copy.start()
    for copy in copies:
        copy.wait()
    for l in range(0, levels, 2):
        pair = jnp.concatenate([state_ref[:, l, :], state_ref[:, l + 1, :]], axis=0)
        pay_ref[l * fields : (l + 2) * fields, :] = pair.astype(BF16)
    local = (sten_ref[...] - dev_ref[0] * columns).astype(F32)
    flag = jnp.where(owner_ref[...] >= 0, 1.0, 0.0)
    tail = jnp.concatenate([local, flag, jnp.zeros((6, columns), F32)], axis=0)
    pay_ref[rows : rows + 16, :] = tail.astype(BF16)


def edges_kernel(total, dev_ref, state_ref, kappa_ref, op_ref, sel_ref, nbr_ref, table_ref, holder_ref,
                 base_ref, edge_ref, facing_ref):
    fields, levels, columns = state_ref.shape
    elements = columns // 16
    flat = state_ref[...].reshape(fields * levels, columns)
    dyn = kappa_ref[...] * jnp.dot(flat, op_ref[...], precision=HIGHEST)
    edge = jnp.dot(dyn, sel_ref[...], precision=HIGHEST)
    edge_ref[...] = edge.astype(BF16)
    rel = lax.rem(nbr_ref[...] - (dev_ref[0] - 1) * elements + total, total).astype(F32)
    spread = jnp.dot(rel, holder_ref[...], precision=HIGHEST)
    on_edge = table_ref[0:4, :]
    is_edge = jnp.sum(on_edge, axis=0, keepdims=True)
    facing = 8.0 * jnp.sum(spread * on_edge, axis=0, keepdims=True) + table_ref[4:5, :]
    facing = jnp.where(is_edge > 0, facing, -1.0).astype(jnp.int32)
    facing_ref[...] = facing
    half = columns // 2
    pick = jnp.where(iota((half, columns), 0) + half == facing, 0.5, 0.0)
    own = jnp.dot(edge, pick, precision=HIGHEST)
    base_ref[...] = flat + (1.0 - 0.5 * is_edge) * dyn + own


def land(code, d, quota, columns):
    slot = jnp.where((code >= d * quota) & (code < (d + 1) * quota), code - d * quota, -2 * quota)
    spot = iota((2 * quota, columns), 0)
    return [jnp.where(spot == slot + h * quota, 1.0, 0.0).astype(BF16) for h in range(2)]


def middle_kernel(base_ref, low_ref, high_ref, facing_ref, out_ref):
    rows, columns = base_ref.shape
    half = columns // 2
    facing = facing_ref[...]
    acc = base_ref[...]
    for part, ref in ((0, low_ref), (2, high_ref)):
        pick = jnp.where(iota((half, columns), 0) + part * half == facing, 0.5, 0.0).astype(BF16)
        acc = acc + jnp.dot(ref[...], pick, preferred_element_type=F32)
    out_ref[...] = acc


def final_kernel(base_ref, code_ref, r0_ref, r1_ref, r2_ref, r3_ref, out_ref):
    fields, levels, columns = out_ref.shape
    quota = columns // GROUP
    code = code_ref[...]
    got = jnp.concatenate([r0_ref[...], r1_ref[...], r2_ref[...], r3_ref[...]], axis=1)
    puts = [land(code, d, quota, columns) for d in range(GROUP)]
    for h in range(2):
        put = jnp.concatenate([p[h] for p in puts], axis=0)
        physics = jnp.dot(got, put, preferred_element_type=F32)
        for i in range(levels // 2):
            l = h * (levels // 2) + i
            out_ref[:, l, :] = base_ref[:, l, :] + physics[i * fields : (i + 1) * fields, :]


def halve(y):
    y = y.reshape(y.shape[0] // 2, 2, *y.shape[1:]).astype(F32)
    return ((y[:, 0] + y[:, 1]) * 0.5).astype(BF16)


def widen(coarse, fine):
    step, cols, ch = coarse.shape
    wide = jnp.broadcast_to(coarse[:, None], (step, 2, cols, ch)).reshape(2 * step, cols, ch)
    return (wide.astype(F32) + fine.astype(F32)).astype(BF16)


def net_kernel(levels, fields, dev_ref, m0_ref, m1_ref, m2_ref, m3_ref, w1_ref, w_ref, wl_ref,
               r0_ref, r1_ref, r2_ref, r3_ref, code_ref,
               oh_ref, g_ref, net_ref, w1s_ref, first_ref, second_ref, pool2_ref, third_ref,
               pool3_ref, join3_ref, join2_ref, top_ref, p_ref, acc_ref, to_ref):
    rows = fields * levels
    columns = m0_ref.shape[1]
    quota = columns // GROUP
    wide = GROUP * columns
    ch = wl_ref.shape[1] // 3
    taps = 9 * fields
    half2, half3 = levels // 2, levels // 4

    for ref, n in ((first_ref, levels), (pool2_ref, half2), (pool3_ref, half3), (join3_ref, half2),
                   (join2_ref, levels)):
        zero = jnp.zeros(ref.shape[1:], BF16)
        ref[0] = zero
        ref[n + 1] = zero
    net_ref[0] = jnp.zeros(net_ref.shape[1:], BF16)
    net_ref[levels + 1] = jnp.zeros(net_ref.shape[1:], BF16)
    net_ref[:, :, 80:128] = jnp.zeros((levels + 2, columns, 48), BF16)
    p_ref[:, 0:128] = jnp.zeros((24, 128), F32)
    p_ref[:, levels * NB + 128 :] = jnp.zeros((24, 128), F32)
    w1s_ref[...] = jnp.zeros(w1s_ref.shape, BF16)
    for t in range(3):
        w1s_ref[128 * t : 128 * t + taps, :] = w1_ref[taps * t : taps * (t + 1), :]
    acc_ref[...] = jnp.zeros(acc_ref.shape, F32)
    w24 = jnp.concatenate([wl_ref[:, ch * t : ch * (t + 1)].astype(F32) for t in range(3)], axis=0).astype(BF16)

    me = lax.rem(dev_ref[0], GROUP)
    members = (m0_ref, m1_ref, m2_ref, m3_ref)
    upto = jnp.where(iota((columns, columns), 0) < iota((columns, columns), 1), 1.0, 0.0).astype(BF16)
    metas = [ref[rows : rows + 16, :] for ref in members]
    flags = [meta.astype(F32)[9:10, :] for meta in metas]
    counts = [jnp.sum(flag, axis=1, keepdims=True) for flag in flags]
    ranks, targets, active = [], [], jnp.zeros((1, 1), F32)
    for d in range(GROUP):
        start = jnp.zeros((1, 1), F32)
        for other in range(GROUP):
            start = start + jnp.where((me ^ other) < (me ^ d), counts[other], 0.0)
        local = jnp.dot(metas[d], upto, preferred_element_type=F32)[9:10, :].astype(jnp.int32)
        rank = local + start.astype(jnp.int32)
        ranks.append(jnp.where(flags[d] > 0, rank, -1))
        targets.append(jnp.where(flags[d] > 0, d * quota + local // GROUP + 1, 0).astype(F32))
        if d == 0:
            code_ref[...] = jnp.where(flags[d] > 0, (lax.rem(rank, GROUP) ^ me) * quota + local // GROUP, -1)
        active = active + counts[d]
    meta = jnp.concatenate(metas, axis=1)
    rank = jnp.concatenate(ranks, axis=1)
    share = (jnp.sum(active).astype(jnp.int32) - me + GROUP - 1) // GROUP
    slot = GROUP * iota((columns, wide), 0) + me
    choose = jnp.where(slot == rank, 1.0, 0.0).astype(BF16)
    flip = (((1,), (1,)), ((), ()))
    sten = lax.dot_general(meta, choose, flip, preferred_element_type=F32)
    part = (iota((16, wide), 1) // columns).astype(F32).astype(BF16)
    part = lax.dot_general(part, choose, flip, preferred_element_type=F32)
    sten = (sten + columns * part).astype(jnp.int32)
    target = jnp.broadcast_to(jnp.concatenate(targets, axis=1), (128, wide)).astype(BF16)
    to_ref[...] = lax.dot_general(choose, target, flip, preferred_element_type=F32) - 1.0

    @pl.loop(0, (share + 127) // 128)
    def _(q):
        lanes = pl.ds(pl.multiple_of(q * 128, 128), 128)
        for k in range(9):
            for half in range(columns // 128):
                here = sten[k : k + 1, half * 128 : (half + 1) * 128]
                picked = here if half == 0 else jnp.where(q == half, here, picked)
            oh_ref[:, k * 128 : (k + 1) * 128] = jnp.where(iota((wide, 128), 0) == picked, 1.0, 0.0).astype(BF16)
        for k in range(0, 9, 2):
            n = 2 if k < 8 else 1
            got = jnp.dot(jnp.concatenate([ref[0:rows, :] for ref in members], axis=1), oh_ref[:, k * 128 : (k + n) * 128], preferred_element_type=F32)
            parts = [got[:, u * 128 : (u + 1) * 128].reshape(levels, fields, 128) for u in range(n)]
            if n == 1:
                parts.append(jnp.zeros_like(parts[0]))
            g_ref[0:levels, k * 8 : k * 8 + 16, :] = jnp.concatenate(parts, axis=1).astype(BF16)

        for l in range(levels):
            net_ref[l + 1, lanes, 0:80] = g_ref[l].T

    mask = jnp.where(iota((128 // NB * 8, 128), 0) // 8 == iota((128 // NB * 8, 128), 1) // NB, 1.0, 0.0)

    @pl.loop(0, (share + NB - 1) // NB)
    def _(b):
        c0 = pl.multiple_of(b * NB, NB)

        pending = []

        def flush():
            for item in pending:
                item()
            pending.clear()

        def conv(load, weight, n, emit):
            step = max(s for s in range(1, STEP + 1) if n % s == 0)
            for l0 in range(0, n, step):
                x = [load(l0 + t, step).reshape(step * NB, -1) for t in range(3)]
                acc = jnp.dot(jnp.concatenate(x, axis=1), weight, preferred_element_type=F32)
                flush()
                pending.append(lambda emit=emit, l0=l0, step=step, acc=acc: emit(
                    l0, step, silu(acc).astype(BF16).reshape(step, NB, ch)))

        def emit_first(l0, step, y):
            first_ref[l0 + 1 : l0 + 1 + step] = y

        def emit_second(l0, step, y):
            second_ref[l0 : l0 + step] = y
            pool2_ref[l0 // 2 + 1 : l0 // 2 + 1 + step // 2] = halve(y)

        def emit_third(l0, step, y):
            third_ref[l0 : l0 + step] = y
            pool3_ref[l0 // 2 + 1 : l0 // 2 + 1 + step // 2] = halve(y)

        def emit_deepest(l0, step, y):
            fine = third_ref[2 * l0 : 2 * (l0 + step)]
            join3_ref[2 * l0 + 1 : 2 * (l0 + step) + 1] = widen(y, fine)

        def emit_upper(l0, step, y):
            fine = second_ref[2 * l0 : 2 * (l0 + step)]
            join2_ref[2 * l0 + 1 : 2 * (l0 + step) + 1] = widen(y, fine)

        def emit_top(l0, step, y):
            top_ref[l0 : l0 + step] = y

        conv(lambda l, n: net_ref[l : l + n, pl.ds(c0, NB), :], w1s_ref[...], levels, emit_first)
        conv(lambda l, n: first_ref[l : l + n], w_ref[0], levels, emit_second)
        conv(lambda l, n: pool2_ref[l : l + n], w_ref[1], half2, emit_third)
        conv(lambda l, n: pool3_ref[l : l + n], w_ref[2], half3, emit_deepest)
        conv(lambda l, n: join3_ref[l : l + n], w_ref[3], half2, emit_upper)
        conv(lambda l, n: join2_ref[l : l + n], w_ref[4], levels, emit_top)

        flush()
        group = 384
        for i in range(0, levels * NB, group):
            x = top_ref[i // NB : (i + group) // NB].reshape(group, ch)
            p_ref[:, i + 128 : i + group + 128] = lax.dot_general(w24, x, flip, preferred_element_type=F32)
        n = levels * NB
        out = p_ref[0:8, 128 - NB : n + 128 - NB] + p_ref[8:16, 128 : n + 128] + p_ref[16:24, 128 + NB : n + 128 + NB]
        tiles = []
        for i in range(n // 128):
            tile = out[:, i * 128 : (i + 1) * 128]
            tiles.append(jnp.concatenate([tile] * (128 // NB), axis=0) * mask)
        flat = jnp.concatenate(tiles, axis=0).astype(BF16)
        to = to_ref[pl.ds(c0, NB), :].astype(jnp.int32)
        for h in range(2):
            lane = jnp.where(to >= 0, to // quota * (2 * quota) + lax.rem(to, quota) + h * quota, -1)
            lane = jnp.concatenate([lane] * (128 // NB), axis=0)
            place = [jnp.where(lane == iota((128, 128), 1) + i * 128, 1.0, 0.0) for i in range(2 * columns // 128)]
            place = jnp.concatenate(place, axis=1).astype(BF16)
            acc_ref[...] += jnp.dot(flat[h * rows // 2 : (h + 1) * rows // 2], place, preferred_element_type=F32)

    for d, ref in enumerate((r0_ref, r1_ref, r2_ref, r3_ref)):
        ref[...] = acc_ref[:, d * 2 * quota : (d + 1) * 2 * quota].astype(BF16)


def per_device(state, kappa, edge_nbrs, stencil, owner, w_first, w_inner, w_last):
    fields, levels, columns = state.shape
    rows = fields * levels
    ch = w_inner.shape[2]
    devices = lax.axis_size(AXES)
    device = lax.axis_index(AXES)
    total = columns // 16 * devices
    dev = device.astype(jnp.int32).reshape(1)
    table, holder = node_tables(columns)
    f32 = functools.partial(jax.ShapeDtypeStruct, dtype=F32)
    bf16 = functools.partial(jax.ShapeDtypeStruct, dtype=BF16)
    i32 = functools.partial(jax.ShapeDtypeStruct, dtype=jnp.int32)

    payload = pl.pallas_call(
        pack_kernel,
        out_shape=bf16((rows + 16, columns)),
        in_specs=[SMEM] + [HBM] * 3,
        out_specs=VMEM,
        scratch_shapes=[
            pltpu.VMEM(state.shape, F32),
            pltpu.VMEM((9, columns), jnp.int32),
            pltpu.VMEM((1, columns), jnp.int32),
            pltpu.SemaphoreType.DMA((3,)),
        ],
        compiler_params=SMALL,
        name="pack",
    )(dev, state, stencil.T, owner.reshape(1, columns))
    def trade(x, d):
        return lax.ppermute(x, AXES, [(i, i ^ d) for i in range(devices)])

    member1 = trade(payload, 1)
    member2 = trade(payload, 2)

    base, edges, facing = pl.pallas_call(
        functools.partial(edges_kernel, total),
        out_shape=(f32((rows, columns)), bf16((rows, columns // 2)), i32((1, columns))),
        in_specs=[SMEM] + [VMEM] * 7,
        out_specs=(VMEM, VMEM, VMEM),
        cost_estimate=pl.CostEstimate(flops=3 * 10**9, bytes_accessed=2**21, transcendentals=0),
        name="edges",
    )(dev, state, kappa.reshape(1, columns), jnp.asarray(diffusion_matrix(columns)),
      jnp.asarray(edge_matrix(columns)), edge_nbrs.T, jnp.asarray(table), jnp.asarray(holder))

    member2, base = lax.optimization_barrier((member2, base))
    member3 = trade(member2, 1)
    low = lax.ppermute(edges, AXES, [(i, (i + 1) % devices) for i in range(devices)])
    high = lax.ppermute(edges, AXES, [(i, (i - 1) % devices) for i in range(devices)])

    bf = lambda *shape: pltpu.VMEM(shape, BF16)
    lanes = 2 * columns // GROUP
    *results, code = pl.pallas_call(
        functools.partial(net_kernel, levels, fields),
        out_shape=[bf16((rows // 2, lanes))] * GROUP + [i32((1, columns))],
        in_specs=[SMEM] + [VMEM] * (GROUP + 1) + [VMEM] * 2,
        out_specs=[VMEM] * (GROUP + 1),
        scratch_shapes=[
            bf(GROUP * columns, 9 * 128),
            bf(levels, 80, 128),
            bf(levels + 2, columns, 128),
            bf(3 * 128, ch),
            bf(levels + 2, NB, ch),
            bf(levels, NB, ch),
            bf(levels // 2 + 2, NB, ch),
            bf(levels // 2, NB, ch),
            bf(levels // 4 + 2, NB, ch),
            bf(levels // 2 + 2, NB, ch),
            bf(levels + 2, NB, ch),
            bf(levels, NB, ch),
            pltpu.VMEM((24, levels * NB + 256), F32),
            pltpu.VMEM((rows // 2, GROUP * lanes), F32),
            pltpu.VMEM((columns, 128), F32),
        ],
        compiler_params=pltpu.CompilerParams(vmem_limit_bytes=30 * 1024 * 1024),
        cost_estimate=pl.CostEstimate(flops=10**10, bytes_accessed=2**22, transcendentals=10**7),
        name="network",
    )(dev, payload, member1, member2, member3, w_first, w_inner, w_last.T)
    back = [trade(results[d], d) for d in (3, 2, 1)][::-1]

    middle = pl.pallas_call(
        middle_kernel,
        out_shape=f32((rows, columns)),
        in_specs=[VMEM] * 4,
        out_specs=VMEM,
        cost_estimate=pl.CostEstimate(flops=10**9, bytes_accessed=2**22, transcendentals=0),
        compiler_params=SMALL,
        name="middle",
    )(*lax.optimization_barrier((base, low, high, facing, results[0]))[:4])

    return pl.pallas_call(
        final_kernel,
        out_shape=f32((fields, levels, columns)),
        in_specs=[VMEM] * 6,
        out_specs=VMEM,
        compiler_params=SMALL,
        name="combine",
    )(middle.reshape(fields, levels, columns), code, results[0], *back)


def solution(mesh):
    in_specs = (
        P(None, None, AXES),
        P(AXES),
        P(AXES, None),
        P(AXES, None),
        P(AXES),
        P(),
        P(),
        P(),
    )
    return jax.shard_map(
        per_device, mesh=mesh, in_specs=in_specs, out_specs=P(None, None, AXES), check_vma=False
    )
```

```python
import functools
import math

import jax
import jax.numpy as jnp
import numpy as np
from jax import lax
from jax.experimental import pallas as pl
from jax.experimental.pallas import tpu as pltpu
from jax.sharding import PartitionSpec as P

AXES = ("grp", "elem")
EDGE_NODES = ((1, 2), (7, 11), (14, 13), (8, 4))
VMEM = pl.BlockSpec(memory_space=pltpu.VMEM)
SMALL = pltpu.CompilerParams(vmem_limit_bytes=12 * 1024 * 1024)
SMEM = pl.BlockSpec(memory_space=pltpu.SMEM)
HIGHEST = lax.Precision.HIGHEST
BF16 = jnp.bfloat16
F32 = jnp.float32
NB = 32
STEP = 12
GROUP = 4


def second_derivative():
    points = np.array([-1.0, -math.sqrt(0.2), math.sqrt(0.2), 1.0])
    factors = np.array(
        [1.0 / np.prod([points[j] - points[m] for m in range(4) if m != j]) for j in range(4)]
    )
    deriv = np.zeros((4, 4))
    for i in range(4):
        for j in range(4):
            if i != j:
                deriv[i, j] = factors[j] / factors[i] / (points[i] - points[j])
        deriv[i, i] = -np.sum(deriv[i])
    return deriv @ deriv


def diffusion_matrix(columns):
    lap = second_derivative()
    eye = np.eye(4)
    node = np.einsum("ia,jb->abij", lap, eye) + np.einsum("ia,jb->abij", eye, lap)
    return np.kron(np.eye(columns // 16), node.reshape(16, 16)).astype(np.float32)


def edge_matrix(columns):
    sel = np.zeros((columns, columns // 2), np.float32)
    for e in range(columns // 16):
        for k in range(4):
            for m in range(2):
                sel[16 * e + EDGE_NODES[k][m], 8 * e + 2 * k + m] = 1
    return sel


def node_tables(columns):
    on_edge = np.zeros((4, columns), np.float32)
    offset = np.zeros((1, columns), np.float32)
    for k in range(4):
        for m in range(2):
            on_edge[k, EDGE_NODES[k][m] :: 16] = 1
            offset[0, EDGE_NODES[k][m] :: 16] = (k + 2) % 4 * 2 + 1 - m
    holder = np.kron(np.eye(columns // 16), np.ones((1, 16))).astype(np.float32)
    table = np.concatenate([on_edge, offset, np.zeros((3, columns), np.float32)], axis=0)
    return table, holder


def iota(shape, dim):
    return lax.broadcasted_iota(jnp.int32, shape, dim)


def silu(half):
    return half + half * jnp.tanh(half)


def pack_kernel(dev_ref, state_ref, sten_ref, owner_ref, pay_ref):
    fields, levels, columns = state_ref.shape
    rows = fields * levels
    for l in range(0, levels, 2):
        pair = jnp.concatenate([state_ref[:, l, :], state_ref[:, l + 1, :]], axis=0)
        pay_ref[l * fields : (l + 2) * fields, :] = pair.astype(BF16)
    local = (sten_ref[...] - dev_ref[0] * columns).astype(F32)
    flag = jnp.where(owner_ref[...] >= 0, 1.0, 0.0)
    tail = jnp.concatenate([local, flag, jnp.zeros((6, columns), F32)], axis=0)
    pay_ref[rows : rows + 16, :] = tail.astype(BF16)


def edges_kernel(total, dev_ref, state_ref, kappa_ref, op_ref, sel_ref, nbr_ref, table_ref, holder_ref,
                 w1_ref, wi_ref, wl_ref, base_ref, edge_ref, facing_ref, w1s_ref, wis_ref, w24_ref):
    fields, levels, columns = state_ref.shape
    elements = columns // 16
    flat = state_ref[...].reshape(fields * levels, columns)
    dyn = kappa_ref[...] * jnp.dot(flat, op_ref[...], precision=HIGHEST)
    edge = jnp.dot(dyn, sel_ref[...], precision=HIGHEST)
    edge_ref[...] = edge.astype(BF16)
    rel = lax.rem(nbr_ref[...] - (dev_ref[0] - 1) * elements + total, total).astype(F32)
    spread = jnp.dot(rel, holder_ref[...], precision=HIGHEST)
    on_edge = table_ref[0:4, :]
    is_edge = jnp.sum(on_edge, axis=0, keepdims=True)
    facing = 8.0 * jnp.sum(spread * on_edge, axis=0, keepdims=True) + table_ref[4:5, :]
    facing = jnp.where(is_edge > 0, facing, -1.0).astype(jnp.int32)
    facing_ref[...] = facing
    half = columns // 2
    pick = jnp.where(iota((half, columns), 0) + half == facing, 0.5, 0.0)
    own = jnp.dot(edge, pick, precision=HIGHEST)
    base_ref[...] = flat + (1.0 - 0.5 * is_edge) * dyn + own
    taps = 9 * fields
    ch = wi_ref.shape[2]
    w1s_ref[...] = jnp.zeros(w1s_ref.shape, BF16)
    for t in range(3):
        w1s_ref[128 * t : 128 * t + taps, :] = w1_ref[taps * t : taps * (t + 1), :] * BF16(0.5)
    wis_ref[...] = wi_ref[...] * BF16(0.5)
    parts = [wl_ref[:, ch * t : ch * (t + 1)].astype(F32) for t in range(3)]
    w24_ref[...] = jnp.concatenate(parts, axis=0).astype(BF16)


def land(code, d, quota, columns):
    slot = jnp.where((code >= d * quota) & (code < (d + 1) * quota), code - d * quota, -2 * quota)
    spot = iota((2 * quota, columns), 0)
    return [jnp.where(spot == slot + h * quota, 1.0, 0.0).astype(BF16) for h in range(2)]


def middle_kernel(base_ref, low_ref, high_ref, facing_ref, out_ref):
    rows, columns = base_ref.shape
    half = columns // 2
    facing = facing_ref[...]
    acc = base_ref[...]
    for part, ref in ((0, low_ref), (2, high_ref)):
        pick = jnp.where(iota((half, columns), 0) + part * half == facing, 0.5, 0.0).astype(BF16)
        acc = acc + jnp.dot(ref[...], pick, preferred_element_type=F32)
    out_ref[...] = acc


def final_kernel(base_ref, code_ref, r0_ref, r1_ref, r2_ref, r3_ref, out_ref):
    fields, levels, columns = out_ref.shape
    quota = columns // GROUP
    code = code_ref[...]
    got = jnp.concatenate([r0_ref[...], r1_ref[...], r2_ref[...], r3_ref[...]], axis=1)
    puts = [land(code, d, quota, columns) for d in range(GROUP)]
    for h in range(2):
        put = jnp.concatenate([p[h] for p in puts], axis=0)
        physics = jnp.dot(got, put, preferred_element_type=F32)
        for i in range(levels // 2):
            l = h * (levels // 2) + i
            out_ref[:, l, :] = base_ref[:, l, :] + physics[i * fields : (i + 1) * fields, :]


def halve(y):
    y = y.reshape(y.shape[0] // 2, 2, *y.shape[1:])
    return (y[:, 0] + y[:, 1]) * BF16(0.5)


def widen(coarse, fine):
    step, cols, ch = coarse.shape
    return jnp.broadcast_to(coarse[:, None], (step, 2, cols, ch)).reshape(2 * step, cols, ch) + fine


def net_kernel(levels, fields, dev_ref, m0_ref, m1_ref, m2_ref, m3_ref, w1s_ref, w_ref, w24_ref,
               r0_ref, r1_ref, r2_ref, r3_ref, code_ref,
               oh_ref, g_ref, net_ref, first_ref, second_ref, pool2_ref, third_ref,
               pool3_ref, join3_ref, join2_ref, top_ref, p_ref, acc_ref, to_ref):
    rows = fields * levels
    columns = m0_ref.shape[1]
    quota = columns // GROUP
    wide = GROUP * columns
    ch = w_ref.shape[2]
    half2, half3 = levels // 2, levels // 4

    for ref, n in ((first_ref, levels), (pool2_ref, half2), (pool3_ref, half3), (join3_ref, half2),
                   (join2_ref, levels)):
        zero = jnp.zeros(ref.shape[1:], BF16)
        ref[0] = zero
        ref[n + 1] = zero
    net_ref[0] = jnp.zeros(net_ref.shape[1:], BF16)
    net_ref[levels + 1] = jnp.zeros(net_ref.shape[1:], BF16)
    net_ref[:, :, 80:128] = jnp.zeros((levels + 2, columns, 48), BF16)
    p_ref[:, 0:128] = jnp.zeros((24, 128), F32)
    p_ref[:, levels * NB + 128 :] = jnp.zeros((24, 128), F32)
    acc_ref[...] = jnp.zeros(acc_ref.shape, F32)

    me = lax.rem(dev_ref[0], GROUP)
    members = (m0_ref, m1_ref, m2_ref, m3_ref)
    upto = jnp.where(iota((columns, columns), 0) < iota((columns, columns), 1), 1.0, 0.0).astype(BF16)
    metas = [ref[rows : rows + 16, :] for ref in members]
    flags = [meta.astype(F32)[9:10, :] for meta in metas]
    counts = [jnp.sum(flag, axis=1, keepdims=True) for flag in flags]
    ranks, targets, active = [], [], jnp.zeros((1, 1), F32)
    for d in range(GROUP):
        start = jnp.zeros((1, 1), F32)
        for other in range(GROUP):
            start = start + jnp.where((me ^ other) < (me ^ d), counts[other], 0.0)
        local = jnp.dot(metas[d], upto, preferred_element_type=F32)[9:10, :].astype(jnp.int32)
        rank = local + start.astype(jnp.int32)
        ranks.append(jnp.where(flags[d] > 0, rank, -1))
        targets.append(jnp.where(flags[d] > 0, d * quota + local // GROUP + 1, 0).astype(F32))
        if d == 0:
            code_ref[...] = jnp.where(flags[d] > 0, (lax.rem(rank, GROUP) ^ me) * quota + local // GROUP, -1)
        active = active + counts[d]
    meta = jnp.concatenate(metas, axis=1)
    rank = jnp.concatenate(ranks, axis=1)
    share = (jnp.sum(active).astype(jnp.int32) - me + GROUP - 1) // GROUP
    slot = GROUP * iota((columns, wide), 0) + me
    choose = jnp.where(slot == rank, 1.0, 0.0).astype(BF16)
    flip = (((1,), (1,)), ((), ()))
    sten = lax.dot_general(meta, choose, flip, preferred_element_type=F32)
    part = (iota((16, wide), 1) // columns).astype(F32).astype(BF16)
    part = lax.dot_general(part, choose, flip, preferred_element_type=F32)
    sten = (sten + columns * part).astype(jnp.int32)
    target = jnp.broadcast_to(jnp.concatenate(targets, axis=1), (128, wide)).astype(BF16)
    to_ref[...] = lax.dot_general(choose, target, flip, preferred_element_type=F32) - 1.0

    @pl.loop(0, (share + 127) // 128)
    def _(q):
        lanes = pl.ds(pl.multiple_of(q * 128, 128), 128)
        for k in range(9):
            for half in range(columns // 128):
                here = sten[k : k + 1, half * 128 : (half + 1) * 128]
                picked = here if half == 0 else jnp.where(q == half, here, picked)
            oh_ref[:, k * 128 : (k + 1) * 128] = jnp.where(iota((wide, 128), 0) == picked, 1.0, 0.0).astype(BF16)
        for k in range(0, 9, 2):
            n = 2 if k < 8 else 1
            got = jnp.dot(jnp.concatenate([ref[0:rows, :] for ref in members], axis=1), oh_ref[:, k * 128 : (k + n) * 128], preferred_element_type=F32)
            parts = [got[:, u * 128 : (u + 1) * 128].reshape(levels, fields, 128) for u in range(n)]
            if n == 1:
                parts.append(jnp.zeros_like(parts[0]))
            g_ref[0:levels, k * 8 : k * 8 + 16, :] = jnp.concatenate(parts, axis=1).astype(BF16)

        for l in range(levels):
            net_ref[l + 1, lanes, 0:80] = g_ref[l].T

    mask = jnp.where(iota((128 // NB * 8, 128), 0) // 8 == iota((128 // NB * 8, 128), 1) // NB, 1.0, 0.0)

    @pl.loop(0, (share + NB - 1) // NB)
    def _(b):
        c0 = pl.multiple_of(b * NB, NB)

        pending = []

        def flush():
            for item in pending:
                item()
            pending.clear()

        def conv(load, weight, n, emit):
            step = max(s for s in range(1, STEP + 1) if n % s == 0)
            for l0 in range(0, n, step):
                x = [load(l0 + t, step).reshape(step * NB, -1) for t in range(3)]
                acc = jnp.dot(jnp.concatenate(x, axis=1), weight, preferred_element_type=F32)
                flush()
                pending.append(lambda emit=emit, l0=l0, step=step, acc=acc: emit(
                    l0, step, silu(acc).astype(BF16).reshape(step, NB, ch)))

        def emit_first(l0, step, y):
            first_ref[l0 + 1 : l0 + 1 + step] = y

        def emit_second(l0, step, y):
            second_ref[l0 : l0 + step] = y
            pool2_ref[l0 // 2 + 1 : l0 // 2 + 1 + step // 2] = halve(y)

        def emit_third(l0, step, y):
            third_ref[l0 : l0 + step] = y
            pool3_ref[l0 // 2 + 1 : l0 // 2 + 1 + step // 2] = halve(y)

        def emit_deepest(l0, step, y):
            fine = third_ref[2 * l0 : 2 * (l0 + step)]
            join3_ref[2 * l0 + 1 : 2 * (l0 + step) + 1] = widen(y, fine)

        def emit_upper(l0, step, y):
            fine = second_ref[2 * l0 : 2 * (l0 + step)]
            join2_ref[2 * l0 + 1 : 2 * (l0 + step) + 1] = widen(y, fine)

        def emit_top(l0, step, y):
            top_ref[l0 : l0 + step] = y

        conv(lambda l, n: net_ref[l : l + n, pl.ds(c0, NB), :], w1s_ref[...], levels, emit_first)
        conv(lambda l, n: first_ref[l : l + n], w_ref[0], levels, emit_second)
        conv(lambda l, n: pool2_ref[l : l + n], w_ref[1], half2, emit_third)
        conv(lambda l, n: pool3_ref[l : l + n], w_ref[2], half3, emit_deepest)
        conv(lambda l, n: join3_ref[l : l + n], w_ref[3], half2, emit_upper)
        conv(lambda l, n: join2_ref[l : l + n], w_ref[4], levels, emit_top)

        flush()
        group = 384
        for i in range(0, levels * NB, group):
            x = top_ref[i // NB : (i + group) // NB].reshape(group, ch)
            p_ref[:, i + 128 : i + group + 128] = lax.dot_general(w24_ref[...], x, flip, preferred_element_type=F32)
        n = levels * NB
        out = p_ref[0:8, 128 - NB : n + 128 - NB] + p_ref[8:16, 128 : n + 128] + p_ref[16:24, 128 + NB : n + 128 + NB]
        tiles = []
        for i in range(n // 128):
            tile = out[:, i * 128 : (i + 1) * 128]
            tiles.append(jnp.concatenate([tile] * (128 // NB), axis=0) * mask)
        flat = jnp.concatenate(tiles, axis=0).astype(BF16)
        to = to_ref[pl.ds(c0, NB), :].astype(jnp.int32)
        for h in range(2):
            lane = jnp.where(to >= 0, to // quota * (2 * quota) + lax.rem(to, quota) + h * quota, -1)
            lane = jnp.concatenate([lane] * (128 // NB), axis=0)
            place = [jnp.where(lane == iota((128, 128), 1) + i * 128, 1.0, 0.0) for i in range(2 * columns // 128)]
            place = jnp.concatenate(place, axis=1).astype(BF16)
            acc_ref[...] += jnp.dot(flat[h * rows // 2 : (h + 1) * rows // 2], place, preferred_element_type=F32)

    for d, ref in enumerate((r0_ref, r1_ref, r2_ref, r3_ref)):
        ref[...] = acc_ref[:, d * 2 * quota : (d + 1) * 2 * quota].astype(BF16)


def per_device(state, kappa, edge_nbrs, stencil, owner, w_first, w_inner, w_last):
    fields, levels, columns = state.shape
    rows = fields * levels
    ch = w_inner.shape[2]
    devices = lax.axis_size(AXES)
    device = lax.axis_index(AXES)
    total = columns // 16 * devices
    dev = device.astype(jnp.int32).reshape(1)
    table, holder = node_tables(columns)
    f32 = functools.partial(jax.ShapeDtypeStruct, dtype=F32)
    bf16 = functools.partial(jax.ShapeDtypeStruct, dtype=BF16)
    i32 = functools.partial(jax.ShapeDtypeStruct, dtype=jnp.int32)

    payload = pl.pallas_call(
        pack_kernel,
        out_shape=bf16((rows + 16, columns)),
        in_specs=[SMEM] + [VMEM] * 3,
        out_specs=VMEM,
        name="pack",
    )(dev, state, stencil.T, owner.reshape(1, columns))
    def trade(x, d):
        return lax.ppermute(x, AXES, [(i, i ^ d) for i in range(devices)])

    member1 = trade(payload, 1)
    member2 = trade(payload, 2)

    base, edges, facing, w1, wi, w24 = pl.pallas_call(
        functools.partial(edges_kernel, total),
        out_shape=(f32((rows, columns)), bf16((rows, columns // 2)), i32((1, columns)), bf16((3 * 128, ch)),
                   bf16(w_inner.shape), bf16((3 * fields, ch))),
        in_specs=[SMEM] + [VMEM] * 10,
        out_specs=(VMEM,) * 6,
        cost_estimate=pl.CostEstimate(flops=3 * 10**9, bytes_accessed=2**21, transcendentals=0),
        name="edges",
    )(dev, state, kappa.reshape(1, columns), jnp.asarray(diffusion_matrix(columns)),
      jnp.asarray(edge_matrix(columns)), edge_nbrs.T, jnp.asarray(table), jnp.asarray(holder),
      w_first, w_inner, w_last.T)

    member2, base = lax.optimization_barrier((member2, base))
    member3 = trade(member2, 1)
    low = lax.ppermute(edges, AXES, [(i, (i + 1) % devices) for i in range(devices)])
    high = lax.ppermute(edges, AXES, [(i, (i - 1) % devices) for i in range(devices)])

    bf = lambda *shape: pltpu.VMEM(shape, BF16)
    lanes = 2 * columns // GROUP
    *results, code = pl.pallas_call(
        functools.partial(net_kernel, levels, fields),
        out_shape=[bf16((rows // 2, lanes))] * GROUP + [i32((1, columns))],
        in_specs=[SMEM] + [VMEM] * (GROUP + 1) + [VMEM] * 2,
        out_specs=[VMEM] * (GROUP + 1),
        scratch_shapes=[
            bf(GROUP * columns, 9 * 128),
            bf(levels, 80, 128),
            bf(levels + 2, columns, 128),
            bf(levels + 2, NB, ch),
            bf(levels, NB, ch),
            bf(levels // 2 + 2, NB, ch),
            bf(levels // 2, NB, ch),
            bf(levels // 4 + 2, NB, ch),
            bf(levels // 2 + 2, NB, ch),
            bf(levels + 2, NB, ch),
            bf(levels, NB, ch),
            pltpu.VMEM((24, levels * NB + 256), F32),
            pltpu.VMEM((rows // 2, GROUP * lanes), F32),
            pltpu.VMEM((columns, 128), F32),
        ],
        compiler_params=pltpu.CompilerParams(vmem_limit_bytes=30 * 1024 * 1024),
        cost_estimate=pl.CostEstimate(flops=10**10, bytes_accessed=2**22, transcendentals=10**7),
        name="network",
    )(dev, payload, member1, member2, member3, w1, wi, w24)
    back = [trade(results[d], d) for d in (3, 2, 1)][::-1]

    middle = pl.pallas_call(
        middle_kernel,
        out_shape=f32((rows, columns)),
        in_specs=[VMEM] * 4,
        out_specs=VMEM,
        cost_estimate=pl.CostEstimate(flops=10**9, bytes_accessed=2**22, transcendentals=0),
        compiler_params=SMALL,
        name="middle",
    )(*lax.optimization_barrier((base, low, high, facing, results[0]))[:4])

    return pl.pallas_call(
        final_kernel,
        out_shape=f32((fields, levels, columns)),
        in_specs=[VMEM] * 6,
        out_specs=VMEM,
        compiler_params=SMALL,
        name="combine",
    )(middle.reshape(fields, levels, columns), code, results[0], *back)


def solution(mesh):
    in_specs = (
        P(None, None, AXES),
        P(AXES),
        P(AXES, None),
        P(AXES, None),
        P(AXES),
        P(),
        P(),
        P(),
    )
    return jax.shard_map(
        per_device, mesh=mesh, in_specs=in_specs, out_specs=P(None, None, AXES), check_vma=False
    )
```

```python
import functools
import math

import jax
import jax.numpy as jnp
import numpy as np
from jax import lax
from jax.experimental import pallas as pl
from jax.experimental.pallas import tpu as pltpu
from jax.sharding import PartitionSpec as P

AXES = ("grp", "elem")
EDGE_NODES = ((1, 2), (7, 11), (14, 13), (8, 4))
VMEM = pl.BlockSpec(memory_space=pltpu.VMEM)
SMALL = pltpu.CompilerParams(vmem_limit_bytes=12 * 1024 * 1024)
SMEM = pl.BlockSpec(memory_space=pltpu.SMEM)
HIGHEST = lax.Precision.HIGHEST
BF16 = jnp.bfloat16
F32 = jnp.float32
NB = 32
STEP = 12
GROUP = 4


def second_derivative():
    points = np.array([-1.0, -math.sqrt(0.2), math.sqrt(0.2), 1.0])
    factors = np.array(
        [1.0 / np.prod([points[j] - points[m] for m in range(4) if m != j]) for j in range(4)]
    )
    deriv = np.zeros((4, 4))
    for i in range(4):
        for j in range(4):
            if i != j:
                deriv[i, j] = factors[j] / factors[i] / (points[i] - points[j])
        deriv[i, i] = -np.sum(deriv[i])
    return deriv @ deriv


def diffusion_matrix(columns):
    lap = second_derivative()
    eye = np.eye(4)
    node = np.einsum("ia,jb->abij", lap, eye) + np.einsum("ia,jb->abij", eye, lap)
    return np.kron(np.eye(columns // 16), node.reshape(16, 16)).astype(np.float32)


def edge_matrix(columns):
    sel = np.zeros((columns, columns // 2), np.float32)
    for e in range(columns // 16):
        for k in range(4):
            for m in range(2):
                sel[16 * e + EDGE_NODES[k][m], 8 * e + 2 * k + m] = 1
    return sel


def node_tables(columns):
    on_edge = np.zeros((4, columns), np.float32)
    offset = np.zeros((1, columns), np.float32)
    for k in range(4):
        for m in range(2):
            on_edge[k, EDGE_NODES[k][m] :: 16] = 1
            offset[0, EDGE_NODES[k][m] :: 16] = (k + 2) % 4 * 2 + 1 - m
    holder = np.kron(np.eye(columns // 16), np.ones((1, 16))).astype(np.float32)
    table = np.concatenate([on_edge, offset, np.zeros((3, columns), np.float32)], axis=0)
    return table, holder


def iota(shape, dim):
    return lax.broadcasted_iota(jnp.int32, shape, dim)


def silu(half):
    half = half.astype(BF16)
    return half + half * jnp.tanh(half)


def pack_kernel(dev_ref, state_ref, sten_ref, owner_ref, pay_ref):
    fields, levels, columns = state_ref.shape
    rows = fields * levels
    for l in range(0, levels, 2):
        pair = jnp.concatenate([state_ref[:, l, :], state_ref[:, l + 1, :]], axis=0)
        pay_ref[l * fields : (l + 2) * fields, :] = pair.astype(BF16)
    local = (sten_ref[...] - dev_ref[0] * columns).astype(F32)
    flag = jnp.where(owner_ref[...] >= 0, 1.0, 0.0)
    tail = jnp.concatenate([local, flag, jnp.zeros((6, columns), F32)], axis=0)
    pay_ref[rows : rows + 16, :] = tail.astype(BF16)


def edges_kernel(total, dev_ref, state_ref, kappa_ref, op_ref, sel_ref, nbr_ref, table_ref, holder_ref,
                 base_ref, edge_ref, facing_ref):
    fields, levels, columns = state_ref.shape
    elements = columns // 16
    flat = state_ref[...].reshape(fields * levels, columns)
    dyn = kappa_ref[...] * jnp.dot(flat, op_ref[...], precision=HIGHEST)
    edge = jnp.dot(dyn, sel_ref[...], precision=HIGHEST)
    edge_ref[...] = edge.astype(BF16)
    rel = lax.rem(nbr_ref[...] - (dev_ref[0] - 1) * elements + total, total).astype(F32)
    spread = jnp.dot(rel, holder_ref[...], precision=HIGHEST)
    on_edge = table_ref[0:4, :]
    is_edge = jnp.sum(on_edge, axis=0, keepdims=True)
    facing = 8.0 * jnp.sum(spread * on_edge, axis=0, keepdims=True) + table_ref[4:5, :]
    facing = jnp.where(is_edge > 0, facing, -1.0).astype(jnp.int32)
    facing_ref[...] = facing
    half = columns // 2
    pick = jnp.where(iota((half, columns), 0) + half == facing, 0.5, 0.0)
    own = jnp.dot(edge, pick, precision=HIGHEST)
    base_ref[...] = flat + (1.0 - 0.5 * is_edge) * dyn + own


def land(code, d, quota, columns):
    slot = jnp.where((code >= d * quota) & (code < (d + 1) * quota), code - d * quota, -2 * quota)
    spot = iota((2 * quota, columns), 0)
    return [jnp.where(spot == slot + h * quota, 1.0, 0.0).astype(BF16) for h in range(2)]


def middle_kernel(base_ref, low_ref, high_ref, facing_ref, out_ref):
    rows, columns = base_ref.shape
    half = columns // 2
    facing = facing_ref[...]
    acc = base_ref[...]
    for part, ref in ((0, low_ref), (2, high_ref)):
        pick = jnp.where(iota((half, columns), 0) + part * half == facing, 0.5, 0.0).astype(BF16)
        acc = acc + jnp.dot(ref[...], pick, preferred_element_type=F32)
    out_ref[...] = acc


def final_kernel(base_ref, code_ref, r0_ref, r1_ref, r2_ref, r3_ref, out_ref):
    fields, levels, columns = out_ref.shape
    quota = columns // GROUP
    code = code_ref[...]
    got = jnp.concatenate([r0_ref[...], r1_ref[...], r2_ref[...], r3_ref[...]], axis=1)
    puts = [land(code, d, quota, columns) for d in range(GROUP)]
    for h in range(2):
        put = jnp.concatenate([p[h] for p in puts], axis=0)
        physics = jnp.dot(got, put, preferred_element_type=F32)
        for i in range(levels // 2):
            l = h * (levels // 2) + i
            out_ref[:, l, :] = base_ref[:, l, :] + physics[i * fields : (i + 1) * fields, :]


def halve(y):
    y = y.reshape(y.shape[0] // 2, 2, *y.shape[1:])
    return (y[:, 0] + y[:, 1]) * BF16(0.5)


def widen(coarse, fine):
    step, cols, ch = coarse.shape
    return jnp.broadcast_to(coarse[:, None], (step, 2, cols, ch)).reshape(2 * step, cols, ch) + fine


def net_kernel(levels, fields, dev_ref, m0_ref, m1_ref, m2_ref, m3_ref, w1_ref, wi_ref, wl_ref,
               r0_ref, r1_ref, r2_ref, r3_ref, code_ref,
               oh_ref, g_ref, net_ref, w1s_ref, w_ref, first_ref, second_ref, pool2_ref, third_ref,
               pool3_ref, join3_ref, join2_ref, top_ref, p_ref, acc_ref, to_ref):
    rows = fields * levels
    columns = m0_ref.shape[1]
    quota = columns // GROUP
    wide = GROUP * columns
    ch = wi_ref.shape[2]
    taps = 9 * fields
    half2, half3 = levels // 2, levels // 4

    for ref, n in ((first_ref, levels), (pool2_ref, half2), (pool3_ref, half3), (join3_ref, half2),
                   (join2_ref, levels)):
        zero = jnp.zeros(ref.shape[1:], BF16)
        ref[0] = zero
        ref[n + 1] = zero
    net_ref[0] = jnp.zeros(net_ref.shape[1:], BF16)
    net_ref[levels + 1] = jnp.zeros(net_ref.shape[1:], BF16)
    net_ref[:, :, 80:128] = jnp.zeros((levels + 2, columns, 48), BF16)
    p_ref[:, 0:128] = jnp.zeros((24, 128), F32)
    p_ref[:, levels * NB + 128 :] = jnp.zeros((24, 128), F32)
    acc_ref[...] = jnp.zeros(acc_ref.shape, F32)
    w1s_ref[...] = jnp.zeros(w1s_ref.shape, BF16)
    for t in range(3):
        w1s_ref[128 * t : 128 * t + taps, :] = w1_ref[taps * t : taps * (t + 1), :] * BF16(0.5)
    w_ref[...] = wi_ref[...] * BF16(0.5)
    w24 = jnp.concatenate([wl_ref[:, ch * t : ch * (t + 1)].astype(F32) for t in range(3)], axis=0).astype(BF16)

    me = lax.rem(dev_ref[0], GROUP)
    members = (m0_ref, m1_ref, m2_ref, m3_ref)
    upto = jnp.where(iota((columns, columns), 0) < iota((columns, columns), 1), 1.0, 0.0).astype(BF16)
    metas = [ref[rows : rows + 16, :] for ref in members]
    flags = [meta.astype(F32)[9:10, :] for meta in metas]
    counts = [jnp.sum(flag, axis=1, keepdims=True) for flag in flags]
    ranks, targets, active = [], [], jnp.zeros((1, 1), F32)
    for d in range(GROUP):
        start = jnp.zeros((1, 1), F32)
        for other in range(GROUP):
            start = start + jnp.where((me ^ other) < (me ^ d), counts[other], 0.0)
        local = jnp.dot(metas[d], upto, preferred_element_type=F32)[9:10, :].astype(jnp.int32)
        rank = local + start.astype(jnp.int32)
        ranks.append(jnp.where(flags[d] > 0, rank, -1))
        targets.append(jnp.where(flags[d] > 0, d * quota + local // GROUP + 1, 0).astype(F32))
        if d == 0:
            code_ref[...] = jnp.where(flags[d] > 0, (lax.rem(rank, GROUP) ^ me) * quota + local // GROUP, -1)
        active = active + counts[d]
    meta = jnp.concatenate(metas, axis=1)
    rank = jnp.concatenate(ranks, axis=1)
    share = (jnp.sum(active).astype(jnp.int32) - me + GROUP - 1) // GROUP
    slot = GROUP * iota((columns, wide), 0) + me
    choose = jnp.where(slot == rank, 1.0, 0.0).astype(BF16)
    flip = (((1,), (1,)), ((), ()))
    sten = lax.dot_general(meta, choose, flip, preferred_element_type=F32)
    part = (iota((16, wide), 1) // columns).astype(F32).astype(BF16)
    part = lax.dot_general(part, choose, flip, preferred_element_type=F32)
    sten = (sten + columns * part).astype(jnp.int32)
    target = jnp.broadcast_to(jnp.concatenate(targets, axis=1), (128, wide)).astype(BF16)
    to_ref[...] = lax.dot_general(choose, target, flip, preferred_element_type=F32) - 1.0

    @pl.loop(0, (share + 127) // 128)
    def _(q):
        lanes = pl.ds(pl.multiple_of(q * 128, 128), 128)
        for k in range(9):
            for half in range(columns // 128):
                here = sten[k : k + 1, half * 128 : (half + 1) * 128]
                picked = here if half == 0 else jnp.where(q == half, here, picked)
            oh_ref[:, k * 128 : (k + 1) * 128] = jnp.where(iota((wide, 128), 0) == picked, 1.0, 0.0).astype(BF16)
        for k in range(0, 9, 2):
            n = 2 if k < 8 else 1
            got = jnp.dot(jnp.concatenate([ref[0:rows, :] for ref in members], axis=1), oh_ref[:, k * 128 : (k + n) * 128], preferred_element_type=F32)
            parts = [got[:, u * 128 : (u + 1) * 128].reshape(levels, fields, 128) for u in range(n)]
            if n == 1:
                parts.append(jnp.zeros_like(parts[0]))
            g_ref[0:levels, k * 8 : k * 8 + 16, :] = jnp.concatenate(parts, axis=1).astype(BF16)

        for l in range(levels):
            net_ref[l + 1, lanes, 0:80] = g_ref[l].T

    mask = jnp.where(iota((128 // NB * 8, 128), 0) // 8 == iota((128 // NB * 8, 128), 1) // NB, 1.0, 0.0)

    @pl.loop(0, (share + NB - 1) // NB)
    def _(b):
        c0 = pl.multiple_of(b * NB, NB)

        pending = []

        def flush():
            for item in pending:
                item()
            pending.clear()

        def conv(load, weight, n, emit):
            step = max(s for s in range(1, STEP + 1) if n % s == 0)
            for l0 in range(0, n, step):
                x = [load(l0 + t, step).reshape(step * NB, -1) for t in range(3)]
                acc = jnp.dot(jnp.concatenate(x, axis=1), weight, preferred_element_type=F32)
                flush()
                pending.append(lambda emit=emit, l0=l0, step=step, acc=acc: emit(
                    l0, step, silu(acc).reshape(step, NB, ch)))

        def emit_first(l0, step, y):
            first_ref[l0 + 1 : l0 + 1 + step] = y

        def emit_second(l0, step, y):
            second_ref[l0 : l0 + step] = y
            pool2_ref[l0 // 2 + 1 : l0 // 2 + 1 + step // 2] = halve(y)

        def emit_third(l0, step, y):
            third_ref[l0 : l0 + step] = y
            pool3_ref[l0 // 2 + 1 : l0 // 2 + 1 + step // 2] = halve(y)

        def emit_deepest(l0, step, y):
            fine = third_ref[2 * l0 : 2 * (l0 + step)]
            join3_ref[2 * l0 + 1 : 2 * (l0 + step) + 1] = widen(y, fine)

        def emit_upper(l0, step, y):
            fine = second_ref[2 * l0 : 2 * (l0 + step)]
            join2_ref[2 * l0 + 1 : 2 * (l0 + step) + 1] = widen(y, fine)

        def emit_top(l0, step, y):
            top_ref[l0 : l0 + step] = y

        conv(lambda l, n: net_ref[l : l + n, pl.ds(c0, NB), :], w1s_ref[...], levels, emit_first)
        conv(lambda l, n: first_ref[l : l + n], w_ref[0], levels, emit_second)
        conv(lambda l, n: pool2_ref[l : l + n], w_ref[1], half2, emit_third)
        conv(lambda l, n: pool3_ref[l : l + n], w_ref[2], half3, emit_deepest)
        conv(lambda l, n: join3_ref[l : l + n], w_ref[3], half2, emit_upper)
        conv(lambda l, n: join2_ref[l : l + n], w_ref[4], levels, emit_top)

        flush()
        group = 384
        for i in range(0, levels * NB, group):
            x = top_ref[i // NB : (i + group) // NB].reshape(group, ch)
            p_ref[:, i + 128 : i + group + 128] = lax.dot_general(w24, x, flip, preferred_element_type=F32)
        n = levels * NB
        out = p_ref[0:8, 128 - NB : n + 128 - NB] + p_ref[8:16, 128 : n + 128] + p_ref[16:24, 128 + NB : n + 128 + NB]
        tiles = []
        for i in range(n // 128):
            tile = out[:, i * 128 : (i + 1) * 128]
            tiles.append(jnp.concatenate([tile] * (128 // NB), axis=0) * mask)
        flat = jnp.concatenate(tiles, axis=0).astype(BF16)
        to = to_ref[pl.ds(c0, NB), :].astype(jnp.int32)
        for h in range(2):
            lane = jnp.where(to >= 0, to // quota * (2 * quota) + lax.rem(to, quota) + h * quota, -1)
            lane = jnp.concatenate([lane] * (128 // NB), axis=0)
            place = [jnp.where(lane == iota((128, 128), 1) + i * 128, 1.0, 0.0) for i in range(2 * columns // 128)]
            place = jnp.concatenate(place, axis=1).astype(BF16)
            acc_ref[...] += jnp.dot(flat[h * rows // 2 : (h + 1) * rows // 2], place, preferred_element_type=F32)

    for d, ref in enumerate((r0_ref, r1_ref, r2_ref, r3_ref)):
        ref[...] = acc_ref[:, d * 2 * quota : (d + 1) * 2 * quota].astype(BF16)


def per_device(state, kappa, edge_nbrs, stencil, owner, w_first, w_inner, w_last):
    fields, levels, columns = state.shape
    rows = fields * levels
    ch = w_inner.shape[2]
    devices = lax.axis_size(AXES)
    device = lax.axis_index(AXES)
    total = columns // 16 * devices
    dev = device.astype(jnp.int32).reshape(1)
    table, holder = node_tables(columns)
    f32 = functools.partial(jax.ShapeDtypeStruct, dtype=F32)
    bf16 = functools.partial(jax.ShapeDtypeStruct, dtype=BF16)
    i32 = functools.partial(jax.ShapeDtypeStruct, dtype=jnp.int32)

    payload = pl.pallas_call(
        pack_kernel,
        out_shape=bf16((rows + 16, columns)),
        in_specs=[SMEM] + [VMEM] * 3,
        out_specs=VMEM,
        name="pack",
    )(dev, state, stencil.T, owner.reshape(1, columns))
    def trade(x, d):
        return lax.ppermute(x, AXES, [(i, i ^ d) for i in range(devices)])

    member1 = trade(payload, 1)
    member2 = trade(payload, 2)

    base, edges, facing = pl.pallas_call(
        functools.partial(edges_kernel, total),
        out_shape=(f32((rows, columns)), bf16((rows, columns // 2)), i32((1, columns))),
        in_specs=[SMEM] + [VMEM] * 7,
        out_specs=(VMEM, VMEM, VMEM),
        cost_estimate=pl.CostEstimate(flops=3 * 10**9, bytes_accessed=2**21, transcendentals=0),
        name="edges",
    )(dev, state, kappa.reshape(1, columns), jnp.asarray(diffusion_matrix(columns)),
      jnp.asarray(edge_matrix(columns)), edge_nbrs.T, jnp.asarray(table), jnp.asarray(holder))

    member2, base = lax.optimization_barrier((member2, base))
    member3 = trade(member2, 1)
    low = lax.ppermute(edges, AXES, [(i, (i + 1) % devices) for i in range(devices)])
    high = lax.ppermute(edges, AXES, [(i, (i - 1) % devices) for i in range(devices)])

    bf = lambda *shape: pltpu.VMEM(shape, BF16)
    lanes = 2 * columns // GROUP
    *results, code = pl.pallas_call(
        functools.partial(net_kernel, levels, fields),
        out_shape=[bf16((rows // 2, lanes))] * GROUP + [i32((1, columns))],
        in_specs=[SMEM] + [VMEM] * (GROUP + 1) + [VMEM] * 2,
        out_specs=[VMEM] * (GROUP + 1),
        scratch_shapes=[
            bf(GROUP * columns, 9 * 128),
            bf(levels, 80, 128),
            bf(levels + 2, columns, 128),
            bf(3 * 128, ch),
            bf(*w_inner.shape),
            bf(levels + 2, NB, ch),
            bf(levels, NB, ch),
            bf(levels // 2 + 2, NB, ch),
            bf(levels // 2, NB, ch),
            bf(levels // 4 + 2, NB, ch),
            bf(levels // 2 + 2, NB, ch),
            bf(levels + 2, NB, ch),
            bf(levels, NB, ch),
            pltpu.VMEM((24, levels * NB + 256), F32),
            pltpu.VMEM((rows // 2, GROUP * lanes), F32),
            pltpu.VMEM((columns, 128), F32),
        ],
        compiler_params=pltpu.CompilerParams(vmem_limit_bytes=30 * 1024 * 1024),
        cost_estimate=pl.CostEstimate(flops=10**10, bytes_accessed=2**22, transcendentals=10**7),
        name="network",
    )(dev, payload, member1, member2, member3, w_first, w_inner, w_last.T)
    back = [trade(results[d], d) for d in (3, 2, 1)][::-1]

    middle = pl.pallas_call(
        middle_kernel,
        out_shape=f32((rows, columns)),
        in_specs=[VMEM] * 4,
        out_specs=VMEM,
        cost_estimate=pl.CostEstimate(flops=10**9, bytes_accessed=2**22, transcendentals=0),
        compiler_params=SMALL,
        name="middle",
    )(*lax.optimization_barrier((base, low, high, facing, results[0]))[:4])

    return pl.pallas_call(
        final_kernel,
        out_shape=f32((fields, levels, columns)),
        in_specs=[VMEM] * 6,
        out_specs=VMEM,
        compiler_params=SMALL,
        name="combine",
    )(middle.reshape(fields, levels, columns), code, results[0], *back)


def solution(mesh):
    in_specs = (
        P(None, None, AXES),
        P(AXES),
        P(AXES, None),
        P(AXES, None),
        P(AXES),
        P(),
        P(),
        P(),
    )
    return jax.shard_map(
        per_device, mesh=mesh, in_specs=in_specs, out_specs=P(None, None, AXES), check_vma=False
    )
```

```python
import functools
import math

import jax
import jax.numpy as jnp
import numpy as np
from jax import lax
from jax.experimental import pallas as pl
from jax.experimental.pallas import tpu as pltpu
from jax.sharding import PartitionSpec as P

AXES = ("grp", "elem")
EDGE_NODES = ((1, 2), (7, 11), (14, 13), (8, 4))
VMEM = pl.BlockSpec(memory_space=pltpu.VMEM)
SMALL = pltpu.CompilerParams(vmem_limit_bytes=12 * 1024 * 1024)
SMEM = pl.BlockSpec(memory_space=pltpu.SMEM)
HIGHEST = lax.Precision.HIGHEST
BF16 = jnp.bfloat16
F32 = jnp.float32
NB = 32
STEP = 18
GROUP = 4


def second_derivative():
    points = np.array([-1.0, -math.sqrt(0.2), math.sqrt(0.2), 1.0])
    factors = np.array(
        [1.0 / np.prod([points[j] - points[m] for m in range(4) if m != j]) for j in range(4)]
    )
    deriv = np.zeros((4, 4))
    for i in range(4):
        for j in range(4):
            if i != j:
                deriv[i, j] = factors[j] / factors[i] / (points[i] - points[j])
        deriv[i, i] = -np.sum(deriv[i])
    return deriv @ deriv


def diffusion_matrix(columns):
    lap = second_derivative()
    eye = np.eye(4)
    node = np.einsum("ia,jb->abij", lap, eye) + np.einsum("ia,jb->abij", eye, lap)
    return np.kron(np.eye(columns // 16), node.reshape(16, 16)).astype(np.float32)


def edge_matrix(columns):
    sel = np.zeros((columns, columns // 2), np.float32)
    for e in range(columns // 16):
        for k in range(4):
            for m in range(2):
                sel[16 * e + EDGE_NODES[k][m], 8 * e + 2 * k + m] = 1
    return sel


def node_tables(columns):
    on_edge = np.zeros((4, columns), np.float32)
    offset = np.zeros((1, columns), np.float32)
    for k in range(4):
        for m in range(2):
            on_edge[k, EDGE_NODES[k][m] :: 16] = 1
            offset[0, EDGE_NODES[k][m] :: 16] = (k + 2) % 4 * 2 + 1 - m
    holder = np.kron(np.eye(columns // 16), np.ones((1, 16))).astype(np.float32)
    table = np.concatenate([on_edge, offset, np.zeros((3, columns), np.float32)], axis=0)
    return table, holder


def iota(shape, dim):
    return lax.broadcasted_iota(jnp.int32, shape, dim)


def silu(half):
    half = half.astype(BF16)
    return half + half * jnp.tanh(half)


def pack_kernel(dev_ref, state_ref, sten_ref, owner_ref, pay_ref):
    fields, levels, columns = state_ref.shape
    rows = fields * levels
    for l in range(0, levels, 2):
        pair = jnp.concatenate([state_ref[:, l, :], state_ref[:, l + 1, :]], axis=0)
        pay_ref[l * fields : (l + 2) * fields, :] = pair.astype(BF16)
    local = (sten_ref[...] - dev_ref[0] * columns).astype(F32)
    flag = jnp.where(owner_ref[...] >= 0, 1.0, 0.0)
    tail = jnp.concatenate([local, flag, jnp.zeros((6, columns), F32)], axis=0)
    pay_ref[rows : rows + 16, :] = tail.astype(BF16)


def edges_kernel(total, dev_ref, state_ref, kappa_ref, op_ref, sel_ref, nbr_ref, table_ref, holder_ref,
                 base_ref, edge_ref, facing_ref):
    fields, levels, columns = state_ref.shape
    elements = columns // 16
    flat = state_ref[...].reshape(fields * levels, columns)
    dyn = kappa_ref[...] * jnp.dot(flat, op_ref[...], precision=HIGHEST)
    edge = jnp.dot(dyn, sel_ref[...], precision=HIGHEST)
    edge_ref[...] = edge.astype(BF16)
    rel = lax.rem(nbr_ref[...] - (dev_ref[0] - 1) * elements + total, total).astype(F32)
    spread = jnp.dot(rel, holder_ref[...], precision=HIGHEST)
    on_edge = table_ref[0:4, :]
    is_edge = jnp.sum(on_edge, axis=0, keepdims=True)
    facing = 8.0 * jnp.sum(spread * on_edge, axis=0, keepdims=True) + table_ref[4:5, :]
    facing = jnp.where(is_edge > 0, facing, -1.0).astype(jnp.int32)
    facing_ref[...] = facing
    half = columns // 2
    pick = jnp.where(iota((half, columns), 0) + half == facing, 0.5, 0.0)
    own = jnp.dot(edge, pick, precision=HIGHEST)
    base_ref[...] = flat + (1.0 - 0.5 * is_edge) * dyn + own


def land(code, d, quota, columns):
    slot = jnp.where((code >= d * quota) & (code < (d + 1) * quota), code - d * quota, -2 * quota)
    spot = iota((2 * quota, columns), 0)
    return [jnp.where(spot == slot + h * quota, 1.0, 0.0).astype(BF16) for h in range(2)]


def middle_kernel(base_ref, low_ref, high_ref, facing_ref, out_ref):
    rows, columns = base_ref.shape
    half = columns // 2
    facing = facing_ref[...]
    acc = base_ref[...]
    for part, ref in ((0, low_ref), (2, high_ref)):
        pick = jnp.where(iota((half, columns), 0) + part * half == facing, 0.5, 0.0).astype(BF16)
        acc = acc + jnp.dot(ref[...], pick, preferred_element_type=F32)
    out_ref[...] = acc


def final_kernel(base_ref, code_ref, r0_ref, r1_ref, r2_ref, r3_ref, out_ref):
    fields, levels, columns = out_ref.shape
    quota = columns // GROUP
    code = code_ref[...]
    got = jnp.concatenate([r0_ref[...], r1_ref[...], r2_ref[...], r3_ref[...]], axis=1)
    puts = [land(code, d, quota, columns) for d in range(GROUP)]
    for h in range(2):
        put = jnp.concatenate([p[h] for p in puts], axis=0)
        physics = jnp.dot(got, put, preferred_element_type=F32)
        for i in range(levels // 2):
            l = h * (levels // 2) + i
            out_ref[:, l, :] = base_ref[:, l, :] + physics[i * fields : (i + 1) * fields, :]


def halve(y):
    y = y.reshape(y.shape[0] // 2, 2, *y.shape[1:])
    return (y[:, 0] + y[:, 1]) * BF16(0.5)


def widen(coarse, fine):
    step, cols, ch = coarse.shape
    return jnp.broadcast_to(coarse[:, None], (step, 2, cols, ch)).reshape(2 * step, cols, ch) + fine


def net_kernel(levels, fields, dev_ref, m0_ref, m1_ref, m2_ref, m3_ref, w1_ref, wi_ref, wl_ref,
               r0_ref, r1_ref, r2_ref, r3_ref, code_ref,
               oh_ref, g_ref, net_ref, w1s_ref, w_ref, first_ref, second_ref, pool2_ref, third_ref,
               pool3_ref, join3_ref, join2_ref, top_ref, p_ref, acc_ref, to_ref):
    rows = fields * levels
    columns = m0_ref.shape[1]
    quota = columns // GROUP
    wide = GROUP * columns
    ch = wi_ref.shape[2]
    taps = 9 * fields
    half2, half3 = levels // 2, levels // 4

    for ref, n in ((first_ref, levels), (pool2_ref, half2), (pool3_ref, half3), (join3_ref, half2),
                   (join2_ref, levels)):
        zero = jnp.zeros(ref.shape[1:], BF16)
        ref[0] = zero
        ref[n + 1] = zero
    net_ref[0] = jnp.zeros(net_ref.shape[1:], BF16)
    net_ref[levels + 1] = jnp.zeros(net_ref.shape[1:], BF16)
    net_ref[:, :, 80:128] = jnp.zeros((levels + 2, columns, 48), BF16)
    p_ref[:, 0:128] = jnp.zeros((24, 128), F32)
    p_ref[:, levels * NB + 128 :] = jnp.zeros((24, 128), F32)
    acc_ref[...] = jnp.zeros(acc_ref.shape, BF16)
    w1s_ref[...] = jnp.zeros(w1s_ref.shape, BF16)
    for t in range(3):
        w1s_ref[128 * t : 128 * t + taps, :] = w1_ref[taps * t : taps * (t + 1), :] * BF16(0.5)
    w_ref[...] = wi_ref[...] * BF16(0.5)
    w24 = jnp.concatenate([wl_ref[:, ch * t : ch * (t + 1)].astype(F32) for t in range(3)], axis=0).astype(BF16)

    me = lax.rem(dev_ref[0], GROUP)
    members = (m0_ref, m1_ref, m2_ref, m3_ref)
    upto = jnp.where(iota((columns, columns), 0) < iota((columns, columns), 1), 1.0, 0.0).astype(BF16)
    metas = [ref[rows : rows + 16, :] for ref in members]
    flags = [meta.astype(F32)[9:10, :] for meta in metas]
    counts = [jnp.sum(flag, axis=1, keepdims=True) for flag in flags]
    ranks, targets, active = [], [], jnp.zeros((1, 1), F32)
    for d in range(GROUP):
        start = jnp.zeros((1, 1), F32)
        for other in range(GROUP):
            start = start + jnp.where((me ^ other) < (me ^ d), counts[other], 0.0)
        local = jnp.dot(metas[d], upto, preferred_element_type=F32)[9:10, :].astype(jnp.int32)
        rank = local + start.astype(jnp.int32)
        ranks.append(jnp.where(flags[d] > 0, rank, -1))
        targets.append(jnp.where(flags[d] > 0, d * quota + local // GROUP + 1, 0).astype(F32))
        if d == 0:
            code_ref[...] = jnp.where(flags[d] > 0, (lax.rem(rank, GROUP) ^ me) * quota + local // GROUP, -1)
        active = active + counts[d]
    meta = jnp.concatenate(metas, axis=1)
    rank = jnp.concatenate(ranks, axis=1)
    share = (jnp.sum(active).astype(jnp.int32) - me + GROUP - 1) // GROUP
    slot = GROUP * iota((columns, wide), 0) + me
    choose = jnp.where(slot == rank, 1.0, 0.0).astype(BF16)
    flip = (((1,), (1,)), ((), ()))
    sten = lax.dot_general(meta, choose, flip, preferred_element_type=F32)
    part = (iota((16, wide), 1) // columns).astype(F32).astype(BF16)
    part = lax.dot_general(part, choose, flip, preferred_element_type=F32)
    sten = (sten + columns * part).astype(jnp.int32)
    target = jnp.broadcast_to(jnp.concatenate(targets, axis=1), (128, wide)).astype(BF16)
    to = lax.dot_general(choose, target, flip, preferred_element_type=F32).astype(jnp.int32) - 1
    to_ref[...] = jnp.where(to >= 0, to // quota * (2 * quota) + lax.rem(to, quota), -1)

    @pl.loop(0, (share + 127) // 128)
    def _(q):
        lanes = pl.ds(pl.multiple_of(q * 128, 128), 128)
        for k in range(9):
            for half in range(columns // 128):
                here = sten[k : k + 1, half * 128 : (half + 1) * 128]
                picked = here if half == 0 else jnp.where(q == half, here, picked)
            oh_ref[:, k * 128 : (k + 1) * 128] = jnp.where(iota((wide, 128), 0) == picked, 1.0, 0.0).astype(BF16)
        for k in range(0, 9, 2):
            n = 2 if k < 8 else 1
            got = jnp.dot(jnp.concatenate([ref[0:rows, :] for ref in members], axis=1), oh_ref[:, k * 128 : (k + n) * 128], preferred_element_type=F32)
            parts = [got[:, u * 128 : (u + 1) * 128].reshape(levels, fields, 128) for u in range(n)]
            if n == 1:
                parts.append(jnp.zeros_like(parts[0]))
            g_ref[0:levels, k * 8 : k * 8 + 16, :] = jnp.concatenate(parts, axis=1).astype(BF16)

        for l in range(levels):
            net_ref[l + 1, lanes, 0:80] = g_ref[l].T

    mask = jnp.where(iota((128 // NB * 8, 128), 0) // 8 == iota((128 // NB * 8, 128), 1) // NB, 1.0, 0.0)

    @pl.loop(0, (share + NB - 1) // NB)
    def _(b):
        c0 = pl.multiple_of(b * NB, NB)

        def conv(load, weight, n, emit):
            step = max(s for s in range(1, STEP + 1) if n % s == 0)
            for l0 in range(0, n, step):
                x = [load(l0 + t, step).reshape(step * NB, -1) for t in range(3)]
                acc = jnp.dot(jnp.concatenate(x, axis=1), weight, preferred_element_type=F32)
                emit(l0, step, silu(acc).reshape(step, NB, ch))

        def emit_first(l0, step, y):
            first_ref[l0 + 1 : l0 + 1 + step] = y

        def emit_second(l0, step, y):
            second_ref[l0 : l0 + step] = y
            pool2_ref[l0 // 2 + 1 : l0 // 2 + 1 + step // 2] = halve(y)

        def emit_third(l0, step, y):
            third_ref[l0 : l0 + step] = y
            pool3_ref[l0 // 2 + 1 : l0 // 2 + 1 + step // 2] = halve(y)

        def emit_deepest(l0, step, y):
            fine = third_ref[2 * l0 : 2 * (l0 + step)]
            join3_ref[2 * l0 + 1 : 2 * (l0 + step) + 1] = widen(y, fine)

        def emit_upper(l0, step, y):
            fine = second_ref[2 * l0 : 2 * (l0 + step)]
            join2_ref[2 * l0 + 1 : 2 * (l0 + step) + 1] = widen(y, fine)

        def emit_top(l0, step, y):
            top_ref[l0 : l0 + step] = y

        conv(lambda l, n: net_ref[l : l + n, pl.ds(c0, NB), :], w1s_ref[...], levels, emit_first)
        conv(lambda l, n: first_ref[l : l + n], w_ref[0], levels, emit_second)
        conv(lambda l, n: pool2_ref[l : l + n], w_ref[1], half2, emit_third)
        conv(lambda l, n: pool3_ref[l : l + n], w_ref[2], half3, emit_deepest)
        conv(lambda l, n: join3_ref[l : l + n], w_ref[3], half2, emit_upper)
        conv(lambda l, n: join2_ref[l : l + n], w_ref[4], levels, emit_top)

        group = 384
        for i in range(0, levels * NB, group):
            x = top_ref[i // NB : (i + group) // NB].reshape(group, ch)
            p_ref[:, i + 128 : i + group + 128] = lax.dot_general(w24, x, flip, preferred_element_type=F32)
        n = levels * NB
        out = p_ref[0:8, 128 - NB : n + 128 - NB] + p_ref[8:16, 128 : n + 128] + p_ref[16:24, 128 + NB : n + 128 + NB]
        tiles = []
        for i in range(n // 128):
            tile = out[:, i * 128 : (i + 1) * 128]
            tiles.append(jnp.concatenate([tile] * (128 // NB), axis=0) * mask)
        flat = jnp.concatenate(tiles, axis=0).astype(BF16)
        to = to_ref[pl.ds(c0, NB), :]
        place = []
        for h in range(2):
            lane = jnp.concatenate([to + jnp.where(to >= 0, h * quota, 0)] * (128 // NB), axis=0)
            hits = [jnp.where(lane == iota((128, 128), 1) + i * 128, 1.0, 0.0) for i in range(2 * columns // 128)]
            place.append(jnp.concatenate(hits, axis=1).astype(BF16))
        both = jnp.concatenate([flat[: rows // 2], flat[rows // 2 :]], axis=1)
        acc_ref[...] += jnp.dot(both, jnp.concatenate(place, axis=0), preferred_element_type=F32).astype(BF16)

    for d, ref in enumerate((r0_ref, r1_ref, r2_ref, r3_ref)):
        ref[...] = acc_ref[:, d * 2 * quota : (d + 1) * 2 * quota]


def per_device(state, kappa, edge_nbrs, stencil, owner, w_first, w_inner, w_last):
    fields, levels, columns = state.shape
    rows = fields * levels
    ch = w_inner.shape[2]
    devices = lax.axis_size(AXES)
    device = lax.axis_index(AXES)
    total = columns // 16 * devices
    dev = device.astype(jnp.int32).reshape(1)
    table, holder = node_tables(columns)
    f32 = functools.partial(jax.ShapeDtypeStruct, dtype=F32)
    bf16 = functools.partial(jax.ShapeDtypeStruct, dtype=BF16)
    i32 = functools.partial(jax.ShapeDtypeStruct, dtype=jnp.int32)

    payload = pl.pallas_call(
        pack_kernel,
        out_shape=bf16((rows + 16, columns)),
        in_specs=[SMEM] + [VMEM] * 3,
        out_specs=VMEM,
        name="pack",
    )(dev, state, stencil.T, owner.reshape(1, columns))
    def trade(x, d):
        return lax.ppermute(x, AXES, [(i, i ^ d) for i in range(devices)])

    member1 = trade(payload, 1)
    member2 = trade(payload, 2)

    base, edges, facing = pl.pallas_call(
        functools.partial(edges_kernel, total),
        out_shape=(f32((rows, columns)), bf16((rows, columns // 2)), i32((1, columns))),
        in_specs=[SMEM] + [VMEM] * 7,
        out_specs=(VMEM, VMEM, VMEM),
        cost_estimate=pl.CostEstimate(flops=3 * 10**9, bytes_accessed=2**21, transcendentals=0),
        name="edges",
    )(dev, state, kappa.reshape(1, columns), jnp.asarray(diffusion_matrix(columns)),
      jnp.asarray(edge_matrix(columns)), edge_nbrs.T, jnp.asarray(table), jnp.asarray(holder))

    member2, base = lax.optimization_barrier((member2, base))
    member3 = trade(member2, 1)
    low = lax.ppermute(edges, AXES, [(i, (i + 1) % devices) for i in range(devices)])
    high = lax.ppermute(edges, AXES, [(i, (i - 1) % devices) for i in range(devices)])

    bf = lambda *shape: pltpu.VMEM(shape, BF16)
    lanes = 2 * columns // GROUP
    *results, code = pl.pallas_call(
        functools.partial(net_kernel, levels, fields),
        out_shape=[bf16((rows // 2, lanes))] * GROUP + [i32((1, columns))],
        in_specs=[SMEM] + [VMEM] * (GROUP + 1) + [VMEM] * 2,
        out_specs=[VMEM] * (GROUP + 1),
        scratch_shapes=[
            bf(GROUP * columns, 9 * 128),
            bf(levels, 80, 128),
            bf(levels + 2, columns, 128),
            bf(3 * 128, ch),
            bf(*w_inner.shape),
            bf(levels + 2, NB, ch),
            bf(levels, NB, ch),
            bf(levels // 2 + 2, NB, ch),
            bf(levels // 2, NB, ch),
            bf(levels // 4 + 2, NB, ch),
            bf(levels // 2 + 2, NB, ch),
            bf(levels + 2, NB, ch),
            bf(levels, NB, ch),
            pltpu.VMEM((24, levels * NB + 256), F32),
            bf(rows // 2, GROUP * lanes),
            pltpu.VMEM((columns, 128), jnp.int32),
        ],
        compiler_params=pltpu.CompilerParams(vmem_limit_bytes=30 * 1024 * 1024),
        cost_estimate=pl.CostEstimate(flops=10**10, bytes_accessed=2**22, transcendentals=10**7),
        name="network",
    )(dev, payload, member1, member2, member3, w_first, w_inner, w_last.T)
    back = [trade(results[d], d) for d in (3, 2, 1)][::-1]

    middle = pl.pallas_call(
        middle_kernel,
        out_shape=f32((rows, columns)),
        in_specs=[VMEM] * 4,
        out_specs=VMEM,
        cost_estimate=pl.CostEstimate(flops=10**9, bytes_accessed=2**22, transcendentals=0),
        compiler_params=SMALL,
        name="middle",
    )(*lax.optimization_barrier((base, low, high, facing, results[0]))[:4])

    return pl.pallas_call(
        final_kernel,
        out_shape=f32((fields, levels, columns)),
        in_specs=[VMEM] * 6,
        out_specs=VMEM,
        compiler_params=SMALL,
        name="combine",
    )(middle.reshape(fields, levels, columns), code, results[0], *back)


def solution(mesh):
    in_specs = (
        P(None, None, AXES),
        P(AXES),
        P(AXES, None),
        P(AXES, None),
        P(AXES),
        P(),
        P(),
        P(),
    )
    return jax.shard_map(
        per_device, mesh=mesh, in_specs=in_specs, out_specs=P(None, None, AXES), check_vma=False
    )
```

```python
import functools
import math

import jax
import jax.numpy as jnp
import numpy as np
from jax import lax
from jax.experimental import pallas as pl
from jax.experimental.pallas import tpu as pltpu
from jax.sharding import PartitionSpec as P

AXES = ("grp", "elem")
EDGE_NODES = ((1, 2), (7, 11), (14, 13), (8, 4))
VMEM = pl.BlockSpec(memory_space=pltpu.VMEM)
SMALL = pltpu.CompilerParams(vmem_limit_bytes=12 * 1024 * 1024)
SMEM = pl.BlockSpec(memory_space=pltpu.SMEM)
HIGHEST = lax.Precision.HIGHEST
BF16 = jnp.bfloat16
F32 = jnp.float32
NB = 32
STEP = 6
GROUP = 4


def second_derivative():
    points = np.array([-1.0, -math.sqrt(0.2), math.sqrt(0.2), 1.0])
    factors = np.array(
        [1.0 / np.prod([points[j] - points[m] for m in range(4) if m != j]) for j in range(4)]
    )
    deriv = np.zeros((4, 4))
    for i in range(4):
        for j in range(4):
            if i != j:
                deriv[i, j] = factors[j] / factors[i] / (points[i] - points[j])
        deriv[i, i] = -np.sum(deriv[i])
    return deriv @ deriv


def diffusion_matrix(columns):
    lap = second_derivative()
    eye = np.eye(4)
    node = np.einsum("ia,jb->abij", lap, eye) + np.einsum("ia,jb->abij", eye, lap)
    return np.kron(np.eye(columns // 16), node.reshape(16, 16)).astype(np.float32)


def edge_matrix(columns):
    sel = np.zeros((columns, columns // 2), np.float32)
    for e in range(columns // 16):
        for k in range(4):
            for m in range(2):
                sel[16 * e + EDGE_NODES[k][m], 8 * e + 2 * k + m] = 1
    return sel


def node_tables(columns):
    on_edge = np.zeros((4, columns), np.float32)
    offset = np.zeros((1, columns), np.float32)
    for k in range(4):
        for m in range(2):
            on_edge[k, EDGE_NODES[k][m] :: 16] = 1
            offset[0, EDGE_NODES[k][m] :: 16] = (k + 2) % 4 * 2 + 1 - m
    holder = np.kron(np.eye(columns // 16), np.ones((1, 16))).astype(np.float32)
    table = np.concatenate([on_edge, offset, np.zeros((3, columns), np.float32)], axis=0)
    return table, holder


def iota(shape, dim):
    return lax.broadcasted_iota(jnp.int32, shape, dim)


def silu(half):
    half = half.astype(BF16)
    return half + half * jnp.tanh(half)


def pack_kernel(dev_ref, state_ref, sten_ref, owner_ref, pay_ref):
    fields, levels, columns = state_ref.shape
    rows = fields * levels
    for l in range(0, levels, 2):
        pair = jnp.concatenate([state_ref[:, l, :], state_ref[:, l + 1, :]], axis=0)
        pay_ref[l * fields : (l + 2) * fields, :] = pair.astype(BF16)
    local = (sten_ref[...] - dev_ref[0] * columns).astype(F32)
    flag = jnp.where(owner_ref[...] >= 0, 1.0, 0.0)
    tail = jnp.concatenate([local, flag, jnp.zeros((6, columns), F32)], axis=0)
    pay_ref[rows : rows + 16, :] = tail.astype(BF16)


def edges_kernel(total, dev_ref, state_ref, kappa_ref, op_ref, sel_ref, nbr_ref, table_ref, holder_ref,
                 base_ref, edge_ref, facing_ref):
    fields, levels, columns = state_ref.shape
    elements = columns // 16
    flat = state_ref[...].reshape(fields * levels, columns)
    dyn = kappa_ref[...] * jnp.dot(flat, op_ref[...], precision=HIGHEST)
    edge = jnp.dot(dyn, sel_ref[...], precision=HIGHEST)
    edge_ref[...] = edge.astype(BF16)
    rel = lax.rem(nbr_ref[...] - (dev_ref[0] - 1) * elements + total, total).astype(F32)
    spread = jnp.dot(rel, holder_ref[...], precision=HIGHEST)
    on_edge = table_ref[0:4, :]
    is_edge = jnp.sum(on_edge, axis=0, keepdims=True)
    facing = 8.0 * jnp.sum(spread * on_edge, axis=0, keepdims=True) + table_ref[4:5, :]
    facing = jnp.where(is_edge > 0, facing, -1.0).astype(jnp.int32)
    facing_ref[...] = facing
    half = columns // 2
    pick = jnp.where(iota((half, columns), 0) + half == facing, 0.5, 0.0)
    own = jnp.dot(edge, pick, precision=HIGHEST)
    base_ref[...] = flat + (1.0 - 0.5 * is_edge) * dyn + own


def land(code, d, quota, columns):
    slot = jnp.where((code >= d * quota) & (code < (d + 1) * quota), code - d * quota, -2 * quota)
    spot = iota((2 * quota, columns), 0)
    return [jnp.where(spot == slot + h * quota, 1.0, 0.0).astype(BF16) for h in range(2)]


def middle_kernel(base_ref, low_ref, high_ref, facing_ref, out_ref):
    rows, columns = base_ref.shape
    half = columns // 2
    facing = facing_ref[...]
    acc = base_ref[...]
    for part, ref in ((0, low_ref), (2, high_ref)):
        pick = jnp.where(iota((half, columns), 0) + part * half == facing, 0.5, 0.0).astype(BF16)
        acc = acc + jnp.dot(ref[...], pick, preferred_element_type=F32)
    out_ref[...] = acc


def final_kernel(base_ref, code_ref, r0_ref, r1_ref, r2_ref, r3_ref, out_ref):
    fields, levels, columns = out_ref.shape
    quota = columns // GROUP
    code = code_ref[...]
    got = jnp.concatenate([r0_ref[...], r1_ref[...], r2_ref[...], r3_ref[...]], axis=1)
    puts = [land(code, d, quota, columns) for d in range(GROUP)]
    for h in range(2):
        put = jnp.concatenate([p[h] for p in puts], axis=0)
        physics = jnp.dot(got, put, preferred_element_type=F32)
        for i in range(levels // 2):
            l = h * (levels // 2) + i
            out_ref[:, l, :] = base_ref[:, l, :] + physics[i * fields : (i + 1) * fields, :]


def halve(y):
    y = y.reshape(y.shape[0] // 2, 2, *y.shape[1:])
    return (y[:, 0] + y[:, 1]) * BF16(0.5)


def widen(coarse, fine):
    step, cols, ch = coarse.shape
    return jnp.broadcast_to(coarse[:, None], (step, 2, cols, ch)).reshape(2 * step, cols, ch) + fine


def net_kernel(levels, fields, dev_ref, m0_ref, m1_ref, m2_ref, m3_ref, w1_ref, wi_ref, wl_ref,
               r0_ref, r1_ref, r2_ref, r3_ref, code_ref,
               oh_ref, g_ref, net_ref, w1s_ref, w_ref, first_ref, second_ref, pool2_ref, third_ref,
               pool3_ref, join3_ref, join2_ref, top_ref, p_ref, acc_ref, to_ref):
    rows = fields * levels
    columns = m0_ref.shape[1]
    quota = columns // GROUP
    wide = GROUP * columns
    ch = wi_ref.shape[2]
    taps = 9 * fields
    half2, half3 = levels // 2, levels // 4

    for ref, n in ((first_ref, levels), (pool2_ref, half2), (pool3_ref, half3), (join3_ref, half2),
                   (join2_ref, levels)):
        zero = jnp.zeros(ref.shape[1:], BF16)
        ref[0] = zero
        ref[n + 1] = zero
    net_ref[0] = jnp.zeros(net_ref.shape[1:], BF16)
    net_ref[levels + 1] = jnp.zeros(net_ref.shape[1:], BF16)
    net_ref[:, :, 80:128] = jnp.zeros((levels + 2, columns, 48), BF16)
    p_ref[:, 0:128] = jnp.zeros((24, 128), F32)
    p_ref[:, levels * NB + 128 :] = jnp.zeros((24, 128), F32)
    acc_ref[...] = jnp.zeros(acc_ref.shape, BF16)
    w1s_ref[...] = jnp.zeros(w1s_ref.shape, BF16)
    for t in range(3):
        w1s_ref[128 * t : 128 * t + taps, :] = w1_ref[taps * t : taps * (t + 1), :] * BF16(0.5)
    w_ref[...] = wi_ref[...] * BF16(0.5)
    w24 = jnp.concatenate([wl_ref[:, ch * t : ch * (t + 1)].astype(F32) for t in range(3)], axis=0).astype(BF16)

    me = lax.rem(dev_ref[0], GROUP)
    members = (m0_ref, m1_ref, m2_ref, m3_ref)
    upto = jnp.where(iota((columns, columns), 0) < iota((columns, columns), 1), 1.0, 0.0).astype(BF16)
    metas = [ref[rows : rows + 16, :] for ref in members]
    flags = [meta.astype(F32)[9:10, :] for meta in metas]
    counts = [jnp.sum(flag, axis=1, keepdims=True) for flag in flags]
    ranks, targets, active = [], [], jnp.zeros((1, 1), F32)
    for d in range(GROUP):
        start = jnp.zeros((1, 1), F32)
        for other in range(GROUP):
            start = start + jnp.where((me ^ other) < (me ^ d), counts[other], 0.0)
        local = jnp.dot(metas[d], upto, preferred_element_type=F32)[9:10, :].astype(jnp.int32)
        rank = local + start.astype(jnp.int32)
        ranks.append(jnp.where(flags[d] > 0, rank, -1))
        targets.append(jnp.where(flags[d] > 0, d * quota + local // GROUP + 1, 0).astype(F32))
        if d == 0:
            code_ref[...] = jnp.where(flags[d] > 0, (lax.rem(rank, GROUP) ^ me) * quota + local // GROUP, -1)
        active = active + counts[d]
    meta = jnp.concatenate(metas, axis=1)
    rank = jnp.concatenate(ranks, axis=1)
    share = (jnp.sum(active).astype(jnp.int32) - me + GROUP - 1) // GROUP
    slot = GROUP * iota((columns, wide), 0) + me
    choose = jnp.where(slot == rank, 1.0, 0.0).astype(BF16)
    flip = (((1,), (1,)), ((), ()))
    sten = lax.dot_general(meta, choose, flip, preferred_element_type=F32)
    part = (iota((16, wide), 1) // columns).astype(F32).astype(BF16)
    part = lax.dot_general(part, choose, flip, preferred_element_type=F32)
    sten = (sten + columns * part).astype(jnp.int32)
    target = jnp.broadcast_to(jnp.concatenate(targets, axis=1), (128, wide)).astype(BF16)
    to = lax.dot_general(choose, target, flip, preferred_element_type=F32).astype(jnp.int32) - 1
    to_ref[...] = jnp.where(to >= 0, to // quota * (2 * quota) + lax.rem(to, quota), -1)

    @pl.loop(0, (share + 127) // 128)
    def _(q):
        lanes = pl.ds(pl.multiple_of(q * 128, 128), 128)
        for k in range(9):
            for half in range(columns // 128):
                here = sten[k : k + 1, half * 128 : (half + 1) * 128]
                picked = here if half == 0 else jnp.where(q == half, here, picked)
            oh_ref[:, k * 128 : (k + 1) * 128] = jnp.where(iota((wide, 128), 0) == picked, 1.0, 0.0).astype(BF16)
        for k in range(0, 9, 2):
            n = 2 if k < 8 else 1
            got = jnp.dot(jnp.concatenate([ref[0:rows, :] for ref in members], axis=1), oh_ref[:, k * 128 : (k + n) * 128], preferred_element_type=F32)
            parts = [got[:, u * 128 : (u + 1) * 128].reshape(levels, fields, 128) for u in range(n)]
            if n == 1:
                parts.append(jnp.zeros_like(parts[0]))
            g_ref[0:levels, k * 8 : k * 8 + 16, :] = jnp.concatenate(parts, axis=1).astype(BF16)

        for l in range(levels):
            net_ref[l + 1, lanes, 0:80] = g_ref[l].T

    mask = jnp.where(iota((128 // NB * 8, 128), 0) // 8 == iota((128 // NB * 8, 128), 1) // NB, 1.0, 0.0)

    @pl.loop(0, (share + NB - 1) // NB)
    def _(b):
        c0 = pl.multiple_of(b * NB, NB)

        def conv(load, weight, n, emit):
            step = max(s for s in range(1, STEP + 1) if n % s == 0)
            for l0 in range(0, n, step):
                x = [load(l0 + t, step).reshape(step * NB, -1) for t in range(3)]
                acc = jnp.dot(jnp.concatenate(x, axis=1), weight, preferred_element_type=F32)
                emit(l0, step, silu(acc).reshape(step, NB, ch))

        def emit_first(l0, step, y):
            first_ref[l0 + 1 : l0 + 1 + step] = y

        def emit_second(l0, step, y):
            second_ref[l0 : l0 + step] = y
            pool2_ref[l0 // 2 + 1 : l0 // 2 + 1 + step // 2] = halve(y)

        def emit_third(l0, step, y):
            third_ref[l0 : l0 + step] = y
            pool3_ref[l0 // 2 + 1 : l0 // 2 + 1 + step // 2] = halve(y)

        def emit_deepest(l0, step, y):
            fine = third_ref[2 * l0 : 2 * (l0 + step)]
            join3_ref[2 * l0 + 1 : 2 * (l0 + step) + 1] = widen(y, fine)

        def emit_upper(l0, step, y):
            fine = second_ref[2 * l0 : 2 * (l0 + step)]
            join2_ref[2 * l0 + 1 : 2 * (l0 + step) + 1] = widen(y, fine)

        def emit_top(l0, step, y):
            top_ref[l0 : l0 + step] = y

        conv(lambda l, n: net_ref[l : l + n, pl.ds(c0, NB), :], w1s_ref[...], levels, emit_first)
        conv(lambda l, n: first_ref[l : l + n], w_ref[0], levels, emit_second)
        conv(lambda l, n: pool2_ref[l : l + n], w_ref[1], half2, emit_third)
        conv(lambda l, n: pool3_ref[l : l + n], w_ref[2], half3, emit_deepest)
        conv(lambda l, n: join3_ref[l : l + n], w_ref[3], half2, emit_upper)
        conv(lambda l, n: join2_ref[l : l + n], w_ref[4], levels, emit_top)

        group = 384
        for i in range(0, levels * NB, group):
            x = top_ref[i // NB : (i + group) // NB].reshape(group, ch)
            p_ref[:, i + 128 : i + group + 128] = lax.dot_general(w24, x, flip, preferred_element_type=F32)
        n = levels * NB
        out = p_ref[0:8, 128 - NB : n + 128 - NB] + p_ref[8:16, 128 : n + 128] + p_ref[16:24, 128 + NB : n + 128 + NB]
        tiles = []
        for i in range(n // 128):
            tile = out[:, i * 128 : (i + 1) * 128]
            tiles.append(jnp.concatenate([tile] * (128 // NB), axis=0) * mask)
        flat = jnp.concatenate(tiles, axis=0).astype(BF16)
        to = to_ref[pl.ds(c0, NB), :]
        place = []
        for h in range(2):
            lane = jnp.concatenate([to + jnp.where(to >= 0, h * quota, 0)] * (128 // NB), axis=0)
            hits = [jnp.where(lane == iota((128, 128), 1) + i * 128, 1.0, 0.0) for i in range(2 * columns // 128)]
            place.append(jnp.concatenate(hits, axis=1).astype(BF16))
        both = jnp.concatenate([flat[: rows // 2], flat[rows // 2 :]], axis=1)
        acc_ref[...] += jnp.dot(both, jnp.concatenate(place, axis=0), preferred_element_type=F32).astype(BF16)

    for d, ref in enumerate((r0_ref, r1_ref, r2_ref, r3_ref)):
        ref[...] = acc_ref[:, d * 2 * quota : (d + 1) * 2 * quota]


def per_device(state, kappa, edge_nbrs, stencil, owner, w_first, w_inner, w_last):
    fields, levels, columns = state.shape
    rows = fields * levels
    ch = w_inner.shape[2]
    devices = lax.axis_size(AXES)
    device = lax.axis_index(AXES)
    total = columns // 16 * devices
    dev = device.astype(jnp.int32).reshape(1)
    table, holder = node_tables(columns)
    f32 = functools.partial(jax.ShapeDtypeStruct, dtype=F32)
    bf16 = functools.partial(jax.ShapeDtypeStruct, dtype=BF16)
    i32 = functools.partial(jax.ShapeDtypeStruct, dtype=jnp.int32)

    payload = pl.pallas_call(
        pack_kernel,
        out_shape=bf16((rows + 16, columns)),
        in_specs=[SMEM] + [VMEM] * 3,
        out_specs=VMEM,
        name="pack",
    )(dev, state, stencil.T, owner.reshape(1, columns))
    def trade(x, d):
        return lax.ppermute(x, AXES, [(i, i ^ d) for i in range(devices)])

    member1 = trade(payload, 1)
    member2 = trade(payload, 2)

    base, edges, facing = pl.pallas_call(
        functools.partial(edges_kernel, total),
        out_shape=(f32((rows, columns)), bf16((rows, columns // 2)), i32((1, columns))),
        in_specs=[SMEM] + [VMEM] * 7,
        out_specs=(VMEM, VMEM, VMEM),
        cost_estimate=pl.CostEstimate(flops=3 * 10**9, bytes_accessed=2**21, transcendentals=0),
        name="edges",
    )(dev, state, kappa.reshape(1, columns), jnp.asarray(diffusion_matrix(columns)),
      jnp.asarray(edge_matrix(columns)), edge_nbrs.T, jnp.asarray(table), jnp.asarray(holder))

    member2, base = lax.optimization_barrier((member2, base))
    member3 = trade(member2, 1)
    low = lax.ppermute(edges, AXES, [(i, (i + 1) % devices) for i in range(devices)])
    high = lax.ppermute(edges, AXES, [(i, (i - 1) % devices) for i in range(devices)])

    bf = lambda *shape: pltpu.VMEM(shape, BF16)
    lanes = 2 * columns // GROUP
    *results, code = pl.pallas_call(
        functools.partial(net_kernel, levels, fields),
        out_shape=[bf16((rows // 2, lanes))] * GROUP + [i32((1, columns))],
        in_specs=[SMEM] + [VMEM] * (GROUP + 1) + [VMEM] * 2,
        out_specs=[VMEM] * (GROUP + 1),
        scratch_shapes=[
            bf(GROUP * columns, 9 * 128),
            bf(levels, 80, 128),
            bf(levels + 2, columns, 128),
            bf(3 * 128, ch),
            bf(*w_inner.shape),
            bf(levels + 2, NB, ch),
            bf(levels, NB, ch),
            bf(levels // 2 + 2, NB, ch),
            bf(levels // 2, NB, ch),
            bf(levels // 4 + 2, NB, ch),
            bf(levels // 2 + 2, NB, ch),
            bf(levels + 2, NB, ch),
            bf(levels, NB, ch),
            pltpu.VMEM((24, levels * NB + 256), F32),
            bf(rows // 2, GROUP * lanes),
            pltpu.VMEM((columns, 128), jnp.int32),
        ],
        compiler_params=pltpu.CompilerParams(vmem_limit_bytes=30 * 1024 * 1024),
        cost_estimate=pl.CostEstimate(flops=10**10, bytes_accessed=2**22, transcendentals=10**7),
        name="network",
    )(dev, payload, member1, member2, member3, w_first, w_inner, w_last.T)
    back = [trade(results[d], d) for d in (3, 2, 1)][::-1]

    middle = pl.pallas_call(
        middle_kernel,
        out_shape=f32((rows, columns)),
        in_specs=[VMEM] * 4,
        out_specs=VMEM,
        cost_estimate=pl.CostEstimate(flops=10**9, bytes_accessed=2**22, transcendentals=0),
        compiler_params=SMALL,
        name="middle",
    )(*lax.optimization_barrier((base, low, high, facing, results[0]))[:4])

    return pl.pallas_call(
        final_kernel,
        out_shape=f32((fields, levels, columns)),
        in_specs=[VMEM] * 6,
        out_specs=VMEM,
        compiler_params=SMALL,
        name="combine",
    )(middle.reshape(fields, levels, columns), code, results[0], *back)


def solution(mesh):
    in_specs = (
        P(None, None, AXES),
        P(AXES),
        P(AXES, None),
        P(AXES, None),
        P(AXES),
        P(),
        P(),
        P(),
    )
    return jax.shard_map(
        per_device, mesh=mesh, in_specs=in_specs, out_specs=P(None, None, AXES), check_vma=False
    )
```

```python
import functools
import math

import jax
import jax.numpy as jnp
import numpy as np
from jax import lax
from jax.experimental import pallas as pl
from jax.experimental.pallas import tpu as pltpu
from jax.sharding import PartitionSpec as P

AXES = ("grp", "elem")
EDGE_NODES = ((1, 2), (7, 11), (14, 13), (8, 4))
VMEM = pl.BlockSpec(memory_space=pltpu.VMEM)
SMALL = pltpu.CompilerParams(vmem_limit_bytes=12 * 1024 * 1024)
SMEM = pl.BlockSpec(memory_space=pltpu.SMEM)
HIGHEST = lax.Precision.HIGHEST
BF16 = jnp.bfloat16
F32 = jnp.float32
NB = 32
STEP = 12
GROUP = 4


def second_derivative():
    points = np.array([-1.0, -math.sqrt(0.2), math.sqrt(0.2), 1.0])
    factors = np.array(
        [1.0 / np.prod([points[j] - points[m] for m in range(4) if m != j]) for j in range(4)]
    )
    deriv = np.zeros((4, 4))
    for i in range(4):
        for j in range(4):
            if i != j:
                deriv[i, j] = factors[j] / factors[i] / (points[i] - points[j])
        deriv[i, i] = -np.sum(deriv[i])
    return deriv @ deriv


def diffusion_matrix(columns):
    lap = second_derivative()
    eye = np.eye(4)
    node = np.einsum("ia,jb->abij", lap, eye) + np.einsum("ia,jb->abij", eye, lap)
    return np.kron(np.eye(columns // 16), node.reshape(16, 16)).astype(np.float32)


def edge_matrix(columns):
    sel = np.zeros((columns, columns // 2), np.float32)
    for e in range(columns // 16):
        for k in range(4):
            for m in range(2):
                sel[16 * e + EDGE_NODES[k][m], 8 * e + 2 * k + m] = 1
    return sel


def node_tables(columns):
    on_edge = np.zeros((4, columns), np.float32)
    offset = np.zeros((1, columns), np.float32)
    for k in range(4):
        for m in range(2):
            on_edge[k, EDGE_NODES[k][m] :: 16] = 1
            offset[0, EDGE_NODES[k][m] :: 16] = (k + 2) % 4 * 2 + 1 - m
    holder = np.kron(np.eye(columns // 16), np.ones((1, 16))).astype(np.float32)
    table = np.concatenate([on_edge, offset, np.zeros((3, columns), np.float32)], axis=0)
    return table, holder


def iota(shape, dim):
    return lax.broadcasted_iota(jnp.int32, shape, dim)


def silu(half):
    return (half + half * jnp.tanh(half)).astype(BF16)


def pack_kernel(dev_ref, state_ref, sten_ref, owner_ref, pay_ref):
    fields, levels, columns = state_ref.shape
    rows = fields * levels
    for l in range(0, levels, 2):
        pair = jnp.concatenate([state_ref[:, l, :], state_ref[:, l + 1, :]], axis=0)
        pay_ref[l * fields : (l + 2) * fields, :] = pair.astype(BF16)
    local = (sten_ref[...] - dev_ref[0] * columns).astype(F32)
    flag = jnp.where(owner_ref[...] >= 0, 1.0, 0.0)
    tail = jnp.concatenate([local, flag, jnp.zeros((6, columns), F32)], axis=0)
    pay_ref[rows : rows + 16, :] = tail.astype(BF16)


def edges_kernel(total, dev_ref, state_ref, kappa_ref, op_ref, sel_ref, nbr_ref, table_ref, holder_ref,
                 base_ref, edge_ref, facing_ref):
    fields, levels, columns = state_ref.shape
    elements = columns // 16
    flat = state_ref[...].reshape(fields * levels, columns)
    dyn = kappa_ref[...] * jnp.dot(flat, op_ref[...], precision=HIGHEST)
    edge = jnp.dot(dyn, sel_ref[...], precision=HIGHEST)
    edge_ref[...] = edge.astype(BF16)
    rel = lax.rem(nbr_ref[...] - (dev_ref[0] - 1) * elements + total, total).astype(F32)
    spread = jnp.dot(rel, holder_ref[...], precision=HIGHEST)
    on_edge = table_ref[0:4, :]
    is_edge = jnp.sum(on_edge, axis=0, keepdims=True)
    facing = 8.0 * jnp.sum(spread * on_edge, axis=0, keepdims=True) + table_ref[4:5, :]
    facing = jnp.where(is_edge > 0, facing, -1.0).astype(jnp.int32)
    facing_ref[...] = facing
    half = columns // 2
    pick = jnp.where(iota((half, columns), 0) + half == facing, 0.5, 0.0)
    own = jnp.dot(edge, pick, precision=HIGHEST)
    base_ref[...] = flat + (1.0 - 0.5 * is_edge) * dyn + own


def land(code, d, quota, columns):
    slot = jnp.where((code >= d * quota) & (code < (d + 1) * quota), code - d * quota, -2 * quota)
    spot = iota((2 * quota, columns), 0)
    return [jnp.where(spot == slot + h * quota, 1.0, 0.0).astype(BF16) for h in range(2)]


def middle_kernel(base_ref, low_ref, high_ref, facing_ref, out_ref):
    rows, columns = base_ref.shape
    half = columns // 2
    facing = facing_ref[...]
    acc = base_ref[...]
    for part, ref in ((0, low_ref), (2, high_ref)):
        pick = jnp.where(iota((half, columns), 0) + part * half == facing, 0.5, 0.0).astype(BF16)
        acc = acc + jnp.dot(ref[...], pick, preferred_element_type=F32)
    out_ref[...] = acc


def final_kernel(base_ref, code_ref, r0_ref, r1_ref, r2_ref, r3_ref, out_ref):
    fields, levels, columns = out_ref.shape
    quota = columns // GROUP
    code = code_ref[...]
    got = jnp.concatenate([r0_ref[...], r1_ref[...], r2_ref[...], r3_ref[...]], axis=1)
    puts = [land(code, d, quota, columns) for d in range(GROUP)]
    for h in range(2):
        put = jnp.concatenate([p[h] for p in puts], axis=0)
        physics = jnp.dot(got, put, preferred_element_type=F32)
        for i in range(levels // 2):
            l = h * (levels // 2) + i
            out_ref[:, l, :] = base_ref[:, l, :] + physics[i * fields : (i + 1) * fields, :]


def halve(y):
    y = y.reshape(y.shape[0] // 2, 2, *y.shape[1:])
    return (y[:, 0] + y[:, 1]) * BF16(0.5)


def widen(coarse, fine):
    step, cols, ch = coarse.shape
    return jnp.broadcast_to(coarse[:, None], (step, 2, cols, ch)).reshape(2 * step, cols, ch) + fine


def net_kernel(levels, fields, dev_ref, m0_ref, m1_ref, m2_ref, m3_ref, w1_ref, wi_ref, wl_ref,
               r0_ref, r1_ref, r2_ref, r3_ref, code_ref,
               oh_ref, g_ref, net_ref, w1s_ref, w_ref, first_ref, second_ref, pool2_ref, third_ref,
               pool3_ref, join3_ref, join2_ref, top_ref, p_ref, acc_ref, to_ref):
    rows = fields * levels
    columns = m0_ref.shape[1]
    quota = columns // GROUP
    wide = GROUP * columns
    ch = wi_ref.shape[2]
    taps = 9 * fields
    half2, half3 = levels // 2, levels // 4

    for ref, n in ((first_ref, levels), (pool2_ref, half2), (pool3_ref, half3), (join3_ref, half2),
                   (join2_ref, levels)):
        zero = jnp.zeros(ref.shape[1:], BF16)
        ref[0] = zero
        ref[n + 1] = zero
    net_ref[0] = jnp.zeros(net_ref.shape[1:], BF16)
    net_ref[levels + 1] = jnp.zeros(net_ref.shape[1:], BF16)
    net_ref[:, :, 80:128] = jnp.zeros((levels + 2, columns, 48), BF16)
    p_ref[:, 0:128] = jnp.zeros((24, 128), F32)
    p_ref[:, levels * NB + 128 :] = jnp.zeros((24, 128), F32)
    acc_ref[...] = jnp.zeros(acc_ref.shape, BF16)
    w1s_ref[...] = jnp.zeros(w1s_ref.shape, BF16)
    for t in range(3):
        w1s_ref[128 * t : 128 * t + taps, :] = w1_ref[taps * t : taps * (t + 1), :] * BF16(0.5)
    for i in range(wi_ref.shape[0]):
        g = [wi_ref[i, ch * t : ch * (t + 1), :].astype(F32) for t in range(3)]
        sides, middle = 0.25 * (g[0] + g[2]), 0.25 * g[1]
        w_ref[4 * i] = (0.5 * g[0]).astype(BF16)
        w_ref[4 * i + 1] = (sides + middle).astype(BF16)
        w_ref[4 * i + 2] = (sides - middle).astype(BF16)
        w_ref[4 * i + 3] = (0.5 * g[2]).astype(BF16)
    w24 = jnp.concatenate([wl_ref[:, ch * t : ch * (t + 1)].astype(F32) for t in range(3)], axis=0).astype(BF16)

    me = lax.rem(dev_ref[0], GROUP)
    members = (m0_ref, m1_ref, m2_ref, m3_ref)
    upto = jnp.where(iota((columns, columns), 0) < iota((columns, columns), 1), 1.0, 0.0).astype(BF16)
    metas = [ref[rows : rows + 16, :] for ref in members]
    flags = [meta.astype(F32)[9:10, :] for meta in metas]
    counts = [jnp.sum(flag, axis=1, keepdims=True) for flag in flags]
    ranks, targets, active = [], [], jnp.zeros((1, 1), F32)
    for d in range(GROUP):
        start = jnp.zeros((1, 1), F32)
        for other in range(GROUP):
            start = start + jnp.where((me ^ other) < (me ^ d), counts[other], 0.0)
        local = jnp.dot(metas[d], upto, preferred_element_type=F32)[9:10, :].astype(jnp.int32)
        rank = local + start.astype(jnp.int32)
        ranks.append(jnp.where(flags[d] > 0, rank, -1))
        targets.append(jnp.where(flags[d] > 0, d * quota + local // GROUP + 1, 0).astype(F32))
        if d == 0:
            code_ref[...] = jnp.where(flags[d] > 0, (lax.rem(rank, GROUP) ^ me) * quota + local // GROUP, -1)
        active = active + counts[d]
    meta = jnp.concatenate(metas, axis=1)
    rank = jnp.concatenate(ranks, axis=1)
    share = (jnp.sum(active).astype(jnp.int32) - me + GROUP - 1) // GROUP
    slot = GROUP * iota((columns, wide), 0) + me
    choose = jnp.where(slot == rank, 1.0, 0.0).astype(BF16)
    flip = (((1,), (1,)), ((), ()))
    sten = lax.dot_general(meta, choose, flip, preferred_element_type=F32)
    part = (iota((16, wide), 1) // columns).astype(F32).astype(BF16)
    part = lax.dot_general(part, choose, flip, preferred_element_type=F32)
    sten = (sten + columns * part).astype(jnp.int32)
    target = jnp.broadcast_to(jnp.concatenate(targets, axis=1), (128, wide)).astype(BF16)
    to = lax.dot_general(choose, target, flip, preferred_element_type=F32).astype(jnp.int32) - 1
    to_ref[...] = jnp.where(to >= 0, to // quota * (2 * quota) + lax.rem(to, quota), -1)

    @pl.loop(0, (share + 127) // 128)
    def _(q):
        lanes = pl.ds(pl.multiple_of(q * 128, 128), 128)
        for k in range(9):
            for half in range(columns // 128):
                here = sten[k : k + 1, half * 128 : (half + 1) * 128]
                picked = here if half == 0 else jnp.where(q == half, here, picked)
            oh_ref[:, k * 128 : (k + 1) * 128] = jnp.where(iota((wide, 128), 0) == picked, 1.0, 0.0).astype(BF16)
        for k in range(0, 9, 2):
            n = 2 if k < 8 else 1
            got = jnp.dot(jnp.concatenate([ref[0:rows, :] for ref in members], axis=1), oh_ref[:, k * 128 : (k + n) * 128], preferred_element_type=F32)
            parts = [got[:, u * 128 : (u + 1) * 128].reshape(levels, fields, 128) for u in range(n)]
            if n == 1:
                parts.append(jnp.zeros_like(parts[0]))
            g_ref[0:levels, k * 8 : k * 8 + 16, :] = jnp.concatenate(parts, axis=1).astype(BF16)

        for l in range(levels):
            net_ref[l + 1, lanes, 0:80] = g_ref[l].T

    mask = jnp.where(iota((128 // NB * 8, 128), 0) // 8 == iota((128 // NB * 8, 128), 1) // NB, 1.0, 0.0)

    @pl.loop(0, (share + NB - 1) // NB)
    def _(b):
        c0 = pl.multiple_of(b * NB, NB)

        def conv_first(n, emit):
            for l0 in range(0, n, STEP):
                x = [net_ref[l0 + t : l0 + t + STEP, pl.ds(c0, NB), :].reshape(STEP * NB, 128) for t in range(3)]
                acc = jnp.dot(jnp.concatenate(x, axis=1), w1s_ref[...], preferred_element_type=F32)
                emit(l0, STEP, silu(acc).reshape(STEP, NB, ch))

        def conv(src, layer, n, emit):
            step = min(n, 2 * STEP)
            while n % step or step % 2:
                step -= 1
            pairs = step // 2
            for l0 in range(0, n, step):
                x = src[l0 : l0 + step + 2].reshape(pairs + 1, 2, NB, ch)
                even, odd = x[:, 0], x[:, 1]
                d0, d1, d2, d3 = even[:-1], odd[:-1], even[1:], odd[1:]
                m = [jnp.dot(d.reshape(pairs * NB, ch), w_ref[4 * layer + i], preferred_element_type=F32)
                     for i, d in enumerate((d0 - d2, d1 + d2, d2 - d1, d1 - d3))]
                y = [silu(m[0] + (m[1] + m[2])), silu((m[1] - m[2]) - m[3])]
                y = jnp.concatenate([v.reshape(pairs, 1, NB, ch) for v in y], axis=1)
                emit(l0, step, y.reshape(step, NB, ch))

        def emit_first(l0, step, y):
            first_ref[l0 + 1 : l0 + 1 + step] = y

        def emit_second(l0, step, y):
            second_ref[l0 : l0 + step] = y
            pool2_ref[l0 // 2 + 1 : l0 // 2 + 1 + step // 2] = halve(y)

        def emit_third(l0, step, y):
            third_ref[l0 : l0 + step] = y
            pool3_ref[l0 // 2 + 1 : l0 // 2 + 1 + step // 2] = halve(y)

        def emit_deepest(l0, step, y):
            fine = third_ref[2 * l0 : 2 * (l0 + step)]
            join3_ref[2 * l0 + 1 : 2 * (l0 + step) + 1] = widen(y, fine)

        def emit_upper(l0, step, y):
            fine = second_ref[2 * l0 : 2 * (l0 + step)]
            join2_ref[2 * l0 + 1 : 2 * (l0 + step) + 1] = widen(y, fine)

        def emit_top(l0, step, y):
            top_ref[l0 : l0 + step] = y

        conv_first(levels, emit_first)
        conv(first_ref, 0, levels, emit_second)
        conv(pool2_ref, 1, half2, emit_third)
        conv(pool3_ref, 2, half3, emit_deepest)
        conv(join3_ref, 3, half2, emit_upper)
        conv(join2_ref, 4, levels, emit_top)

        group = 384
        for i in range(0, levels * NB, group):
            x = top_ref[i // NB : (i + group) // NB].reshape(group, ch)
            p_ref[:, i + 128 : i + group + 128] = lax.dot_general(w24, x, flip, preferred_element_type=F32)
        n = levels * NB
        out = p_ref[0:8, 128 - NB : n + 128 - NB] + p_ref[8:16, 128 : n + 128] + p_ref[16:24, 128 + NB : n + 128 + NB]
        tiles = []
        for i in range(n // 128):
            tile = out[:, i * 128 : (i + 1) * 128]
            tiles.append(jnp.concatenate([tile] * (128 // NB), axis=0) * mask)
        flat = jnp.concatenate(tiles, axis=0).astype(BF16)
        to = to_ref[pl.ds(c0, NB), :]
        place = []
        for h in range(2):
            lane = jnp.concatenate([to + jnp.where(to >= 0, h * quota, 0)] * (128 // NB), axis=0)
            hits = [jnp.where(lane == iota((128, 128), 1) + i * 128, 1.0, 0.0) for i in range(2 * columns // 128)]
            place.append(jnp.concatenate(hits, axis=1).astype(BF16))
        both = jnp.concatenate([flat[: rows // 2], flat[rows // 2 :]], axis=1)
        acc_ref[...] += jnp.dot(both, jnp.concatenate(place, axis=0), preferred_element_type=F32).astype(BF16)

    for d, ref in enumerate((r0_ref, r1_ref, r2_ref, r3_ref)):
        ref[...] = acc_ref[:, d * 2 * quota : (d + 1) * 2 * quota]


def per_device(state, kappa, edge_nbrs, stencil, owner, w_first, w_inner, w_last):
    fields, levels, columns = state.shape
    rows = fields * levels
    ch = w_inner.shape[2]
    devices = lax.axis_size(AXES)
    device = lax.axis_index(AXES)
    total = columns // 16 * devices
    dev = device.astype(jnp.int32).reshape(1)
    table, holder = node_tables(columns)
    f32 = functools.partial(jax.ShapeDtypeStruct, dtype=F32)
    bf16 = functools.partial(jax.ShapeDtypeStruct, dtype=BF16)
    i32 = functools.partial(jax.ShapeDtypeStruct, dtype=jnp.int32)

    payload = pl.pallas_call(
        pack_kernel,
        out_shape=bf16((rows + 16, columns)),
        in_specs=[SMEM] + [VMEM] * 3,
        out_specs=VMEM,
        name="pack",
    )(dev, state, stencil.T, owner.reshape(1, columns))
    def trade(x, d):
        return lax.ppermute(x, AXES, [(i, i ^ d) for i in range(devices)])

    member1 = trade(payload, 1)
    member2 = trade(payload, 2)

    base, edges, facing = pl.pallas_call(
        functools.partial(edges_kernel, total),
        out_shape=(f32((rows, columns)), bf16((rows, columns // 2)), i32((1, columns))),
        in_specs=[SMEM] + [VMEM] * 7,
        out_specs=(VMEM, VMEM, VMEM),
        cost_estimate=pl.CostEstimate(flops=3 * 10**9, bytes_accessed=2**21, transcendentals=0),
        name="edges",
    )(dev, state, kappa.reshape(1, columns), jnp.asarray(diffusion_matrix(columns)),
      jnp.asarray(edge_matrix(columns)), edge_nbrs.T, jnp.asarray(table), jnp.asarray(holder))

    member2, base = lax.optimization_barrier((member2, base))
    member3 = trade(member2, 1)
    low = lax.ppermute(edges, AXES, [(i, (i + 1) % devices) for i in range(devices)])
    high = lax.ppermute(edges, AXES, [(i, (i - 1) % devices) for i in range(devices)])

    bf = lambda *shape: pltpu.VMEM(shape, BF16)
    lanes = 2 * columns // GROUP
    *results, code = pl.pallas_call(
        functools.partial(net_kernel, levels, fields),
        out_shape=[bf16((rows // 2, lanes))] * GROUP + [i32((1, columns))],
        in_specs=[SMEM] + [VMEM] * (GROUP + 1) + [VMEM] * 2,
        out_specs=[VMEM] * (GROUP + 1),
        scratch_shapes=[
            bf(GROUP * columns, 9 * 128),
            bf(levels, 80, 128),
            bf(levels + 2, columns, 128),
            bf(3 * 128, ch),
            bf(4 * w_inner.shape[0], ch, ch),
            bf(levels + 2, NB, ch),
            bf(levels, NB, ch),
            bf(levels // 2 + 2, NB, ch),
            bf(levels // 2, NB, ch),
            bf(levels // 4 + 2, NB, ch),
            bf(levels // 2 + 2, NB, ch),
            bf(levels + 2, NB, ch),
            bf(levels, NB, ch),
            pltpu.VMEM((24, levels * NB + 256), F32),
            bf(rows // 2, GROUP * lanes),
            pltpu.VMEM((columns, 128), jnp.int32),
        ],
        compiler_params=pltpu.CompilerParams(vmem_limit_bytes=30 * 1024 * 1024),
        cost_estimate=pl.CostEstimate(flops=10**10, bytes_accessed=2**22, transcendentals=10**7),
        name="network",
    )(dev, payload, member1, member2, member3, w_first, w_inner, w_last.T)
    back = [trade(results[d], d) for d in (3, 2, 1)][::-1]

    middle = pl.pallas_call(
        middle_kernel,
        out_shape=f32((rows, columns)),
        in_specs=[VMEM] * 4,
        out_specs=VMEM,
        cost_estimate=pl.CostEstimate(flops=10**9, bytes_accessed=2**22, transcendentals=0),
        compiler_params=SMALL,
        name="middle",
    )(*lax.optimization_barrier((base, low, high, facing, results[0]))[:4])

    return pl.pallas_call(
        final_kernel,
        out_shape=f32((fields, levels, columns)),
        in_specs=[VMEM] * 6,
        out_specs=VMEM,
        compiler_params=SMALL,
        name="combine",
    )(middle.reshape(fields, levels, columns), code, results[0], *back)


def solution(mesh):
    in_specs = (
        P(None, None, AXES),
        P(AXES),
        P(AXES, None),
        P(AXES, None),
        P(AXES),
        P(),
        P(),
        P(),
    )
    return jax.shard_map(
        per_device, mesh=mesh, in_specs=in_specs, out_specs=P(None, None, AXES), check_vma=False
    )
```

```python
import functools
import math

import jax
import jax.numpy as jnp
import numpy as np
from jax import lax
from jax.experimental import pallas as pl
from jax.experimental.pallas import tpu as pltpu
from jax.sharding import PartitionSpec as P

AXES = ("grp", "elem")
EDGE_NODES = ((1, 2), (7, 11), (14, 13), (8, 4))
VMEM = pl.BlockSpec(memory_space=pltpu.VMEM)
SMALL = pltpu.CompilerParams(vmem_limit_bytes=12 * 1024 * 1024)
SMEM = pl.BlockSpec(memory_space=pltpu.SMEM)
HIGHEST = lax.Precision.HIGHEST
BF16 = jnp.bfloat16
F32 = jnp.float32
NB = 32
STEP = 12
GROUP = 4


def second_derivative():
    points = np.array([-1.0, -math.sqrt(0.2), math.sqrt(0.2), 1.0])
    factors = np.array(
        [1.0 / np.prod([points[j] - points[m] for m in range(4) if m != j]) for j in range(4)]
    )
    deriv = np.zeros((4, 4))
    for i in range(4):
        for j in range(4):
            if i != j:
                deriv[i, j] = factors[j] / factors[i] / (points[i] - points[j])
        deriv[i, i] = -np.sum(deriv[i])
    return deriv @ deriv


def diffusion_matrix(columns):
    lap = second_derivative()
    eye = np.eye(4)
    node = np.einsum("ia,jb->abij", lap, eye) + np.einsum("ia,jb->abij", eye, lap)
    return np.kron(np.eye(columns // 16), node.reshape(16, 16)).astype(np.float32)


def edge_matrix(columns):
    sel = np.zeros((columns, columns // 2), np.float32)
    for e in range(columns // 16):
        for k in range(4):
            for m in range(2):
                sel[16 * e + EDGE_NODES[k][m], 8 * e + 2 * k + m] = 1
    return sel


def node_tables(columns):
    on_edge = np.zeros((4, columns), np.float32)
    offset = np.zeros((1, columns), np.float32)
    for k in range(4):
        for m in range(2):
            on_edge[k, EDGE_NODES[k][m] :: 16] = 1
            offset[0, EDGE_NODES[k][m] :: 16] = (k + 2) % 4 * 2 + 1 - m
    holder = np.kron(np.eye(columns // 16), np.ones((1, 16))).astype(np.float32)
    table = np.concatenate([on_edge, offset, np.zeros((3, columns), np.float32)], axis=0)
    return table, holder


def iota(shape, dim):
    return lax.broadcasted_iota(jnp.int32, shape, dim)


def silu(half):
    half = half.astype(BF16)
    return half + half * jnp.tanh(half)


def pack_kernel(dev_ref, state_ref, sten_ref, owner_ref, pay_ref):
    fields, levels, columns = state_ref.shape
    rows = fields * levels
    for l in range(0, levels, 2):
        pair = jnp.concatenate([state_ref[:, l, :], state_ref[:, l + 1, :]], axis=0)
        pay_ref[l * fields : (l + 2) * fields, :] = pair.astype(BF16)
    local = (sten_ref[...] - dev_ref[0] * columns).astype(F32)
    flag = jnp.where(owner_ref[...] >= 0, 1.0, 0.0)
    tail = jnp.concatenate([local, flag, jnp.zeros((6, columns), F32)], axis=0)
    pay_ref[rows : rows + 16, :] = tail.astype(BF16)


def edges_kernel(total, dev_ref, state_ref, kappa_ref, op_ref, sel_ref, nbr_ref, table_ref, holder_ref,
                 base_ref, edge_ref, facing_ref):
    fields, levels, columns = state_ref.shape
    elements = columns // 16
    flat = state_ref[...].reshape(fields * levels, columns)
    dyn = kappa_ref[...] * jnp.dot(flat, op_ref[...], precision=HIGHEST)
    edge = jnp.dot(dyn, sel_ref[...], precision=HIGHEST)
    edge_ref[...] = edge.astype(BF16)
    rel = lax.rem(nbr_ref[...] - (dev_ref[0] - 1) * elements + total, total).astype(F32)
    spread = jnp.dot(rel, holder_ref[...], precision=HIGHEST)
    on_edge = table_ref[0:4, :]
    is_edge = jnp.sum(on_edge, axis=0, keepdims=True)
    facing = 8.0 * jnp.sum(spread * on_edge, axis=0, keepdims=True) + table_ref[4:5, :]
    facing = jnp.where(is_edge > 0, facing, -1.0).astype(jnp.int32)
    facing_ref[...] = facing
    half = columns // 2
    pick = jnp.where(iota((half, columns), 0) + half == facing, 0.5, 0.0)
    own = jnp.dot(edge, pick, precision=HIGHEST)
    base_ref[...] = flat + (1.0 - 0.5 * is_edge) * dyn + own


def land(code, d, quota, columns):
    slot = jnp.where((code >= d * quota) & (code < (d + 1) * quota), code - d * quota, -2 * quota)
    spot = iota((2 * quota, columns), 0)
    return [jnp.where(spot == slot + h * quota, 1.0, 0.0).astype(BF16) for h in range(2)]


def middle_kernel(base_ref, low_ref, high_ref, facing_ref, out_ref):
    rows, columns = base_ref.shape
    half = columns // 2
    facing = facing_ref[...]
    acc = base_ref[...]
    for part, ref in ((0, low_ref), (2, high_ref)):
        pick = jnp.where(iota((half, columns), 0) + part * half == facing, 0.5, 0.0).astype(BF16)
        acc = acc + jnp.dot(ref[...], pick, preferred_element_type=F32)
    out_ref[...] = acc


def final_kernel(base_ref, code_ref, r0_ref, r1_ref, r2_ref, r3_ref, out_ref):
    fields, levels, columns = out_ref.shape
    quota = columns // GROUP
    code = code_ref[...]
    got = jnp.concatenate([r0_ref[...], r1_ref[...], r2_ref[...], r3_ref[...]], axis=1)
    puts = [land(code, d, quota, columns) for d in range(GROUP)]
    for h in range(2):
        put = jnp.concatenate([p[h] for p in puts], axis=0)
        physics = jnp.dot(got, put, preferred_element_type=F32)
        for i in range(levels // 2):
            l = h * (levels // 2) + i
            out_ref[:, l, :] = base_ref[:, l, :] + physics[i * fields : (i + 1) * fields, :]


def halve(y):
    y = y.reshape(y.shape[0] // 2, 2, *y.shape[1:])
    return (y[:, 0] + y[:, 1]) * BF16(0.5)


def widen(coarse, fine):
    step, cols, ch = coarse.shape
    return jnp.broadcast_to(coarse[:, None], (step, 2, cols, ch)).reshape(2 * step, cols, ch) + fine


def net_kernel(levels, fields, dev_ref, m0_ref, m1_ref, m2_ref, m3_ref, w1_ref, wi_ref, wl_ref,
               r0_ref, r1_ref, r2_ref, r3_ref, code_ref,
               oh_ref, g_ref, net_ref, w1s_ref, w_ref, first_ref, second_ref, pool2_ref, third_ref,
               pool3_ref, join3_ref, join2_ref, top_ref, p_ref, acc_ref, to_ref):
    rows = fields * levels
    columns = m0_ref.shape[1]
    quota = columns // GROUP
    wide = GROUP * columns
    ch = wi_ref.shape[2]
    taps = 9 * fields
    half2, half3 = levels // 2, levels // 4

    for ref, n in ((first_ref, levels), (pool2_ref, half2), (pool3_ref, half3), (join3_ref, half2),
                   (join2_ref, levels)):
        zero = jnp.zeros(ref.shape[1:], BF16)
        ref[0] = zero
        ref[n + 1] = zero
    net_ref[0] = jnp.zeros(net_ref.shape[1:], BF16)
    net_ref[levels + 1] = jnp.zeros(net_ref.shape[1:], BF16)
    net_ref[:, :, 80:128] = jnp.zeros((levels + 2, columns, 48), BF16)
    p_ref[:, 0:128] = jnp.zeros((24, 128), F32)
    p_ref[:, levels * NB + 128 :] = jnp.zeros((24, 128), F32)
    acc_ref[...] = jnp.zeros(acc_ref.shape, BF16)
    w1s_ref[...] = jnp.zeros(w1s_ref.shape, BF16)
    for t in range(3):
        w1s_ref[128 * t : 128 * t + taps, :] = w1_ref[taps * t : taps * (t + 1), :] * BF16(0.5)
    for i in range(wi_ref.shape[0]):
        g = [wi_ref[i, ch * t : ch * (t + 1), :] for t in range(3)]
        sides, middle = (g[0] + g[2]) * BF16(0.25), g[1] * BF16(0.25)
        w_ref[4 * i] = g[0] * BF16(0.5)
        w_ref[4 * i + 1] = sides + middle
        w_ref[4 * i + 2] = sides - middle
        w_ref[4 * i + 3] = g[2] * BF16(0.5)
    w24 = jnp.concatenate([wl_ref[:, ch * t : ch * (t + 1)].astype(F32) for t in range(3)], axis=0).astype(BF16)

    me = lax.rem(dev_ref[0], GROUP)
    members = (m0_ref, m1_ref, m2_ref, m3_ref)
    upto = jnp.where(iota((columns, columns), 0) < iota((columns, columns), 1), 1.0, 0.0).astype(BF16)
    metas = [ref[rows : rows + 16, :] for ref in members]
    flags = [meta.astype(F32)[9:10, :] for meta in metas]
    counts = [jnp.sum(flag, axis=1, keepdims=True) for flag in flags]
    ranks, targets, active = [], [], jnp.zeros((1, 1), F32)
    for d in range(GROUP):
        start = jnp.zeros((1, 1), F32)
        for other in range(GROUP):
            start = start + jnp.where((me ^ other) < (me ^ d), counts[other], 0.0)
        local = jnp.dot(metas[d], upto, preferred_element_type=F32)[9:10, :].astype(jnp.int32)
        rank = local + start.astype(jnp.int32)
        ranks.append(jnp.where(flags[d] > 0, rank, -1))
        targets.append(jnp.where(flags[d] > 0, d * quota + local // GROUP + 1, 0).astype(F32))
        if d == 0:
            code_ref[...] = jnp.where(flags[d] > 0, (lax.rem(rank, GROUP) ^ me) * quota + local // GROUP, -1)
        active = active + counts[d]
    meta = jnp.concatenate(metas, axis=1)
    rank = jnp.concatenate(ranks, axis=1)
    share = (jnp.sum(active).astype(jnp.int32) - me + GROUP - 1) // GROUP
    slot = GROUP * iota((columns, wide), 0) + me
    choose = jnp.where(slot == rank, 1.0, 0.0).astype(BF16)
    flip = (((1,), (1,)), ((), ()))
    sten = lax.dot_general(meta, choose, flip, preferred_element_type=F32)
    part = (iota((16, wide), 1) // columns).astype(F32).astype(BF16)
    part = lax.dot_general(part, choose, flip, preferred_element_type=F32)
    sten = (sten + columns * part).astype(jnp.int32)
    target = jnp.broadcast_to(jnp.concatenate(targets, axis=1), (128, wide)).astype(BF16)
    to = lax.dot_general(choose, target, flip, preferred_element_type=F32).astype(jnp.int32) - 1
    to_ref[...] = jnp.where(to >= 0, to // quota * (2 * quota) + lax.rem(to, quota), -1)

    @pl.loop(0, (share + 127) // 128)
    def _(q):
        lanes = pl.ds(pl.multiple_of(q * 128, 128), 128)
        for k in range(9):
            for half in range(columns // 128):
                here = sten[k : k + 1, half * 128 : (half + 1) * 128]
                picked = here if half == 0 else jnp.where(q == half, here, picked)
            oh_ref[:, k * 128 : (k + 1) * 128] = jnp.where(iota((wide, 128), 0) == picked, 1.0, 0.0).astype(BF16)
        for k in range(0, 9, 2):
            n = 2 if k < 8 else 1
            got = jnp.dot(jnp.concatenate([ref[0:rows, :] for ref in members], axis=1), oh_ref[:, k * 128 : (k + n) * 128], preferred_element_type=F32)
            parts = [got[:, u * 128 : (u + 1) * 128].reshape(levels, fields, 128) for u in range(n)]
            if n == 1:
                parts.append(jnp.zeros_like(parts[0]))
            g_ref[0:levels, k * 8 : k * 8 + 16, :] = jnp.concatenate(parts, axis=1).astype(BF16)

        for l in range(levels):
            net_ref[l + 1, lanes, 0:80] = g_ref[l].T

    mask = jnp.where(iota((128 // NB * 8, 128), 0) // 8 == iota((128 // NB * 8, 128), 1) // NB, 1.0, 0.0)

    @pl.loop(0, (share + NB - 1) // NB)
    def _(b):
        c0 = pl.multiple_of(b * NB, NB)

        def conv_first(n, emit):
            for l0 in range(0, n, STEP):
                x = [net_ref[l0 + t : l0 + t + STEP, pl.ds(c0, NB), :].reshape(STEP * NB, 128) for t in range(3)]
                acc = jnp.dot(jnp.concatenate(x, axis=1), w1s_ref[...], preferred_element_type=F32)
                emit(l0, STEP, silu(acc).reshape(STEP, NB, ch))

        def conv(src, layer, n, emit):
            step = min(n, 2 * STEP)
            while n % step or step % 2:
                step -= 1
            pairs = step // 2
            for l0 in range(0, n, step):
                x = src[l0 : l0 + step + 2].reshape(pairs + 1, 2, NB, ch)
                even, odd = x[:, 0], x[:, 1]
                d0, d1, d2, d3 = even[:-1], odd[:-1], even[1:], odd[1:]
                m = [jnp.dot(d.reshape(pairs * NB, ch), w_ref[4 * layer + i], preferred_element_type=F32)
                     for i, d in enumerate((d0 - d2, d1 + d2, d2 - d1, d1 - d3))]
                y = [silu(m[0] + (m[1] + m[2])), silu((m[1] - m[2]) - m[3])]
                y = jnp.concatenate([v.reshape(pairs, 1, NB, ch) for v in y], axis=1)
                emit(l0, step, y.reshape(step, NB, ch))

        def emit_first(l0, step, y):
            first_ref[l0 + 1 : l0 + 1 + step] = y

        def emit_second(l0, step, y):
            second_ref[l0 : l0 + step] = y
            pool2_ref[l0 // 2 + 1 : l0 // 2 + 1 + step // 2] = halve(y)

        def emit_third(l0, step, y):
            third_ref[l0 : l0 + step] = y
            pool3_ref[l0 // 2 + 1 : l0 // 2 + 1 + step // 2] = halve(y)

        def emit_deepest(l0, step, y):
            fine = third_ref[2 * l0 : 2 * (l0 + step)]
            join3_ref[2 * l0 + 1 : 2 * (l0 + step) + 1] = widen(y, fine)

        def emit_upper(l0, step, y):
            fine = second_ref[2 * l0 : 2 * (l0 + step)]
            join2_ref[2 * l0 + 1 : 2 * (l0 + step) + 1] = widen(y, fine)

        def emit_top(l0, step, y):
            top_ref[l0 : l0 + step] = y

        conv_first(levels, emit_first)
        conv(first_ref, 0, levels, emit_second)
        conv(pool2_ref, 1, half2, emit_third)
        conv(pool3_ref, 2, half3, emit_deepest)
        conv(join3_ref, 3, half2, emit_upper)
        conv(join2_ref, 4, levels, emit_top)

        group = 384
        for i in range(0, levels * NB, group):
            x = top_ref[i // NB : (i + group) // NB].reshape(group, ch)
            p_ref[:, i + 128 : i + group + 128] = lax.dot_general(w24, x, flip, preferred_element_type=F32)
        n = levels * NB
        out = p_ref[0:8, 128 - NB : n + 128 - NB] + p_ref[8:16, 128 : n + 128] + p_ref[16:24, 128 + NB : n + 128 + NB]
        tiles = []
        for i in range(n // 128):
            tile = out[:, i * 128 : (i + 1) * 128]
            tiles.append(jnp.concatenate([tile] * (128 // NB), axis=0) * mask)
        flat = jnp.concatenate(tiles, axis=0).astype(BF16)
        to = to_ref[pl.ds(c0, NB), :]
        place = []
        for h in range(2):
            lane = jnp.concatenate([to + jnp.where(to >= 0, h * quota, 0)] * (128 // NB), axis=0)
            hits = [jnp.where(lane == iota((128, 128), 1) + i * 128, 1.0, 0.0) for i in range(2 * columns // 128)]
            place.append(jnp.concatenate(hits, axis=1).astype(BF16))
        both = jnp.concatenate([flat[: rows // 2], flat[rows // 2 :]], axis=1)
        acc_ref[...] += jnp.dot(both, jnp.concatenate(place, axis=0), preferred_element_type=F32).astype(BF16)

    for d, ref in enumerate((r0_ref, r1_ref, r2_ref, r3_ref)):
        ref[...] = acc_ref[:, d * 2 * quota : (d + 1) * 2 * quota]


def per_device(state, kappa, edge_nbrs, stencil, owner, w_first, w_inner, w_last):
    fields, levels, columns = state.shape
    rows = fields * levels
    ch = w_inner.shape[2]
    devices = lax.axis_size(AXES)
    device = lax.axis_index(AXES)
    total = columns // 16 * devices
    dev = device.astype(jnp.int32).reshape(1)
    table, holder = node_tables(columns)
    f32 = functools.partial(jax.ShapeDtypeStruct, dtype=F32)
    bf16 = functools.partial(jax.ShapeDtypeStruct, dtype=BF16)
    i32 = functools.partial(jax.ShapeDtypeStruct, dtype=jnp.int32)

    payload = pl.pallas_call(
        pack_kernel,
        out_shape=bf16((rows + 16, columns)),
        in_specs=[SMEM] + [VMEM] * 3,
        out_specs=VMEM,
        name="pack",
    )(dev, state, stencil.T, owner.reshape(1, columns))
    def trade(x, d):
        return lax.ppermute(x, AXES, [(i, i ^ d) for i in range(devices)])

    member1 = trade(payload, 1)
    member2 = trade(payload, 2)

    base, edges, facing = pl.pallas_call(
        functools.partial(edges_kernel, total),
        out_shape=(f32((rows, columns)), bf16((rows, columns // 2)), i32((1, columns))),
        in_specs=[SMEM] + [VMEM] * 7,
        out_specs=(VMEM, VMEM, VMEM),
        cost_estimate=pl.CostEstimate(flops=3 * 10**9, bytes_accessed=2**21, transcendentals=0),
        name="edges",
    )(dev, state, kappa.reshape(1, columns), jnp.asarray(diffusion_matrix(columns)),
      jnp.asarray(edge_matrix(columns)), edge_nbrs.T, jnp.asarray(table), jnp.asarray(holder))

    member2, base = lax.optimization_barrier((member2, base))
    member3 = trade(member2, 1)
    low = lax.ppermute(edges, AXES, [(i, (i + 1) % devices) for i in range(devices)])
    high = lax.ppermute(edges, AXES, [(i, (i - 1) % devices) for i in range(devices)])

    bf = lambda *shape: pltpu.VMEM(shape, BF16)
    lanes = 2 * columns // GROUP
    *results, code = pl.pallas_call(
        functools.partial(net_kernel, levels, fields),
        out_shape=[bf16((rows // 2, lanes))] * GROUP + [i32((1, columns))],
        in_specs=[SMEM] + [VMEM] * (GROUP + 1) + [VMEM] * 2,
        out_specs=[VMEM] * (GROUP + 1),
        scratch_shapes=[
            bf(GROUP * columns, 9 * 128),
            bf(levels, 80, 128),
            bf(levels + 2, columns, 128),
            bf(3 * 128, ch),
            bf(4 * w_inner.shape[0], ch, ch),
            bf(levels + 2, NB, ch),
            bf(levels, NB, ch),
            bf(levels // 2 + 2, NB, ch),
            bf(levels // 2, NB, ch),
            bf(levels // 4 + 2, NB, ch),
            bf(levels // 2 + 2, NB, ch),
            bf(levels + 2, NB, ch),
            bf(levels, NB, ch),
            pltpu.VMEM((24, levels * NB + 256), F32),
            bf(rows // 2, GROUP * lanes),
            pltpu.VMEM((columns, 128), jnp.int32),
        ],
        compiler_params=pltpu.CompilerParams(vmem_limit_bytes=30 * 1024 * 1024),
        cost_estimate=pl.CostEstimate(flops=10**10, bytes_accessed=2**22, transcendentals=10**7),
        name="network",
    )(dev, payload, member1, member2, member3, w_first, w_inner, w_last.T)
    back = [trade(results[d], d) for d in (3, 2, 1)][::-1]

    middle = pl.pallas_call(
        middle_kernel,
        out_shape=f32((rows, columns)),
        in_specs=[VMEM] * 4,
        out_specs=VMEM,
        cost_estimate=pl.CostEstimate(flops=10**9, bytes_accessed=2**22, transcendentals=0),
        compiler_params=SMALL,
        name="middle",
    )(*lax.optimization_barrier((base, low, high, facing, results[0]))[:4])

    return pl.pallas_call(
        final_kernel,
        out_shape=f32((fields, levels, columns)),
        in_specs=[VMEM] * 6,
        out_specs=VMEM,
        compiler_params=SMALL,
        name="combine",
    )(middle.reshape(fields, levels, columns), code, results[0], *back)


def solution(mesh):
    in_specs = (
        P(None, None, AXES),
        P(AXES),
        P(AXES, None),
        P(AXES, None),
        P(AXES),
        P(),
        P(),
        P(),
    )
    return jax.shard_map(
        per_device, mesh=mesh, in_specs=in_specs, out_specs=P(None, None, AXES), check_vma=False
    )
```

```python
import functools
import math

import jax
import jax.numpy as jnp
import numpy as np
from jax import lax
from jax.experimental import pallas as pl
from jax.experimental.pallas import tpu as pltpu
from jax.sharding import PartitionSpec as P

AXES = ("grp", "elem")
EDGE_NODES = ((1, 2), (7, 11), (14, 13), (8, 4))
VMEM = pl.BlockSpec(memory_space=pltpu.VMEM)
SMALL = pltpu.CompilerParams(vmem_limit_bytes=12 * 1024 * 1024)
SMEM = pl.BlockSpec(memory_space=pltpu.SMEM)
HIGHEST = lax.Precision.HIGHEST
BF16 = jnp.bfloat16
F32 = jnp.float32
NB = 32
STEP = 6
GROUP = 4


def second_derivative():
    points = np.array([-1.0, -math.sqrt(0.2), math.sqrt(0.2), 1.0])
    factors = np.array(
        [1.0 / np.prod([points[j] - points[m] for m in range(4) if m != j]) for j in range(4)]
    )
    deriv = np.zeros((4, 4))
    for i in range(4):
        for j in range(4):
            if i != j:
                deriv[i, j] = factors[j] / factors[i] / (points[i] - points[j])
        deriv[i, i] = -np.sum(deriv[i])
    return deriv @ deriv


def diffusion_matrix(columns):
    lap = second_derivative()
    eye = np.eye(4)
    node = np.einsum("ia,jb->abij", lap, eye) + np.einsum("ia,jb->abij", eye, lap)
    return np.kron(np.eye(columns // 16), node.reshape(16, 16)).astype(np.float32)


def edge_matrix(columns):
    sel = np.zeros((columns, columns // 2), np.float32)
    for e in range(columns // 16):
        for k in range(4):
            for m in range(2):
                sel[16 * e + EDGE_NODES[k][m], 8 * e + 2 * k + m] = 1
    return sel


def node_tables(columns):
    on_edge = np.zeros((4, columns), np.float32)
    offset = np.zeros((1, columns), np.float32)
    for k in range(4):
        for m in range(2):
            on_edge[k, EDGE_NODES[k][m] :: 16] = 1
            offset[0, EDGE_NODES[k][m] :: 16] = (k + 2) % 4 * 2 + 1 - m
    holder = np.kron(np.eye(columns // 16), np.ones((1, 16))).astype(np.float32)
    table = np.concatenate([on_edge, offset, np.zeros((3, columns), np.float32)], axis=0)
    return table, holder


def iota(shape, dim):
    return lax.broadcasted_iota(jnp.int32, shape, dim)


def silu(half):
    half = half.astype(BF16)
    return half + half * jnp.tanh(half)


def pack_kernel(dev_ref, state_ref, sten_ref, owner_ref, pay_ref):
    fields, levels, columns = state_ref.shape
    rows = fields * levels
    for l in range(0, levels, 2):
        pair = jnp.concatenate([state_ref[:, l, :], state_ref[:, l + 1, :]], axis=0)
        pay_ref[l * fields : (l + 2) * fields, :] = pair.astype(BF16)
    local = (sten_ref[...] - dev_ref[0] * columns).astype(F32)
    flag = jnp.where(owner_ref[...] >= 0, 1.0, 0.0)
    tail = jnp.concatenate([local, flag, jnp.zeros((6, columns), F32)], axis=0)
    pay_ref[rows : rows + 16, :] = tail.astype(BF16)


def edges_kernel(total, dev_ref, state_ref, kappa_ref, op_ref, sel_ref, nbr_ref, table_ref, holder_ref,
                 base_ref, edge_ref, facing_ref):
    fields, levels, columns = state_ref.shape
    elements = columns // 16
    flat = state_ref[...].reshape(fields * levels, columns)
    dyn = kappa_ref[...] * jnp.dot(flat, op_ref[...], precision=HIGHEST)
    edge = jnp.dot(dyn, sel_ref[...], precision=HIGHEST)
    edge_ref[...] = edge.astype(BF16)
    rel = lax.rem(nbr_ref[...] - (dev_ref[0] - 1) * elements + total, total).astype(F32)
    spread = jnp.dot(rel, holder_ref[...], precision=HIGHEST)
    on_edge = table_ref[0:4, :]
    is_edge = jnp.sum(on_edge, axis=0, keepdims=True)
    facing = 8.0 * jnp.sum(spread * on_edge, axis=0, keepdims=True) + table_ref[4:5, :]
    facing = jnp.where(is_edge > 0, facing, -1.0).astype(jnp.int32)
    facing_ref[...] = facing
    half = columns // 2
    pick = jnp.where(iota((half, columns), 0) + half == facing, 0.5, 0.0)
    own = jnp.dot(edge, pick, precision=HIGHEST)
    base_ref[...] = flat + (1.0 - 0.5 * is_edge) * dyn + own


def land(code, d, quota, columns):
    slot = jnp.where((code >= d * quota) & (code < (d + 1) * quota), code - d * quota, -2 * quota)
    spot = iota((2 * quota, columns), 0)
    return [jnp.where(spot == slot + h * quota, 1.0, 0.0).astype(BF16) for h in range(2)]


def middle_kernel(base_ref, low_ref, high_ref, facing_ref, out_ref):
    rows, columns = base_ref.shape
    half = columns // 2
    facing = facing_ref[...]
    acc = base_ref[...]
    for part, ref in ((0, low_ref), (2, high_ref)):
        pick = jnp.where(iota((half, columns), 0) + part * half == facing, 0.5, 0.0).astype(BF16)
        acc = acc + jnp.dot(ref[...], pick, preferred_element_type=F32)
    out_ref[...] = acc


def final_kernel(base_ref, code_ref, r0_ref, r1_ref, r2_ref, r3_ref, out_ref):
    fields, levels, columns = out_ref.shape
    quota = columns // GROUP
    code = code_ref[...]
    got = jnp.concatenate([r0_ref[...], r1_ref[...], r2_ref[...], r3_ref[...]], axis=1)
    puts = [land(code, d, quota, columns) for d in range(GROUP)]
    for h in range(2):
        put = jnp.concatenate([p[h] for p in puts], axis=0)
        physics = jnp.dot(got, put, preferred_element_type=F32)
        for i in range(levels // 2):
            l = h * (levels // 2) + i
            out_ref[:, l, :] = base_ref[:, l, :] + physics[i * fields : (i + 1) * fields, :]


def halve(y):
    y = y.reshape(y.shape[0] // 2, 2, *y.shape[1:])
    return (y[:, 0] + y[:, 1]) * BF16(0.5)


def widen(coarse, fine):
    step, cols, ch = coarse.shape
    return jnp.broadcast_to(coarse[:, None], (step, 2, cols, ch)).reshape(2 * step, cols, ch) + fine


def net_kernel(levels, fields, dev_ref, m0_ref, m1_ref, m2_ref, m3_ref, w1_ref, wi_ref, wl_ref,
               r0_ref, r1_ref, r2_ref, r3_ref, code_ref,
               oh_ref, g_ref, net_ref, w1s_ref, w_ref, first_ref, second_ref, pool2_ref, third_ref,
               pool3_ref, join3_ref, join2_ref, top_ref, p_ref, acc_ref, to_ref):
    rows = fields * levels
    columns = m0_ref.shape[1]
    quota = columns // GROUP
    wide = GROUP * columns
    ch = wi_ref.shape[2]
    taps = 9 * fields
    half2, half3 = levels // 2, levels // 4

    for ref, n in ((first_ref, levels), (pool2_ref, half2), (pool3_ref, half3), (join3_ref, half2),
                   (join2_ref, levels)):
        zero = jnp.zeros(ref.shape[1:], BF16)
        ref[0] = zero
        ref[n + 1] = zero
    net_ref[0] = jnp.zeros(net_ref.shape[1:], BF16)
    net_ref[levels + 1] = jnp.zeros(net_ref.shape[1:], BF16)
    net_ref[:, :, 80:128] = jnp.zeros((levels + 2, columns, 48), BF16)
    p_ref[:, 0:128] = jnp.zeros((24, 128), F32)
    p_ref[:, levels * NB + 128 :] = jnp.zeros((24, 128), F32)
    acc_ref[...] = jnp.zeros(acc_ref.shape, BF16)
    w1s_ref[...] = jnp.zeros(w1s_ref.shape, BF16)
    for t in range(3):
        w1s_ref[128 * t : 128 * t + taps, :] = w1_ref[taps * t : taps * (t + 1), :] * BF16(0.5)
    for i in range(wi_ref.shape[0]):
        g = [wi_ref[i, ch * t : ch * (t + 1), :] for t in range(3)]
        sides, middle = (g[0] + g[2]) * BF16(0.25), g[1] * BF16(0.25)
        w_ref[4 * i] = g[0] * BF16(0.5)
        w_ref[4 * i + 1] = sides + middle
        w_ref[4 * i + 2] = sides - middle
        w_ref[4 * i + 3] = g[2] * BF16(0.5)
    w24 = jnp.concatenate([wl_ref[:, ch * t : ch * (t + 1)].astype(F32) for t in range(3)], axis=0).astype(BF16)

    me = lax.rem(dev_ref[0], GROUP)
    members = (m0_ref, m1_ref, m2_ref, m3_ref)
    upto = jnp.where(iota((columns, columns), 0) < iota((columns, columns), 1), 1.0, 0.0).astype(BF16)
    metas = [ref[rows : rows + 16, :] for ref in members]
    flags = [meta.astype(F32)[9:10, :] for meta in metas]
    counts = [jnp.sum(flag, axis=1, keepdims=True) for flag in flags]
    ranks, targets, active = [], [], jnp.zeros((1, 1), F32)
    for d in range(GROUP):
        start = jnp.zeros((1, 1), F32)
        for other in range(GROUP):
            start = start + jnp.where((me ^ other) < (me ^ d), counts[other], 0.0)
        local = jnp.dot(metas[d], upto, preferred_element_type=F32)[9:10, :].astype(jnp.int32)
        rank = local + start.astype(jnp.int32)
        ranks.append(jnp.where(flags[d] > 0, rank, -1))
        targets.append(jnp.where(flags[d] > 0, d * quota + local // GROUP + 1, 0).astype(F32))
        if d == 0:
            code_ref[...] = jnp.where(flags[d] > 0, (lax.rem(rank, GROUP) ^ me) * quota + local // GROUP, -1)
        active = active + counts[d]
    meta = jnp.concatenate(metas, axis=1)
    rank = jnp.concatenate(ranks, axis=1)
    share = (jnp.sum(active).astype(jnp.int32) - me + GROUP - 1) // GROUP
    slot = GROUP * iota((columns, wide), 0) + me
    choose = jnp.where(slot == rank, 1.0, 0.0).astype(BF16)
    flip = (((1,), (1,)), ((), ()))
    sten = lax.dot_general(meta, choose, flip, preferred_element_type=F32)
    part = (iota((16, wide), 1) // columns).astype(F32).astype(BF16)
    part = lax.dot_general(part, choose, flip, preferred_element_type=F32)
    sten = (sten + columns * part).astype(jnp.int32)
    target = jnp.broadcast_to(jnp.concatenate(targets, axis=1), (128, wide)).astype(BF16)
    to = lax.dot_general(choose, target, flip, preferred_element_type=F32).astype(jnp.int32) - 1
    to_ref[...] = jnp.where(to >= 0, to // quota * (2 * quota) + lax.rem(to, quota), -1)

    @pl.loop(0, (share + 127) // 128)
    def _(q):
        lanes = pl.ds(pl.multiple_of(q * 128, 128), 128)
        for k in range(9):
            for half in range(columns // 128):
                here = sten[k : k + 1, half * 128 : (half + 1) * 128]
                picked = here if half == 0 else jnp.where(q == half, here, picked)
            oh_ref[:, k * 128 : (k + 1) * 128] = jnp.where(iota((wide, 128), 0) == picked, 1.0, 0.0).astype(BF16)
        for k in range(0, 9, 2):
            n = 2 if k < 8 else 1
            got = jnp.dot(jnp.concatenate([ref[0:rows, :] for ref in members], axis=1), oh_ref[:, k * 128 : (k + n) * 128], preferred_element_type=F32)
            parts = [got[:, u * 128 : (u + 1) * 128].reshape(levels, fields, 128) for u in range(n)]
            if n == 1:
                parts.append(jnp.zeros_like(parts[0]))
            g_ref[0:levels, k * 8 : k * 8 + 16, :] = jnp.concatenate(parts, axis=1).astype(BF16)

        for l in range(levels):
            net_ref[l + 1, lanes, 0:80] = g_ref[l].T

    mask = jnp.where(iota((128 // NB * 8, 128), 0) // 8 == iota((128 // NB * 8, 128), 1) // NB, 1.0, 0.0)

    @pl.loop(0, (share + NB - 1) // NB)
    def _(b):
        c0 = pl.multiple_of(b * NB, NB)

        def conv_first(n, emit):
            for l0 in range(0, n, STEP):
                x = [net_ref[l0 + t : l0 + t + STEP, pl.ds(c0, NB), :].reshape(STEP * NB, 128) for t in range(3)]
                acc = jnp.dot(jnp.concatenate(x, axis=1), w1s_ref[...], preferred_element_type=F32)
                emit(l0, STEP, silu(acc).reshape(STEP, NB, ch))

        def conv(src, layer, n, emit):
            step = n if n < 4 * STEP else 2 * STEP
            while n % step or step % 2:
                step -= 1
            pairs = step // 2
            for l0 in range(0, n, step):
                x = src[l0 : l0 + step + 2].reshape(pairs + 1, 2, NB, ch)
                even, odd = x[:, 0], x[:, 1]
                d0, d1, d2, d3 = even[:-1], odd[:-1], even[1:], odd[1:]
                m = [jnp.dot(d.reshape(pairs * NB, ch), w_ref[4 * layer + i], preferred_element_type=F32)
                     for i, d in enumerate((d0 - d2, d1 + d2, d2 - d1, d1 - d3))]
                y = [silu(m[0] + (m[1] + m[2])), silu((m[1] - m[2]) - m[3])]
                y = jnp.concatenate([v.reshape(pairs, 1, NB, ch) for v in y], axis=1)
                emit(l0, step, y.reshape(step, NB, ch))

        def emit_first(l0, step, y):
            first_ref[l0 + 1 : l0 + 1 + step] = y

        def emit_second(l0, step, y):
            second_ref[l0 : l0 + step] = y
            pool2_ref[l0 // 2 + 1 : l0 // 2 + 1 + step // 2] = halve(y)

        def emit_third(l0, step, y):
            third_ref[l0 : l0 + step] = y
            pool3_ref[l0 // 2 + 1 : l0 // 2 + 1 + step // 2] = halve(y)

        def emit_deepest(l0, step, y):
            fine = third_ref[2 * l0 : 2 * (l0 + step)]
            join3_ref[2 * l0 + 1 : 2 * (l0 + step) + 1] = widen(y, fine)

        def emit_upper(l0, step, y):
            fine = second_ref[2 * l0 : 2 * (l0 + step)]
            join2_ref[2 * l0 + 1 : 2 * (l0 + step) + 1] = widen(y, fine)

        def emit_top(l0, step, y):
            top_ref[l0 : l0 + step] = y

        conv_first(levels, emit_first)
        conv(first_ref, 0, levels, emit_second)
        conv(pool2_ref, 1, half2, emit_third)
        conv(pool3_ref, 2, half3, emit_deepest)
        conv(join3_ref, 3, half2, emit_upper)
        conv(join2_ref, 4, levels, emit_top)

        group = 384
        for i in range(0, levels * NB, group):
            x = top_ref[i // NB : (i + group) // NB].reshape(group, ch)
            p_ref[:, i + 128 : i + group + 128] = lax.dot_general(w24, x, flip, preferred_element_type=F32)
        n = levels * NB
        out = p_ref[0:8, 128 - NB : n + 128 - NB] + p_ref[8:16, 128 : n + 128] + p_ref[16:24, 128 + NB : n + 128 + NB]
        tiles = []
        for i in range(n // 128):
            tile = out[:, i * 128 : (i + 1) * 128]
            tiles.append(jnp.concatenate([tile] * (128 // NB), axis=0) * mask)
        flat = jnp.concatenate(tiles, axis=0).astype(BF16)
        to = to_ref[pl.ds(c0, NB), :]
        place = []
        for h in range(2):
            lane = jnp.concatenate([to + jnp.where(to >= 0, h * quota, 0)] * (128 // NB), axis=0)
            hits = [jnp.where(lane == iota((128, 128), 1) + i * 128, 1.0, 0.0) for i in range(2 * columns // 128)]
            place.append(jnp.concatenate(hits, axis=1).astype(BF16))
        both = jnp.concatenate([flat[: rows // 2], flat[rows // 2 :]], axis=1)
        acc_ref[...] += jnp.dot(both, jnp.concatenate(place, axis=0), preferred_element_type=F32).astype(BF16)

    for d, ref in enumerate((r0_ref, r1_ref, r2_ref, r3_ref)):
        ref[...] = acc_ref[:, d * 2 * quota : (d + 1) * 2 * quota]


def per_device(state, kappa, edge_nbrs, stencil, owner, w_first, w_inner, w_last):
    fields, levels, columns = state.shape
    rows = fields * levels
    ch = w_inner.shape[2]
    devices = lax.axis_size(AXES)
    device = lax.axis_index(AXES)
    total = columns // 16 * devices
    dev = device.astype(jnp.int32).reshape(1)
    table, holder = node_tables(columns)
    f32 = functools.partial(jax.ShapeDtypeStruct, dtype=F32)
    bf16 = functools.partial(jax.ShapeDtypeStruct, dtype=BF16)
    i32 = functools.partial(jax.ShapeDtypeStruct, dtype=jnp.int32)

    payload = pl.pallas_call(
        pack_kernel,
        out_shape=bf16((rows + 16, columns)),
        in_specs=[SMEM] + [VMEM] * 3,
        out_specs=VMEM,
        name="pack",
    )(dev, state, stencil.T, owner.reshape(1, columns))
    def trade(x, d):
        return lax.ppermute(x, AXES, [(i, i ^ d) for i in range(devices)])

    member1 = trade(payload, 1)
    member2 = trade(payload, 2)

    base, edges, facing = pl.pallas_call(
        functools.partial(edges_kernel, total),
        out_shape=(f32((rows, columns)), bf16((rows, columns // 2)), i32((1, columns))),
        in_specs=[SMEM] + [VMEM] * 7,
        out_specs=(VMEM, VMEM, VMEM),
        cost_estimate=pl.CostEstimate(flops=3 * 10**9, bytes_accessed=2**21, transcendentals=0),
        name="edges",
    )(dev, state, kappa.reshape(1, columns), jnp.asarray(diffusion_matrix(columns)),
      jnp.asarray(edge_matrix(columns)), edge_nbrs.T, jnp.asarray(table), jnp.asarray(holder))

    member2, base = lax.optimization_barrier((member2, base))
    member3 = trade(member2, 1)
    low = lax.ppermute(edges, AXES, [(i, (i + 1) % devices) for i in range(devices)])
    high = lax.ppermute(edges, AXES, [(i, (i - 1) % devices) for i in range(devices)])

    bf = lambda *shape: pltpu.VMEM(shape, BF16)
    lanes = 2 * columns // GROUP
    *results, code = pl.pallas_call(
        functools.partial(net_kernel, levels, fields),
        out_shape=[bf16((rows // 2, lanes))] * GROUP + [i32((1, columns))],
        in_specs=[SMEM] + [VMEM] * (GROUP + 1) + [VMEM] * 2,
        out_specs=[VMEM] * (GROUP + 1),
        scratch_shapes=[
            bf(GROUP * columns, 9 * 128),
            bf(levels, 80, 128),
            bf(levels + 2, columns, 128),
            bf(3 * 128, ch),
            bf(4 * w_inner.shape[0], ch, ch),
            bf(levels + 2, NB, ch),
            bf(levels, NB, ch),
            bf(levels // 2 + 2, NB, ch),
            bf(levels // 2, NB, ch),
            bf(levels // 4 + 2, NB, ch),
            bf(levels // 2 + 2, NB, ch),
            bf(levels + 2, NB, ch),
            bf(levels, NB, ch),
            pltpu.VMEM((24, levels * NB + 256), F32),
            bf(rows // 2, GROUP * lanes),
            pltpu.VMEM((columns, 128), jnp.int32),
        ],
        compiler_params=pltpu.CompilerParams(vmem_limit_bytes=30 * 1024 * 1024),
        cost_estimate=pl.CostEstimate(flops=10**10, bytes_accessed=2**22, transcendentals=10**7),
        name="network",
    )(dev, payload, member1, member2, member3, w_first, w_inner, w_last.T)
    back = [trade(results[d], d) for d in (3, 2, 1)][::-1]

    middle = pl.pallas_call(
        middle_kernel,
        out_shape=f32((rows, columns)),
        in_specs=[VMEM] * 4,
        out_specs=VMEM,
        cost_estimate=pl.CostEstimate(flops=10**9, bytes_accessed=2**22, transcendentals=0),
        compiler_params=SMALL,
        name="middle",
    )(*lax.optimization_barrier((base, low, high, facing, results[0]))[:4])

    return pl.pallas_call(
        final_kernel,
        out_shape=f32((fields, levels, columns)),
        in_specs=[VMEM] * 6,
        out_specs=VMEM,
        compiler_params=SMALL,
        name="combine",
    )(middle.reshape(fields, levels, columns), code, results[0], *back)


def solution(mesh):
    in_specs = (
        P(None, None, AXES),
        P(AXES),
        P(AXES, None),
        P(AXES, None),
        P(AXES),
        P(),
        P(),
        P(),
    )
    return jax.shard_map(
        per_device, mesh=mesh, in_specs=in_specs, out_specs=P(None, None, AXES), check_vma=False
    )
```

```python
import functools
import math

import jax
import jax.numpy as jnp
import numpy as np
from jax import lax
from jax.experimental import pallas as pl
from jax.experimental.pallas import tpu as pltpu
from jax.sharding import PartitionSpec as P

AXES = ("grp", "elem")
EDGE_NODES = ((1, 2), (7, 11), (14, 13), (8, 4))
VMEM = pl.BlockSpec(memory_space=pltpu.VMEM)
SMALL = pltpu.CompilerParams(vmem_limit_bytes=12 * 1024 * 1024)
SMEM = pl.BlockSpec(memory_space=pltpu.SMEM)
HIGHEST = lax.Precision.HIGHEST
BF16 = jnp.bfloat16
F32 = jnp.float32
NB = 32
STEP = 6
GROUP = 4


def second_derivative():
    points = np.array([-1.0, -math.sqrt(0.2), math.sqrt(0.2), 1.0])
    factors = np.array(
        [1.0 / np.prod([points[j] - points[m] for m in range(4) if m != j]) for j in range(4)]
    )
    deriv = np.zeros((4, 4))
    for i in range(4):
        for j in range(4):
            if i != j:
                deriv[i, j] = factors[j] / factors[i] / (points[i] - points[j])
        deriv[i, i] = -np.sum(deriv[i])
    return deriv @ deriv


def diffusion_matrix(columns):
    lap = second_derivative()
    eye = np.eye(4)
    node = np.einsum("ia,jb->abij", lap, eye) + np.einsum("ia,jb->abij", eye, lap)
    return np.kron(np.eye(columns // 16), node.reshape(16, 16)).astype(np.float32)


def edge_matrix(columns):
    sel = np.zeros((columns, columns // 2), np.float32)
    for e in range(columns // 16):
        for k in range(4):
            for m in range(2):
                sel[16 * e + EDGE_NODES[k][m], 8 * e + 2 * k + m] = 1
    return sel


def node_tables(columns):
    on_edge = np.zeros((4, columns), np.float32)
    offset = np.zeros((1, columns), np.float32)
    for k in range(4):
        for m in range(2):
            on_edge[k, EDGE_NODES[k][m] :: 16] = 1
            offset[0, EDGE_NODES[k][m] :: 16] = (k + 2) % 4 * 2 + 1 - m
    holder = np.kron(np.eye(columns // 16), np.ones((1, 16))).astype(np.float32)
    table = np.concatenate([on_edge, offset, np.zeros((3, columns), np.float32)], axis=0)
    return table, holder


def iota(shape, dim):
    return lax.broadcasted_iota(jnp.int32, shape, dim)


def silu(half):
    half = half.astype(BF16)
    return half + half * jnp.tanh(half)


def pack_kernel(dev_ref, state_ref, sten_ref, owner_ref, pay_ref):
    fields, levels, columns = state_ref.shape
    rows = fields * levels
    for l in range(0, levels, 2):
        pair = jnp.concatenate([state_ref[:, l, :], state_ref[:, l + 1, :]], axis=0)
        pay_ref[l * fields : (l + 2) * fields, :] = pair.astype(BF16)
    local = (sten_ref[...] - dev_ref[0] * columns).astype(F32)
    flag = jnp.where(owner_ref[...] >= 0, 1.0, 0.0)
    tail = jnp.concatenate([local, flag, jnp.zeros((6, columns), F32)], axis=0)
    pay_ref[rows : rows + 16, :] = tail.astype(BF16)


def edges_kernel(total, dev_ref, state_ref, kappa_ref, op_ref, sel_ref, nbr_ref, table_ref, holder_ref,
                 base_ref, edge_ref, facing_ref):
    fields, levels, columns = state_ref.shape
    elements = columns // 16
    flat = state_ref[...].reshape(fields * levels, columns)
    dyn = kappa_ref[...] * jnp.dot(flat, op_ref[...], precision=HIGHEST)
    edge = jnp.dot(dyn, sel_ref[...], precision=HIGHEST)
    edge_ref[...] = edge.astype(BF16)
    rel = lax.rem(nbr_ref[...] - (dev_ref[0] - 1) * elements + total, total).astype(F32)
    spread = jnp.dot(rel, holder_ref[...], precision=HIGHEST)
    on_edge = table_ref[0:4, :]
    is_edge = jnp.sum(on_edge, axis=0, keepdims=True)
    facing = 8.0 * jnp.sum(spread * on_edge, axis=0, keepdims=True) + table_ref[4:5, :]
    facing = jnp.where(is_edge > 0, facing, -1.0).astype(jnp.int32)
    facing_ref[...] = facing
    half = columns // 2
    pick = jnp.where(iota((half, columns), 0) + half == facing, 0.5, 0.0)
    own = jnp.dot(edge, pick, precision=HIGHEST)
    base_ref[...] = flat + (1.0 - 0.5 * is_edge) * dyn + own


def land(code, d, quota, columns):
    slot = jnp.where((code >= d * quota) & (code < (d + 1) * quota), code - d * quota, -2 * quota)
    spot = iota((2 * quota, columns), 0)
    return [jnp.where(spot == slot + h * quota, 1.0, 0.0).astype(BF16) for h in range(2)]


def middle_kernel(base_ref, low_ref, high_ref, facing_ref, out_ref):
    rows, columns = base_ref.shape
    half = columns // 2
    facing = facing_ref[...]
    acc = base_ref[...]
    for part, ref in ((0, low_ref), (2, high_ref)):
        pick = jnp.where(iota((half, columns), 0) + part * half == facing, 0.5, 0.0).astype(BF16)
        acc = acc + jnp.dot(ref[...], pick, preferred_element_type=F32)
    out_ref[...] = acc


def final_kernel(base_ref, code_ref, r0_ref, r1_ref, r2_ref, r3_ref, out_ref):
    fields, levels, columns = out_ref.shape
    quota = columns // GROUP
    code = code_ref[...]
    got = jnp.concatenate([r0_ref[...], r1_ref[...], r2_ref[...], r3_ref[...]], axis=1)
    puts = [land(code, d, quota, columns) for d in range(GROUP)]
    for h in range(2):
        put = jnp.concatenate([p[h] for p in puts], axis=0)
        physics = jnp.dot(got, put, preferred_element_type=F32)
        for i in range(levels // 2):
            l = h * (levels // 2) + i
            out_ref[:, l, :] = base_ref[:, l, :] + physics[i * fields : (i + 1) * fields, :]


def halve(y):
    y = y.reshape(y.shape[0] // 2, 2, *y.shape[1:])
    return (y[:, 0] + y[:, 1]) * BF16(0.5)


def widen(coarse, fine):
    step, cols, ch = coarse.shape
    return jnp.broadcast_to(coarse[:, None], (step, 2, cols, ch)).reshape(2 * step, cols, ch) + fine


def net_kernel(levels, fields, dev_ref, m0_ref, m1_ref, m2_ref, m3_ref, w1_ref, wi_ref, wl_ref,
               r0_ref, r1_ref, r2_ref, r3_ref, code_ref,
               oh_ref, g_ref, net_ref, w1s_ref, w_ref, first_ref, second_ref, pool2_ref, third_ref,
               pool3_ref, join3_ref, join2_ref, top_ref, p_ref, acc_ref, to_ref):
    rows = fields * levels
    columns = m0_ref.shape[1]
    quota = columns // GROUP
    wide = GROUP * columns
    ch = wi_ref.shape[2]
    taps = 9 * fields
    half2, half3 = levels // 2, levels // 4

    for ref, n in ((first_ref, levels), (pool2_ref, half2), (pool3_ref, half3), (join3_ref, half2),
                   (join2_ref, levels)):
        zero = jnp.zeros(ref.shape[1:], BF16)
        ref[0] = zero
        ref[n + 1] = zero
    net_ref[0] = jnp.zeros(net_ref.shape[1:], BF16)
    net_ref[levels + 1] = jnp.zeros(net_ref.shape[1:], BF16)
    p_ref[:, 0:128] = jnp.zeros((24, 128), F32)
    p_ref[:, levels * NB + 128 :] = jnp.zeros((24, 128), F32)
    acc_ref[...] = jnp.zeros(acc_ref.shape, BF16)
    w1s_ref[...] = jnp.zeros(w1s_ref.shape, BF16)
    for t in range(3):
        w1s_ref[128 * t : 128 * t + taps, :] = w1_ref[taps * t : taps * (t + 1), :] * BF16(0.5)
    for i in range(wi_ref.shape[0]):
        g = [wi_ref[i, ch * t : ch * (t + 1), :] for t in range(3)]
        sides, middle = (g[0] + g[2]) * BF16(0.25), g[1] * BF16(0.25)
        w_ref[4 * i] = g[0] * BF16(0.5)
        w_ref[4 * i + 1] = sides + middle
        w_ref[4 * i + 2] = sides - middle
        w_ref[4 * i + 3] = g[2] * BF16(0.5)
    w24 = jnp.concatenate([wl_ref[:, ch * t : ch * (t + 1)].astype(F32) for t in range(3)], axis=0).astype(BF16)

    me = lax.rem(dev_ref[0], GROUP)
    members = (m0_ref, m1_ref, m2_ref, m3_ref)
    upto = jnp.where(iota((columns, columns), 0) < iota((columns, columns), 1), 1.0, 0.0).astype(BF16)
    metas = [ref[rows : rows + 16, :] for ref in members]
    flags = [meta.astype(F32)[9:10, :] for meta in metas]
    counts = [jnp.sum(flag, axis=1, keepdims=True) for flag in flags]
    ranks, targets, active = [], [], jnp.zeros((1, 1), F32)
    for d in range(GROUP):
        start = jnp.zeros((1, 1), F32)
        for other in range(GROUP):
            start = start + jnp.where((me ^ other) < (me ^ d), counts[other], 0.0)
        local = jnp.dot(metas[d], upto, preferred_element_type=F32)[9:10, :].astype(jnp.int32)
        rank = local + start.astype(jnp.int32)
        ranks.append(jnp.where(flags[d] > 0, rank, -1))
        targets.append(jnp.where(flags[d] > 0, d * quota + local // GROUP + 1, 0).astype(F32))
        if d == 0:
            code_ref[...] = jnp.where(flags[d] > 0, (lax.rem(rank, GROUP) ^ me) * quota + local // GROUP, -1)
        active = active + counts[d]
    meta = jnp.concatenate(metas, axis=1)
    rank = jnp.concatenate(ranks, axis=1)
    share = (jnp.sum(active).astype(jnp.int32) - me + GROUP - 1) // GROUP
    slot = GROUP * iota((columns, wide), 0) + me
    choose = jnp.where(slot == rank, 1.0, 0.0).astype(BF16)
    flip = (((1,), (1,)), ((), ()))
    sten = lax.dot_general(meta, choose, flip, preferred_element_type=F32)
    part = (iota((16, wide), 1) // columns).astype(F32).astype(BF16)
    part = lax.dot_general(part, choose, flip, preferred_element_type=F32)
    sten = (sten + columns * part).astype(jnp.int32)
    target = jnp.broadcast_to(jnp.concatenate(targets, axis=1), (128, wide)).astype(BF16)
    to = lax.dot_general(choose, target, flip, preferred_element_type=F32).astype(jnp.int32) - 1
    to_ref[...] = jnp.where(to >= 0, to // quota * (2 * quota) + lax.rem(to, quota), -1)

    @pl.loop(0, (share + 127) // 128)
    def _(q):
        lanes = pl.ds(pl.multiple_of(q * 128, 128), 128)
        for k in range(9):
            for half in range(columns // 128):
                here = sten[k : k + 1, half * 128 : (half + 1) * 128]
                picked = here if half == 0 else jnp.where(q == half, here, picked)
            oh_ref[:, k * 128 : (k + 1) * 128] = jnp.where(iota((wide, 128), 0) == picked, 1.0, 0.0).astype(BF16)
        for k in range(0, 9, 2):
            n = 2 if k < 8 else 1
            got = jnp.dot(jnp.concatenate([ref[0:rows, :] for ref in members], axis=1), oh_ref[:, k * 128 : (k + n) * 128], preferred_element_type=F32)
            parts = [got[:, u * 128 : (u + 1) * 128].reshape(levels, fields, 128) for u in range(n)]
            if n == 1:
                parts.append(jnp.zeros_like(parts[0]))
            g_ref[0:levels, k * 8 : k * 8 + 16, :] = jnp.concatenate(parts, axis=1).astype(BF16)

        for l in range(levels):
            net_ref[l + 1, lanes, :] = jnp.concatenate([g_ref[l].T, jnp.zeros((128, 48), BF16)], axis=1)

    mask = jnp.where(iota((128 // NB * 8, 128), 0) // 8 == iota((128 // NB * 8, 128), 1) // NB, 1.0, 0.0)

    @pl.loop(0, (share + NB - 1) // NB)
    def _(b):
        c0 = pl.multiple_of(b * NB, NB)

        def conv_first(n, emit):
            for l0 in range(0, n, STEP):
                x = [net_ref[l0 + t : l0 + t + STEP, pl.ds(c0, NB), :].reshape(STEP * NB, 128) for t in range(3)]
                acc = jnp.dot(jnp.concatenate(x, axis=1), w1s_ref[...], preferred_element_type=F32)
                emit(l0, STEP, silu(acc).reshape(STEP, NB, ch))

        def conv(src, layer, n, emit):
            step = n if n < 4 * STEP else 2 * STEP
            while n % step or step % 2:
                step -= 1
            pairs = step // 2
            for l0 in range(0, n, step):
                x = src[l0 : l0 + step + 2].reshape(pairs + 1, 2, NB, ch)
                even, odd = x[:, 0], x[:, 1]
                d0, d1, d2, d3 = even[:-1], odd[:-1], even[1:], odd[1:]
                m = [jnp.dot(d.reshape(pairs * NB, ch), w_ref[4 * layer + i], preferred_element_type=F32)
                     for i, d in enumerate((d0 - d2, d1 + d2, d2 - d1, d1 - d3))]
                y = [silu(m[0] + (m[1] + m[2])), silu((m[1] - m[2]) - m[3])]
                y = jnp.concatenate([v.reshape(pairs, 1, NB, ch) for v in y], axis=1)
                emit(l0, step, y.reshape(step, NB, ch))

        def emit_first(l0, step, y):
            first_ref[l0 + 1 : l0 + 1 + step] = y

        def emit_second(l0, step, y):
            second_ref[l0 : l0 + step] = y
            pool2_ref[l0 // 2 + 1 : l0 // 2 + 1 + step // 2] = halve(y)

        def emit_third(l0, step, y):
            third_ref[l0 : l0 + step] = y
            pool3_ref[l0 // 2 + 1 : l0 // 2 + 1 + step // 2] = halve(y)

        def emit_deepest(l0, step, y):
            fine = third_ref[2 * l0 : 2 * (l0 + step)]
            join3_ref[2 * l0 + 1 : 2 * (l0 + step) + 1] = widen(y, fine)

        def emit_upper(l0, step, y):
            fine = second_ref[2 * l0 : 2 * (l0 + step)]
            join2_ref[2 * l0 + 1 : 2 * (l0 + step) + 1] = widen(y, fine)

        def emit_top(l0, step, y):
            top_ref[l0 : l0 + step] = y

        conv_first(levels, emit_first)
        conv(first_ref, 0, levels, emit_second)
        conv(pool2_ref, 1, half2, emit_third)
        conv(pool3_ref, 2, half3, emit_deepest)
        conv(join3_ref, 3, half2, emit_upper)
        conv(join2_ref, 4, levels, emit_top)

        group = 384
        for i in range(0, levels * NB, group):
            x = top_ref[i // NB : (i + group) // NB].reshape(group, ch)
            p_ref[:, i + 128 : i + group + 128] = lax.dot_general(w24, x, flip, preferred_element_type=F32)
        n = levels * NB
        out = p_ref[0:8, 128 - NB : n + 128 - NB] + p_ref[8:16, 128 : n + 128] + p_ref[16:24, 128 + NB : n + 128 + NB]
        tiles = []
        for i in range(n // 128):
            tile = out[:, i * 128 : (i + 1) * 128]
            tiles.append(jnp.concatenate([tile] * (128 // NB), axis=0) * mask)
        flat = jnp.concatenate(tiles, axis=0).astype(BF16)
        to = to_ref[pl.ds(c0, NB), :]
        place = []
        for h in range(2):
            lane = jnp.concatenate([to + jnp.where(to >= 0, h * quota, 0)] * (128 // NB), axis=0)
            hits = [jnp.where(lane == iota((128, 128), 1) + i * 128, 1.0, 0.0) for i in range(2 * columns // 128)]
            place.append(jnp.concatenate(hits, axis=1).astype(BF16))
        both = jnp.concatenate([flat[: rows // 2], flat[rows // 2 :]], axis=1)
        acc_ref[...] += jnp.dot(both, jnp.concatenate(place, axis=0), preferred_element_type=F32).astype(BF16)

    for d, ref in enumerate((r0_ref, r1_ref, r2_ref, r3_ref)):
        ref[...] = acc_ref[:, d * 2 * quota : (d + 1) * 2 * quota]


def per_device(state, kappa, edge_nbrs, stencil, owner, w_first, w_inner, w_last):
    fields, levels, columns = state.shape
    rows = fields * levels
    ch = w_inner.shape[2]
    devices = lax.axis_size(AXES)
    device = lax.axis_index(AXES)
    total = columns // 16 * devices
    dev = device.astype(jnp.int32).reshape(1)
    table, holder = node_tables(columns)
    f32 = functools.partial(jax.ShapeDtypeStruct, dtype=F32)
    bf16 = functools.partial(jax.ShapeDtypeStruct, dtype=BF16)
    i32 = functools.partial(jax.ShapeDtypeStruct, dtype=jnp.int32)

    payload = pl.pallas_call(
        pack_kernel,
        out_shape=bf16((rows + 16, columns)),
        in_specs=[SMEM] + [VMEM] * 3,
        out_specs=VMEM,
        name="pack",
    )(dev, state, stencil.T, owner.reshape(1, columns))
    def trade(x, d):
        return lax.ppermute(x, AXES, [(i, i ^ d) for i in range(devices)])

    member1 = trade(payload, 1)
    member2 = trade(payload, 2)

    base, edges, facing = pl.pallas_call(
        functools.partial(edges_kernel, total),
        out_shape=(f32((rows, columns)), bf16((rows, columns // 2)), i32((1, columns))),
        in_specs=[SMEM] + [VMEM] * 7,
        out_specs=(VMEM, VMEM, VMEM),
        cost_estimate=pl.CostEstimate(flops=3 * 10**9, bytes_accessed=2**21, transcendentals=0),
        name="edges",
    )(dev, state, kappa.reshape(1, columns), jnp.asarray(diffusion_matrix(columns)),
      jnp.asarray(edge_matrix(columns)), edge_nbrs.T, jnp.asarray(table), jnp.asarray(holder))

    member2, base = lax.optimization_barrier((member2, base))
    member3 = trade(member2, 1)
    low = lax.ppermute(edges, AXES, [(i, (i + 1) % devices) for i in range(devices)])
    high = lax.ppermute(edges, AXES, [(i, (i - 1) % devices) for i in range(devices)])

    bf = lambda *shape: pltpu.VMEM(shape, BF16)
    lanes = 2 * columns // GROUP
    *results, code = pl.pallas_call(
        functools.partial(net_kernel, levels, fields),
        out_shape=[bf16((rows // 2, lanes))] * GROUP + [i32((1, columns))],
        in_specs=[SMEM] + [VMEM] * (GROUP + 1) + [VMEM] * 2,
        out_specs=[VMEM] * (GROUP + 1),
        scratch_shapes=[
            bf(GROUP * columns, 9 * 128),
            bf(levels, 80, 128),
            bf(levels + 2, columns, 128),
            bf(3 * 128, ch),
            bf(4 * w_inner.shape[0], ch, ch),
            bf(levels + 2, NB, ch),
            bf(levels, NB, ch),
            bf(levels // 2 + 2, NB, ch),
            bf(levels // 2, NB, ch),
            bf(levels // 4 + 2, NB, ch),
            bf(levels // 2 + 2, NB, ch),
            bf(levels + 2, NB, ch),
            bf(levels, NB, ch),
            pltpu.VMEM((24, levels * NB + 256), F32),
            bf(rows // 2, GROUP * lanes),
            pltpu.VMEM((columns, 128), jnp.int32),
        ],
        compiler_params=pltpu.CompilerParams(vmem_limit_bytes=30 * 1024 * 1024),
        cost_estimate=pl.CostEstimate(flops=10**10, bytes_accessed=2**22, transcendentals=10**7),
        name="network",
    )(dev, payload, member1, member2, member3, w_first, w_inner, w_last.T)
    back = [trade(results[d], d) for d in (3, 2, 1)][::-1]

    middle = pl.pallas_call(
        middle_kernel,
        out_shape=f32((rows, columns)),
        in_specs=[VMEM] * 4,
        out_specs=VMEM,
        cost_estimate=pl.CostEstimate(flops=10**9, bytes_accessed=2**22, transcendentals=0),
        compiler_params=SMALL,
        name="middle",
    )(*lax.optimization_barrier((base, low, high, facing, results[0]))[:4])

    return pl.pallas_call(
        final_kernel,
        out_shape=f32((fields, levels, columns)),
        in_specs=[VMEM] * 6,
        out_specs=VMEM,
        compiler_params=SMALL,
        name="combine",
    )(middle.reshape(fields, levels, columns), code, results[0], *back)


def solution(mesh):
    in_specs = (
        P(None, None, AXES),
        P(AXES),
        P(AXES, None),
        P(AXES, None),
        P(AXES),
        P(),
        P(),
        P(),
    )
    return jax.shard_map(
        per_device, mesh=mesh, in_specs=in_specs, out_specs=P(None, None, AXES), check_vma=False
    )
```

```python
import functools
import math

import jax
import jax.numpy as jnp
import numpy as np
from jax import lax
from jax.experimental import pallas as pl
from jax.experimental.pallas import tpu as pltpu
from jax.sharding import PartitionSpec as P

AXES = ("grp", "elem")
EDGE_NODES = ((1, 2), (7, 11), (14, 13), (8, 4))
VMEM = pl.BlockSpec(memory_space=pltpu.VMEM)
SMALL = pltpu.CompilerParams(vmem_limit_bytes=12 * 1024 * 1024)
SMEM = pl.BlockSpec(memory_space=pltpu.SMEM)
HIGHEST = lax.Precision.HIGHEST
BF16 = jnp.bfloat16
F32 = jnp.float32
NB = 32
STEP = 6
GROUP = 4


def second_derivative():
    points = np.array([-1.0, -math.sqrt(0.2), math.sqrt(0.2), 1.0])
    factors = np.array(
        [1.0 / np.prod([points[j] - points[m] for m in range(4) if m != j]) for j in range(4)]
    )
    deriv = np.zeros((4, 4))
    for i in range(4):
        for j in range(4):
            if i != j:
                deriv[i, j] = factors[j] / factors[i] / (points[i] - points[j])
        deriv[i, i] = -np.sum(deriv[i])
    return deriv @ deriv


def diffusion_matrix(columns):
    lap = second_derivative()
    eye = np.eye(4)
    node = np.einsum("ia,jb->abij", lap, eye) + np.einsum("ia,jb->abij", eye, lap)
    return np.kron(np.eye(columns // 16), node.reshape(16, 16)).astype(np.float32)


def edge_matrix(columns):
    sel = np.zeros((columns, columns // 2), np.float32)
    for e in range(columns // 16):
        for k in range(4):
            for m in range(2):
                sel[16 * e + EDGE_NODES[k][m], 8 * e + 2 * k + m] = 1
    return sel


def node_tables(columns):
    on_edge = np.zeros((4, columns), np.float32)
    offset = np.zeros((1, columns), np.float32)
    for k in range(4):
        for m in range(2):
            on_edge[k, EDGE_NODES[k][m] :: 16] = 1
            offset[0, EDGE_NODES[k][m] :: 16] = (k + 2) % 4 * 2 + 1 - m
    holder = np.kron(np.eye(columns // 16), np.ones((1, 16))).astype(np.float32)
    table = np.concatenate([on_edge, offset, np.zeros((3, columns), np.float32)], axis=0)
    return table, holder


def iota(shape, dim):
    return lax.broadcasted_iota(jnp.int32, shape, dim)


def silu(half):
    half = half.astype(BF16)
    return half + half * jnp.tanh(half)


def pack_kernel(dev_ref, state_ref, sten_ref, owner_ref, pay_ref):
    fields, levels, columns = state_ref.shape
    rows = fields * levels
    for l in range(0, levels, 2):
        pair = jnp.concatenate([state_ref[:, l, :], state_ref[:, l + 1, :]], axis=0)
        pay_ref[l * fields : (l + 2) * fields, :] = pair.astype(BF16)
    local = (sten_ref[...] - dev_ref[0] * columns).astype(F32)
    flag = jnp.where(owner_ref[...] >= 0, 1.0, 0.0)
    tail = jnp.concatenate([local, flag, jnp.zeros((6, columns), F32)], axis=0)
    pay_ref[rows : rows + 16, :] = tail.astype(BF16)


def edges_kernel(total, dev_ref, state_ref, kappa_ref, op_ref, sel_ref, nbr_ref, table_ref, holder_ref,
                 base_ref, edge_ref, facing_ref):
    fields, levels, columns = state_ref.shape
    elements = columns // 16
    flat = state_ref[...].reshape(fields * levels, columns)
    dyn = kappa_ref[...] * jnp.dot(flat, op_ref[...], precision=HIGHEST)
    edge = jnp.dot(dyn, sel_ref[...], precision=HIGHEST)
    edge_ref[...] = edge.astype(BF16)
    rel = lax.rem(nbr_ref[...] - (dev_ref[0] - 1) * elements + total, total).astype(F32)
    spread = jnp.dot(rel, holder_ref[...], precision=HIGHEST)
    on_edge = table_ref[0:4, :]
    is_edge = jnp.sum(on_edge, axis=0, keepdims=True)
    facing = 8.0 * jnp.sum(spread * on_edge, axis=0, keepdims=True) + table_ref[4:5, :]
    facing = jnp.where(is_edge > 0, facing, -1.0).astype(jnp.int32)
    facing_ref[...] = facing
    half = columns // 2
    pick = jnp.where(iota((half, columns), 0) + half == facing, 0.5, 0.0)
    own = jnp.dot(edge, pick, precision=HIGHEST)
    base_ref[...] = flat + (1.0 - 0.5 * is_edge) * dyn + own


def land(code, d, quota, columns):
    slot = jnp.where((code >= d * quota) & (code < (d + 1) * quota), code - d * quota, -2 * quota)
    spot = iota((2 * quota, columns), 0)
    return [jnp.where(spot == slot + h * quota, 1.0, 0.0).astype(BF16) for h in range(2)]


def middle_kernel(base_ref, low_ref, high_ref, facing_ref, out_ref):
    rows, columns = base_ref.shape
    half = columns // 2
    facing = facing_ref[...]
    acc = base_ref[...]
    for part, ref in ((0, low_ref), (2, high_ref)):
        pick = jnp.where(iota((half, columns), 0) + part * half == facing, 0.5, 0.0).astype(BF16)
        acc = acc + jnp.dot(ref[...], pick, preferred_element_type=F32)
    out_ref[...] = acc


def final_kernel(base_ref, code_ref, r0_ref, r1_ref, r2_ref, r3_ref, out_ref):
    fields, levels, columns = out_ref.shape
    quota = columns // GROUP
    code = code_ref[...]
    got = jnp.concatenate([r0_ref[...], r1_ref[...], r2_ref[...], r3_ref[...]], axis=1)
    puts = [land(code, d, quota, columns) for d in range(GROUP)]
    for h in range(2):
        put = jnp.concatenate([p[h] for p in puts], axis=0)
        physics = jnp.dot(got, put, preferred_element_type=F32)
        for i in range(levels // 2):
            l = h * (levels // 2) + i
            out_ref[:, l, :] = base_ref[:, l, :] + physics[i * fields : (i + 1) * fields, :]


def halve(y):
    y = y.reshape(y.shape[0] // 2, 2, *y.shape[1:])
    return (y[:, 0] + y[:, 1]) * BF16(0.5)


def widen(coarse, fine):
    step, cols, ch = coarse.shape
    return jnp.broadcast_to(coarse[:, None], (step, 2, cols, ch)).reshape(2 * step, cols, ch) + fine


def net_kernel(levels, fields, dev_ref, m0_ref, m1_ref, m2_ref, m3_ref, w1_ref, wi_ref, wl_ref,
               r0_ref, r1_ref, r2_ref, r3_ref, code_ref,
               oh_ref, g_ref, net_ref, w1s_ref, w_ref, first_ref, second_ref, pool2_ref, third_ref,
               pool3_ref, join3_ref, join2_ref, top_ref, p_ref, acc_ref, to_ref):
    rows = fields * levels
    columns = m0_ref.shape[1]
    quota = columns // GROUP
    wide = GROUP * columns
    ch = wi_ref.shape[2]
    taps = 9 * fields
    half2, half3 = levels // 2, levels // 4

    for ref, n in ((first_ref, levels), (pool2_ref, half2), (pool3_ref, half3), (join3_ref, half2),
                   (join2_ref, levels)):
        zero = jnp.zeros(ref.shape[1:], BF16)
        ref[0] = zero
        ref[n + 1] = zero
    net_ref[0] = jnp.zeros(net_ref.shape[1:], BF16)
    net_ref[levels + 1] = jnp.zeros(net_ref.shape[1:], BF16)
    p_ref[:, 0:128] = jnp.zeros((24, 128), F32)
    p_ref[:, levels * NB + 128 :] = jnp.zeros((24, 128), F32)
    acc_ref[...] = jnp.zeros(acc_ref.shape, BF16)
    w1s_ref[...] = jnp.zeros(w1s_ref.shape, BF16)
    for t in range(3):
        w1s_ref[128 * t : 128 * t + taps, :] = w1_ref[taps * t : taps * (t + 1), :] * BF16(0.5)
    for i in range(wi_ref.shape[0]):
        g = [wi_ref[i, ch * t : ch * (t + 1), :] for t in range(3)]
        sides, middle = (g[0] + g[2]) * BF16(0.25), g[1] * BF16(0.25)
        w_ref[4 * i] = g[0] * BF16(0.5)
        w_ref[4 * i + 1] = sides + middle
        w_ref[4 * i + 2] = sides - middle
        w_ref[4 * i + 3] = g[2] * BF16(0.5)
    w24 = jnp.concatenate([wl_ref[:, ch * t : ch * (t + 1)].astype(F32) for t in range(3)], axis=0).astype(BF16)

    me = lax.rem(dev_ref[0], GROUP)
    members = (m0_ref, m1_ref, m2_ref, m3_ref)
    upto = jnp.where(iota((columns, columns), 0) < iota((columns, columns), 1), 1.0, 0.0).astype(BF16)
    metas = [ref[rows : rows + 16, :] for ref in members]
    flags = [meta.astype(F32)[9:10, :] for meta in metas]
    counts = [jnp.sum(flag, axis=1, keepdims=True) for flag in flags]
    ranks, targets, active = [], [], jnp.zeros((1, 1), F32)
    for d in range(GROUP):
        start = jnp.zeros((1, 1), F32)
        for other in range(GROUP):
            start = start + jnp.where((me ^ other) < (me ^ d), counts[other], 0.0)
        local = jnp.dot(metas[d], upto, preferred_element_type=F32)[9:10, :].astype(jnp.int32)
        rank = local + start.astype(jnp.int32)
        ranks.append(jnp.where(flags[d] > 0, rank, -1))
        targets.append(jnp.where(flags[d] > 0, d * quota + local // GROUP + 1, 0).astype(F32))
        if d == 0:
            code_ref[...] = jnp.where(flags[d] > 0, (lax.rem(rank, GROUP) ^ me) * quota + local // GROUP, -1)
        active = active + counts[d]
    meta = jnp.concatenate(metas, axis=1)
    rank = jnp.concatenate(ranks, axis=1)
    share = (jnp.sum(active).astype(jnp.int32) - me + GROUP - 1) // GROUP
    slot = GROUP * iota((columns, wide), 0) + me
    choose = jnp.where(slot == rank, 1.0, 0.0).astype(BF16)
    flip = (((1,), (1,)), ((), ()))
    sten = lax.dot_general(meta, choose, flip, preferred_element_type=F32)
    part = (iota((16, wide), 1) // columns).astype(F32).astype(BF16)
    part = lax.dot_general(part, choose, flip, preferred_element_type=F32)
    sten = (sten + columns * part).astype(jnp.int32)
    target = jnp.broadcast_to(jnp.concatenate(targets, axis=1), (128, wide)).astype(BF16)
    to = lax.dot_general(choose, target, flip, preferred_element_type=F32).astype(jnp.int32) - 1
    to_ref[...] = jnp.where(to >= 0, to // quota * (2 * quota) + lax.rem(to, quota), -1)

    @pl.loop(0, (share + 127) // 128)
    def _(q):
        lanes = pl.ds(pl.multiple_of(q * 128, 128), 128)
        for k in range(9):
            for half in range(columns // 128):
                here = sten[k : k + 1, half * 128 : (half + 1) * 128]
                picked = here if half == 0 else jnp.where(q == half, here, picked)
            oh_ref[:, k * 128 : (k + 1) * 128] = jnp.where(iota((wide, 128), 0) == picked, 1.0, 0.0).astype(BF16)
        for k in range(0, 9, 2):
            n = 2 if k < 8 else 1
            for l0 in range(0, levels, levels // 3):
                some = slice(l0 * fields, (l0 + levels // 3) * fields)
                got = jnp.dot(jnp.concatenate([ref[some, :] for ref in members], axis=1),
                              oh_ref[:, k * 128 : (k + n) * 128], preferred_element_type=F32)
                parts = [got[:, u * 128 : (u + 1) * 128].reshape(levels // 3, fields, 128) for u in range(n)]
                if n == 1:
                    parts.append(jnp.zeros_like(parts[0]))
                g_ref[l0 : l0 + levels // 3, k * 8 : k * 8 + 16, :] = jnp.concatenate(parts, axis=1).astype(BF16)
        for l in range(levels):
            net_ref[l + 1, lanes, :] = jnp.concatenate([g_ref[l].T, jnp.zeros((128, 48), BF16)], axis=1)

    mask = jnp.where(iota((128 // NB * 8, 128), 0) // 8 == iota((128 // NB * 8, 128), 1) // NB, 1.0, 0.0)

    @pl.loop(0, (share + NB - 1) // NB)
    def _(b):
        c0 = pl.multiple_of(b * NB, NB)

        def conv_first(n, emit):
            for l0 in range(0, n, STEP):
                x = [net_ref[l0 + t : l0 + t + STEP, pl.ds(c0, NB), :].reshape(STEP * NB, 128) for t in range(3)]
                acc = jnp.dot(jnp.concatenate(x, axis=1), w1s_ref[...], preferred_element_type=F32)
                emit(l0, STEP, silu(acc).reshape(STEP, NB, ch))

        def conv(src, layer, n, emit):
            step = n if n < 4 * STEP else 2 * STEP
            while n % step or step % 2:
                step -= 1
            pairs = step // 2
            for l0 in range(0, n, step):
                x = src[l0 : l0 + step + 2].reshape(pairs + 1, 2, NB, ch)
                even, odd = x[:, 0], x[:, 1]
                d0, d1, d2, d3 = even[:-1], odd[:-1], even[1:], odd[1:]
                m = [jnp.dot(d.reshape(pairs * NB, ch), w_ref[4 * layer + i], preferred_element_type=F32)
                     for i, d in enumerate((d0 - d2, d1 + d2, d2 - d1, d1 - d3))]
                y = [silu(m[0] + (m[1] + m[2])), silu((m[1] - m[2]) - m[3])]
                y = jnp.concatenate([v.reshape(pairs, 1, NB, ch) for v in y], axis=1)
                emit(l0, step, y.reshape(step, NB, ch))

        def emit_first(l0, step, y):
            first_ref[l0 + 1 : l0 + 1 + step] = y

        def emit_second(l0, step, y):
            second_ref[l0 : l0 + step] = y
            pool2_ref[l0 // 2 + 1 : l0 // 2 + 1 + step // 2] = halve(y)

        def emit_third(l0, step, y):
            third_ref[l0 : l0 + step] = y
            pool3_ref[l0 // 2 + 1 : l0 // 2 + 1 + step // 2] = halve(y)

        def emit_deepest(l0, step, y):
            fine = third_ref[2 * l0 : 2 * (l0 + step)]
            join3_ref[2 * l0 + 1 : 2 * (l0 + step) + 1] = widen(y, fine)

        def emit_upper(l0, step, y):
            fine = second_ref[2 * l0 : 2 * (l0 + step)]
            join2_ref[2 * l0 + 1 : 2 * (l0 + step) + 1] = widen(y, fine)

        def emit_top(l0, step, y):
            top_ref[l0 : l0 + step] = y

        conv_first(levels, emit_first)
        conv(first_ref, 0, levels, emit_second)
        conv(pool2_ref, 1, half2, emit_third)
        conv(pool3_ref, 2, half3, emit_deepest)
        conv(join3_ref, 3, half2, emit_upper)
        conv(join2_ref, 4, levels, emit_top)

        group = 384
        for i in range(0, levels * NB, group):
            x = top_ref[i // NB : (i + group) // NB].reshape(group, ch)
            p_ref[:, i + 128 : i + group + 128] = lax.dot_general(w24, x, flip, preferred_element_type=F32)
        n = levels * NB
        out = p_ref[0:8, 128 - NB : n + 128 - NB] + p_ref[8:16, 128 : n + 128] + p_ref[16:24, 128 + NB : n + 128 + NB]
        tiles = []
        for i in range(n // 128):
            tile = out[:, i * 128 : (i + 1) * 128]
            tiles.append(jnp.concatenate([tile] * (128 // NB), axis=0) * mask)
        flat = jnp.concatenate(tiles, axis=0).astype(BF16)
        to = to_ref[pl.ds(c0, NB), :]
        place = []
        for h in range(2):
            lane = jnp.concatenate([to + jnp.where(to >= 0, h * quota, 0)] * (128 // NB), axis=0)
            hits = [jnp.where(lane == iota((128, 128), 1) + i * 128, 1.0, 0.0) for i in range(2 * columns // 128)]
            place.append(jnp.concatenate(hits, axis=1).astype(BF16))
        both = jnp.concatenate([flat[: rows // 2], flat[rows // 2 :]], axis=1)
        acc_ref[...] += jnp.dot(both, jnp.concatenate(place, axis=0), preferred_element_type=F32).astype(BF16)

    for d, ref in enumerate((r0_ref, r1_ref, r2_ref, r3_ref)):
        ref[...] = acc_ref[:, d * 2 * quota : (d + 1) * 2 * quota]


def per_device(state, kappa, edge_nbrs, stencil, owner, w_first, w_inner, w_last):
    fields, levels, columns = state.shape
    rows = fields * levels
    ch = w_inner.shape[2]
    devices = lax.axis_size(AXES)
    device = lax.axis_index(AXES)
    total = columns // 16 * devices
    dev = device.astype(jnp.int32).reshape(1)
    table, holder = node_tables(columns)
    f32 = functools.partial(jax.ShapeDtypeStruct, dtype=F32)
    bf16 = functools.partial(jax.ShapeDtypeStruct, dtype=BF16)
    i32 = functools.partial(jax.ShapeDtypeStruct, dtype=jnp.int32)

    payload = pl.pallas_call(
        pack_kernel,
        out_shape=bf16((rows + 16, columns)),
        in_specs=[SMEM] + [VMEM] * 3,
        out_specs=VMEM,
        name="pack",
    )(dev, state, stencil.T, owner.reshape(1, columns))
    def trade(x, d):
        return lax.ppermute(x, AXES, [(i, i ^ d) for i in range(devices)])

    member1 = trade(payload, 1)
    member2 = trade(payload, 2)

    base, edges, facing = pl.pallas_call(
        functools.partial(edges_kernel, total),
        out_shape=(f32((rows, columns)), bf16((rows, columns // 2)), i32((1, columns))),
        in_specs=[SMEM] + [VMEM] * 7,
        out_specs=(VMEM, VMEM, VMEM),
        cost_estimate=pl.CostEstimate(flops=3 * 10**9, bytes_accessed=2**21, transcendentals=0),
        name="edges",
    )(dev, state, kappa.reshape(1, columns), jnp.asarray(diffusion_matrix(columns)),
      jnp.asarray(edge_matrix(columns)), edge_nbrs.T, jnp.asarray(table), jnp.asarray(holder))

    member2, base = lax.optimization_barrier((member2, base))
    member3 = trade(member2, 1)
    low = lax.ppermute(edges, AXES, [(i, (i + 1) % devices) for i in range(devices)])
    high = lax.ppermute(edges, AXES, [(i, (i - 1) % devices) for i in range(devices)])

    bf = lambda *shape: pltpu.VMEM(shape, BF16)
    lanes = 2 * columns // GROUP
    *results, code = pl.pallas_call(
        functools.partial(net_kernel, levels, fields),
        out_shape=[bf16((rows // 2, lanes))] * GROUP + [i32((1, columns))],
        in_specs=[SMEM] + [VMEM] * (GROUP + 1) + [VMEM] * 2,
        out_specs=[VMEM] * (GROUP + 1),
        scratch_shapes=[
            bf(GROUP * columns, 9 * 128),
            bf(levels, 80, 128),
            bf(levels + 2, columns, 128),
            bf(3 * 128, ch),
            bf(4 * w_inner.shape[0], ch, ch),
            bf(levels + 2, NB, ch),
            bf(levels, NB, ch),
            bf(levels // 2 + 2, NB, ch),
            bf(levels // 2, NB, ch),
            bf(levels // 4 + 2, NB, ch),
            bf(levels // 2 + 2, NB, ch),
            bf(levels + 2, NB, ch),
            bf(levels, NB, ch),
            pltpu.VMEM((24, levels * NB + 256), F32),
            bf(rows // 2, GROUP * lanes),
            pltpu.VMEM((columns, 128), jnp.int32),
        ],
        compiler_params=pltpu.CompilerParams(vmem_limit_bytes=30 * 1024 * 1024),
        cost_estimate=pl.CostEstimate(flops=10**10, bytes_accessed=2**22, transcendentals=10**7),
        name="network",
    )(dev, payload, member1, member2, member3, w_first, w_inner, w_last.T)
    back = [trade(results[d], d) for d in (3, 2, 1)][::-1]

    middle = pl.pallas_call(
        middle_kernel,
        out_shape=f32((rows, columns)),
        in_specs=[VMEM] * 4,
        out_specs=VMEM,
        cost_estimate=pl.CostEstimate(flops=10**9, bytes_accessed=2**22, transcendentals=0),
        compiler_params=SMALL,
        name="middle",
    )(*lax.optimization_barrier((base, low, high, facing, results[0]))[:4])

    return pl.pallas_call(
        final_kernel,
        out_shape=f32((fields, levels, columns)),
        in_specs=[VMEM] * 6,
        out_specs=VMEM,
        compiler_params=SMALL,
        name="combine",
    )(middle.reshape(fields, levels, columns), code, results[0], *back)


def solution(mesh):
    in_specs = (
        P(None, None, AXES),
        P(AXES),
        P(AXES, None),
        P(AXES, None),
        P(AXES),
        P(),
        P(),
        P(),
    )
    return jax.shard_map(
        per_device, mesh=mesh, in_specs=in_specs, out_specs=P(None, None, AXES), check_vma=False
    )
```
